32 devices in a mesh: wide: 8 (over z, y), narrow: 4 (over x, core).
Axes of the slice: x: 2, y: 2, z: 4, core: 2. Of those that a mesh axis runs over, the one named last changes fastest.
Arguments:
- word_states: float32 [32, 512, 768], P(('wide', 'narrow')), may hold values from -6 to 6
- entity_states: float32 [32, 128, 768], P(('wide', 'narrow')), may hold values from -6 to 6
- seq_counts: int32 [32, 2], P(('wide', 'narrow')), may hold values from 0 to 512, as said below
- attention_weight: float32 [7, 768, 768], P(None, 'narrow', 'wide')
- expand_weight: float32 [768, 3072], P('narrow', 'wide')
- reduce_weight: float32 [3072, 768], P('narrow', 'wide')
- norm_params: float32 [4, 768], replicated
- moment_attention: float32 [7, 768, 768], P(None, 'narrow', 'wide')
- moment_expand: float32 [768, 3072], P('narrow', 'wide')
- moment_reduce: float32 [3072, 768], P('narrow', 'wide')
- moment_norms: float32 [4, 768], replicated
- square_attention: float32 [7, 768, 768], P(None, 'narrow', 'wide')
- square_expand: float32 [768, 3072], P('narrow', 'wide')
- square_reduce: float32 [3072, 768], P('narrow', 'wide')
- square_norms: float32 [4, 768], replicated
- word_cotangent: float32 [32, 512, 768], P(('wide', 'narrow')), may hold values from -6 to 6
- entity_cotangent: float32 [32, 128, 768], P(('wide', 'narrow')), may hold values from -6 to 6
Outputs:
- word_output: float32 [32, 512, 768], P(('wide', 'narrow'))
- entity_output: float32 [32, 128, 768], P(('wide', 'narrow'))
- word_grad: float32 [32, 512, 768], P(('wide', 'narrow'))
- entity_grad: float32 [32, 128, 768], P(('wide', 'narrow'))
- new_attention: float32 [7, 768, 768], P(None, 'narrow', 'wide')
- new_expand: float32 [768, 3072], P('narrow', 'wide')
- new_reduce: float32 [3072, 768], P('narrow', 'wide')
- new_norms: float32 [4, 768], replicated
- moment_attention_new: float32 [7, 768, 768], P(None, 'narrow', 'wide')
- moment_expand_new: float32 [768, 3072], P('narrow', 'wide')
- moment_reduce_new: float32 [3072, 768], P('narrow', 'wide')
- moment_norms_new: float32 [4, 768], replicated
- square_attention_new: float32 [7, 768, 768], P(None, 'narrow', 'wide')
- square_expand_new: float32 [768, 3072], P('narrow', 'wide')
- square_reduce_new: float32 [3072, 768], P('narrow', 'wide')
- square_norms_new: float32 [4, 768], replicated
- trust_stats: float32 [13, 3], replicated
The draws below stay inside these ranges and needn't reach their ends.
Inputs may be any that keep to these rules, and one draw needn't show every extreme that they name: seq_counts[s, 0] is 256 to 512 and seq_counts[s, 1] is 0 to 128; some sequence has exactly 512 live words and some exactly 128 live entities.
All inputs are finite; a program needn't handle non-finite values.
Results may differ from the reference program's by a relative error of at most 0.024.
The reference program's roundings to bfloat16 on the way count: a program that leaves them out, or rounds other values in their place, can miss the bound.
Values may be sent and summed in bfloat16 or wider, within the bound.
No kernel may reach another device: no remote copies, remote signals or barrier semaphores. Data moves between devices by JAX's collectives and lax.ppermute only.
A program may use at most 192 MiB of HBM per device.

```python
import math
import jax
import jax.numpy as jnp
from jax import lax

D = 768
HEADS = 12
HEAD = 64
FF = 3072
WORDS = 512
ENTS = 128
STEP = 7
SEQS = 32


def rise_table(rows, cols, spread):
    row_part = 1.0 + spread * jnp.arange(rows, dtype=jnp.float32) / rows
    col_part = 1.0 + spread * jnp.arange(cols, dtype=jnp.float32) / cols
    return jnp.sqrt(row_part[:, None] * col_part[None, :]) / (1.0 + 0.5 * spread)


def token_root():
    return math.sqrt(SEQS * (WORDS + ENTS))


def draw_seq_counts(key, part):
    key = jax.random.fold_in(key, 9)
    keys = jax.random.split(key, 5)
    words = jax.random.randint(keys[0], (SEQS,), WORDS // 2, WORDS + 1)
    first = jax.random.randint(keys[1], (SEQS,), 0, ENTS + 1)
    second = jax.random.randint(keys[2], (SEQS,), 0, ENTS + 1)
    entities = first * second // ENTS
    index = jnp.arange(SEQS, dtype=jnp.int32)
    words = jnp.where(index == jax.random.randint(keys[3], (), 0, SEQS), WORDS, words)
    entities = jnp.where(index == jax.random.randint(keys[4], (), 0, SEQS), ENTS, entities)
    return jnp.stack([words, entities], 1).astype(jnp.int32)


def draw_attention_weight(key, part):
    key = jax.random.fold_in(key, 11)
    noise = jax.random.normal(key, (7, D, D), jnp.float32)
    spread = 2.0
    slices = jnp.array([1.5, 1.5, 1.5, 1.5, 1.0, 1.0, 3.0], jnp.float32)
    return noise * rise_table(D, D, spread)[None] * slices[:, None, None] / math.sqrt(D)


def draw_expand_weight(key, part):
    key = jax.random.fold_in(key, 12)
    noise = jax.random.normal(key, (D, FF), jnp.float32)
    spread = 2.0
    return noise * rise_table(D, FF, spread) / math.sqrt(D)


def draw_reduce_weight(key, part):
    key = jax.random.fold_in(key, 13)
    noise = jax.random.normal(key, (FF, D), jnp.float32)
    spread = 2.0
    return noise * rise_table(FF, D, spread) / math.sqrt(FF)


def draw_norm_params(key, part):
    key = jax.random.fold_in(key, 14)
    gains = jax.random.uniform(jax.random.fold_in(key, 1), (2, D), jnp.float32, 0.6, 1.4)
    shifts = 0.5 * jax.random.normal(jax.random.fold_in(key, 2), (2, D), jnp.float32)
    return jnp.stack([gains[0], shifts[0], gains[1], shifts[1]])


def draw_moment_attention(key, part):
    key = jax.random.fold_in(key, 21)
    noise = jax.random.normal(key, (7, D, D), jnp.float32)
    slices = jnp.array([0.1, 0.1, 0.1, 0.1, 0.1, 0.5, 0.3], jnp.float32) * token_root()
    return noise * rise_table(D, D, 2.0)[None] * slices[:, None, None]


def draw_moment_expand(key, part):
    key = jax.random.fold_in(key, 22)
    noise = jax.random.normal(key, (D, FF), jnp.float32)
    return noise * rise_table(D, FF, 2.0) * (0.25 * token_root())


def draw_moment_reduce(key, part):
    key = jax.random.fold_in(key, 23)
    noise = jax.random.normal(key, (FF, D), jnp.float32)
    return noise * rise_table(FF, D, 2.0) * (0.6 * token_root())


def draw_moment_norms(key, part):
    key = jax.random.fold_in(key, 24)
    return jax.random.normal(key, (4, D), jnp.float32) * token_root()


def draw_square_attention(key, part):
    key = jax.random.fold_in(key, 31)
    level = jnp.exp(jax.random.uniform(key, (7, D, D), jnp.float32, 0.0, math.log(4.0)))
    base = 0.4 * token_root()
    return level * (base * base)


def draw_square_expand(key, part):
    key = jax.random.fold_in(key, 32)
    level = jnp.exp(jax.random.uniform(key, (D, FF), jnp.float32, 0.0, math.log(4.0)))
    return level * (0.25 * token_root()) ** 2


def draw_square_reduce(key, part):
    key = jax.random.fold_in(key, 33)
    level = jnp.exp(jax.random.uniform(key, (FF, D), jnp.float32, 0.0, math.log(4.0)))
    return level * (0.6 * token_root()) ** 2


def draw_square_norms(key, part):
    key = jax.random.fold_in(key, 34)
    level = jnp.exp(jax.random.uniform(key, (4, D), jnp.float32, 0.0, math.log(4.0)))
    return level * token_root() ** 2


def level_of(own_key, extent, pieces, low, top_value):
    level, own = 1.0, jax.random.fold_in(own_key, 6)
    for axis_at, blocks in pieces:
        steps = jnp.exp(jax.random.uniform(jax.random.fold_in(own, axis_at), (blocks,), jnp.float32, low / len(pieces), top_value / len(pieces)))
        level = level * jnp.repeat(steps, extent[axis_at] // blocks).reshape([-1 if axis == axis_at else 1 for axis in range(len(extent))])
    return level


def bell_draw(own_key, dims, deviation, limit, cuts=(), kind=jnp.bfloat16):
    drawn = deviation * jax.random.normal(own_key, dims, jnp.float32)
    if cuts:
        drawn = drawn * level_of(own_key, dims, cuts, -0.22, 0.18)
    return jnp.clip(drawn, -limit, limit).astype(kind)


def setup_inputs(seed: int = 0) -> dict:
    key_list = jax.random.split(jax.random.key(seed), 18)
    return {
        "word_states": bell_draw(key_list[0], (SEQS, WORDS, D), 1.0, 6.0, ((0, 32),), jnp.float32),
        "entity_states": bell_draw(key_list[1], (SEQS, ENTS, D), 1.0, 6.0, ((0, 32),), jnp.float32),
        "seq_counts": draw_seq_counts(jax.random.fold_in(key_list[17], 71), 0),
        "attention_weight": draw_attention_weight(jax.random.fold_in(key_list[17], 71), 0),
        "expand_weight": draw_expand_weight(jax.random.fold_in(key_list[17], 71), 0),
        "reduce_weight": draw_reduce_weight(jax.random.fold_in(key_list[17], 71), 0),
        "norm_params": draw_norm_params(jax.random.fold_in(key_list[17], 71), 0),
        "moment_attention": draw_moment_attention(jax.random.fold_in(key_list[17], 71), 0),
        "moment_expand": draw_moment_expand(jax.random.fold_in(key_list[17], 71), 0),
        "moment_reduce": draw_moment_reduce(jax.random.fold_in(key_list[17], 71), 0),
        "moment_norms": draw_moment_norms(jax.random.fold_in(key_list[17], 71), 0),
        "square_attention": draw_square_attention(jax.random.fold_in(key_list[17], 71), 0),
        "square_expand": draw_square_expand(jax.random.fold_in(key_list[17], 71), 0),
        "square_reduce": draw_square_reduce(jax.random.fold_in(key_list[17], 71), 0),
        "square_norms": draw_square_norms(jax.random.fold_in(key_list[17], 71), 0),
        "word_cotangent": bell_draw(key_list[15], (SEQS, WORDS, D), 1.0, 6.0, ((0, 32),), jnp.float32),
        "entity_cotangent": bell_draw(key_list[16], (SEQS, ENTS, D), 1.0, 6.0, ((0, 32),), jnp.float32),
    }


@jax.custom_vjp
def low(v):
    return lax.optimization_barrier(v.astype(jnp.bfloat16)).astype(jnp.float32)

@jax.custom_vjp
def low_back(v):
    return v

def low_keep(v):
    return (low(v), None)

def low_pass(kept, grad):
    return (grad,)

def back_keep(v):
    return (v, None)

def back_low(kept, grad):
    return (low(grad),)
low.defvjp(low_keep, low_pass)
low_back.defvjp(back_keep, back_low)
HIGH = lax.Precision.HIGHEST
eps_norm = 1e-05
adam_eps = 1e-06
matrix_decay = 0.01
learn_rate = 0.5
masked_score = -1e+30

def both_ways(value):
    return low_back(low(value))

def matmul(left, right):
    return jnp.dot(left, right, precision=HIGH)

def layer_norm(value, gain, shift):
    center = value - lax.optimization_barrier(jnp.mean(value, axis=-1, keepdims=True))
    spread = lax.optimization_barrier(jnp.mean(center * center, axis=-1, keepdims=True))
    return center * lax.rsqrt(spread + eps_norm) * gain + shift

def split_heads(value):
    return value.reshape(value.shape[0], HEADS, HEAD)

def head_scores(query, key):
    return jnp.einsum('qhd,khd->hqk', split_heads(query), split_heads(key), precision=HIGH) * HEAD ** (-0.5)

def sequence_out(params, word_rows, entity_rows, counts):
    attention = low(params[0])
    expand = low(params[1])
    shrink = low(params[2])
    norms = params[3]
    hidden = jnp.concatenate([word_rows, entity_rows], 0)
    hidden_low = low(hidden)
    keys = both_ways(matmul(hidden_low, attention[4]))
    values = both_ways(matmul(hidden_low, attention[5]))
    word_query = both_ways(jnp.einsum('ld,kde->kle', hidden_low[:WORDS], attention[0:2], precision=HIGH))
    entity_query = both_ways(jnp.einsum('ld,kde->kle', hidden_low[WORDS:], attention[2:4], precision=HIGH))
    key_words = keys[:WORDS]
    key_entities = keys[WORDS:]
    upper = jnp.concatenate([head_scores(word_query[0], key_words), head_scores(word_query[1], key_entities)], 2)
    lower = jnp.concatenate([head_scores(entity_query[0], key_words), head_scores(entity_query[1], key_entities)], 2)
    scores = low_back(jnp.concatenate([upper, lower], 1))
    live = jnp.concatenate([jnp.arange(WORDS, dtype=jnp.int32) < counts[0], jnp.arange(ENTS, dtype=jnp.int32) < counts[1]])
    scores = jnp.where(live[None, None, :], scores, masked_score)
    top = lax.optimization_barrier(jnp.max(scores, axis=2, keepdims=True))
    expd = jnp.exp(scores - top)
    probs = low(expd / lax.optimization_barrier(jnp.sum(expd, axis=2, keepdims=True)))
    context = jnp.einsum('hqk,khd->qhd', probs, split_heads(values), precision=HIGH).reshape(-1, D)
    context = both_ways(context)
    attended = low_back(matmul(context, attention[6]))
    middle = layer_norm(hidden + attended, norms[0], norms[1])
    middle_low = low(middle)
    inner = low_back(matmul(middle_low, expand))
    activated = low(jax.nn.gelu(inner, approximate=False))
    ffn_out = low_back(matmul(activated, shrink))
    result = layer_norm(middle + ffn_out, norms[2], norms[3])
    return (result[:WORDS], result[WORDS:])

def adapt(weight, grad, first, second, decay):
    first = 0.5 * first + 0.5 * grad
    second = 0.5 * second + 0.5 * grad * grad
    fix_first = 1.0 - 0.5 ** STEP
    fix_second = 1.0 - 0.5 ** STEP
    update = first / fix_first / (jnp.sqrt(second / fix_second) + adam_eps) + decay * weight
    return (first, second, update)

def reference(word_states, entity_states, seq_counts, attention_weight, expand_weight, reduce_weight, norm_params, moment_attention, moment_expand, moment_reduce, moment_norms, square_attention, square_expand, square_reduce, square_norms, word_cotangent, entity_cotangent):
    params = (attention_weight, expand_weight, reduce_weight, norm_params)

    def one_sequence(totals, items):
        word_rows, entity_rows, counts, word_cot, entity_cot = items

        def forward(p, w, e):
            return sequence_out(p, w, e, counts)
        outs, pull = jax.vjp(forward, params, word_rows, entity_rows)
        grad_params, grad_words, grad_entities = pull((word_cot, entity_cot))
        totals = jax.tree.map(jnp.add, totals, grad_params)
        return (totals, (outs[0], outs[1], grad_words, grad_entities))
    zeros = jax.tree.map(jnp.zeros_like, params)
    grads, (word_output, entity_output, word_grad, entity_grad) = lax.scan(one_sequence, zeros, (word_states, entity_states, seq_counts, word_cotangent, entity_cotangent))
    att_first, att_second, att_update = adapt(attention_weight, grads[0], moment_attention, square_attention, matrix_decay)
    exp_first, exp_second, exp_update = adapt(expand_weight, grads[1], moment_expand, square_expand, matrix_decay)
    red_first, red_second, red_update = adapt(reduce_weight, grads[2], moment_reduce, square_reduce, matrix_decay)
    nrm_first, nrm_second, nrm_update = adapt(norm_params, grads[3], moment_norms, square_norms, 0.0)
    weight_sq = jnp.concatenate([lax.optimization_barrier(jnp.sum(attention_weight * attention_weight, axis=(1, 2))), jnp.sum(expand_weight * expand_weight)[None], jnp.sum(reduce_weight * reduce_weight)[None], lax.optimization_barrier(jnp.sum(norm_params * norm_params, axis=1))])
    update_sq = jnp.concatenate([lax.optimization_barrier(jnp.sum(att_update * att_update, axis=(1, 2))), jnp.sum(exp_update * exp_update)[None], jnp.sum(red_update * red_update)[None], lax.optimization_barrier(jnp.sum(nrm_update * nrm_update, axis=1))])
    weight_norm = jnp.sqrt(weight_sq)
    update_norm = jnp.sqrt(update_sq)
    trust = weight_norm / update_norm
    new_attention = attention_weight - learn_rate * trust[0:7, None, None] * att_update
    new_expand = expand_weight - learn_rate * trust[7] * exp_update
    new_reduce = reduce_weight - learn_rate * trust[8] * red_update
    new_norms = norm_params - learn_rate * trust[9:13, None] * nrm_update
    trust_stats = jnp.stack([jnp.log(weight_norm), jnp.log(update_norm), jnp.log(trust)], 1)
    return (word_output, entity_output, word_grad, entity_grad, new_attention, new_expand, new_reduce, new_norms, att_first, exp_first, red_first, nrm_first, att_second, exp_second, red_second, nrm_second, trust_stats)
```

```python
import functools

import jax
import jax.numpy as jnp
from jax import lax
from jax.experimental import pallas as pl
from jax.experimental.pallas import tpu as pltpu
from jax.sharding import PartitionSpec as P

D = 768
FF = 3072
HEADS = 12
HEAD = 64
WORDS = 512
ENTS = 128
ROWS = WORDS + ENTS
STEP = 7

eps_norm = 1e-05
adam_eps = 1e-06
matrix_decay = 0.01
learn_rate = 0.5
masked_score = -1e30

f32 = jnp.float32
bf16 = jnp.bfloat16
NN = (((1,), (0,)), ((), ()))
NT = (((1,), (1,)), ((), ()))
TN = (((0,), (0,)), ((), ()))
VMEM = pl.BlockSpec(memory_space=pltpu.VMEM)
SMEM = pl.BlockSpec(memory_space=pltpu.SMEM)
ANY = pl.BlockSpec(memory_space=pl.ANY)
PARAMS = pltpu.CompilerParams(vmem_limit_bytes=60 * 2**20)


def dot(left, right, dims):
    return lax.dot_general(left, right, dims, preferred_element_type=f32)


def shape(dims, dtype):
    return jax.ShapeDtypeStruct(dims, dtype)


def cost(flops, moved):
    return pl.CostEstimate(flops=flops, bytes_accessed=moved, transcendentals=0)


def away_blocks():
    for core in range(2):
        for outer in range(2):
            for lead in range(2):
                for low in range(2):
                    for high in range(2):
                        yield core, outer, lead, low, high


def places(wide, narrow, second, block):
    core, outer, lead, low, high = block
    x_away, y_away = (outer, lead) if second else (lead, outer)
    w = wide ^ (high * 4 + low * 2 + y_away)
    n = narrow ^ (x_away * 2 + core)
    return w, n


def piece_of(bufs, block):
    core, outer, lead, low, high = block
    return bufs[core * 2 + outer].at[lead, low, high]


def coords():
    return lax.axis_index("wide"), lax.axis_index("narrow")


def start_attention(bufs, second, target, slots, sem):
    wide, narrow = coords()
    for block in away_blocks():
        w, n = places(wide, narrow, second, block)
        row = pl.multiple_of(w * 96 + (n % 2) * 48, 16)
        lane = pl.multiple_of((n // 2) * 384, 128)
        src = piece_of(bufs, block)
        pltpu.make_async_copy(src, target.at[slots, pl.ds(row, 48), pl.ds(lane, 384)], sem).start()


def drain(ref, sem):
    pltpu.make_async_copy(ref, ref, sem).wait()


def prep_kernel(att, exp, red, keep, send, exp_low, red_low, sums):
    narrow = lax.axis_index("narrow")
    core = narrow % 2
    total = []
    for i in range(7):
        value = att[i]
        total.append(jnp.sum(value * value))
        turned = value.T.astype(bf16)
        halves = turned.reshape(2, 48, 192)

        @pl.when(core == 0)
        def _():
            keep[i] = halves[0]
            send[i] = halves[1]

        @pl.when(core == 1)
        def _():
            keep[i] = halves[1]
            send[i] = halves[0]

    value = exp[...]
    total.append(jnp.sum(value * value))
    exp_low[...] = value.astype(bf16)
    value = red[...]
    total.append(jnp.sum(value * value))
    turned = value.T.astype(bf16)
    red_low[0] = turned[:, :384]
    red_low[1] = turned[:, 384:]
    for i in range(9):
        sums[i] = total[i]


def prep(att, exp, red):
    return pl.pallas_call(
        prep_kernel,
        in_specs=[VMEM] * 3,
        out_specs=[VMEM] * 4 + [SMEM],
        out_shape=[
            shape((7, 48, 192), bf16),
            shape((7, 48, 192), bf16),
            shape((192, 384), bf16),
            shape((2, 96, 384), bf16),
            shape((9,), f32),
        ],
        compiler_params=PARAMS,
        name="prep",
    )(att, exp, red)


def project_kv_kernel(fast, word, ent, *refs):
    if fast:
        first, second, refs = refs[:4], refs[4:8], refs[8:]
    else:
        whole, refs = refs[0], refs[1:]
    low, keys, values, target, sem = refs
    if fast:
        start_attention(first, False, target, pl.ds(0, 1), sem)
        start_attention(second, True, target, pl.ds(1, 1), sem)
    else:
        pltpu.make_async_copy(whole.at[pl.ds(4, 2)], target, sem).start()
    low[:WORDS] = word[...].astype(bf16)
    low[WORDS:] = ent[...].astype(bf16)
    drain(target, sem)
    keys[...] = dot(low[...], target[0], NT).astype(bf16)
    values[...] = dot(low[...], target[1], NT).astype(bf16)


def project_kv(fast, word, ent, pieces):
    return pl.pallas_call(
        functools.partial(project_kv_kernel, fast),
        in_specs=[VMEM, VMEM] + [ANY] * len(pieces),
        out_specs=[VMEM] * 4,
        out_shape=[shape((ROWS, D), bf16)] * 3 + [shape((2, D, D), bf16)],
        scratch_shapes=[pltpu.SemaphoreType.DMA],
        compiler_params=PARAMS,
        cost_estimate=cost(2 * ROWS * D * D * 2, 8000000),
        name="project_kv",
    )(word, ent, *pieces)


def project_q_kernel(fast, low, *refs):
    if fast:
        first, second, refs = refs[:4], refs[4:8], refs[8:]
    else:
        whole, refs = refs[0], refs[1:]
    to_words, to_ents, target, sem = refs
    if fast:
        start_attention(first, False, target, pl.ds(0, 2), sem)
        start_attention(second, True, target, pl.ds(2, 2), sem)
    else:
        for slot, k in enumerate((0, 2, 1, 3)):
            pltpu.make_async_copy(whole.at[k], target.at[slot], sem).start()
    drain(target, sem)
    scale = HEAD ** (-0.5)
    word = low[:WORDS]
    ent = low[WORDS:]
    to_words[:WORDS] = (dot(word, target[0], NT) * scale).astype(bf16)
    to_words[WORDS:] = (dot(ent, target[1], NT) * scale).astype(bf16)
    to_ents[:WORDS] = (dot(word, target[2], NT) * scale).astype(bf16)
    to_ents[WORDS:] = (dot(ent, target[3], NT) * scale).astype(bf16)


def project_q(fast, low, pieces):
    return pl.pallas_call(
        functools.partial(project_q_kernel, fast),
        in_specs=[VMEM] + [ANY] * len(pieces),
        out_specs=[VMEM] * 3,
        out_shape=[shape((ROWS, D), bf16)] * 2 + [shape((4, D, D), bf16)],
        scratch_shapes=[pltpu.SemaphoreType.DMA],
        compiler_params=PARAMS,
        cost_estimate=cost(2 * ROWS * D * D * 2, 8000000),
        name="project_q",
    )(low, *pieces)


def head_masks(counts):
    lane = lax.broadcasted_iota(jnp.int32, (ROWS, 128), 1)
    row = lax.broadcasted_iota(jnp.int32, (ROWS, 128), 0)
    edge = jnp.where(row < WORDS, counts[0], counts[1] + WORDS)
    bias = jnp.where(row < edge, 0.0, masked_score)
    out = []
    for h in range(2):
        own = jnp.where((lane < HEAD) if h == 0 else (lane >= HEAD), 1.0, 0.0).astype(bf16)
        mark = jnp.where(lane == (HEAD if h == 0 else 0), 1.0, 0.0)
        rest = (1.0 - mark).astype(bf16)
        tag = (bias * mark).astype(bf16)
        out.append((own, mark.astype(bf16), rest, tag))
    return out


def scores_of(masks, keys, to_words, to_ents):
    own, mark, rest, tag = masks
    tagged = keys * own + tag
    upper = dot(tagged[:WORDS], to_words * rest + mark, NT)
    lower = dot(tagged[WORDS:], to_ents * rest + mark, NT)
    return jnp.concatenate([upper, lower], 0)


def attend_kernel(counts, to_words, to_ents, keys, values, context, exact, lse):
    masks = head_masks(counts)
    outs = []
    for h in range(2):
        scores = scores_of(masks[h], keys[...], to_words[...], to_ents[...])
        top = jnp.max(scores, axis=0, keepdims=True)
        expd = jnp.exp(scores - top)
        total = jnp.sum(expd, axis=0, keepdims=True)
        lse[h : h + 1, :] = top + jnp.log(total)
        mixed = dot(values[:, h * HEAD : (h + 1) * HEAD], expd.astype(bf16), TN)
        outs.append(mixed * (1.0 / total))
    joined = jnp.concatenate(outs, 0).T
    exact[...] = joined
    context[...] = joined.astype(bf16)


def attend(counts, to_words, to_ents, keys, values):
    pair = pl.BlockSpec((ROWS, 128), lambda i: (0, i))
    stat = pl.BlockSpec((None, 2, ROWS), lambda i: (i, 0, 0))
    return pl.pallas_call(
        attend_kernel,
        grid=(HEADS // 2,),
        in_specs=[SMEM, pair, pair, pair, pair],
        out_specs=[pair, pair, stat],
        out_shape=[
            shape((ROWS, D), bf16),
            shape((ROWS, D), f32),
            shape((HEADS // 2, 2, ROWS), f32),
        ],
        compiler_params=PARAMS,
        cost_estimate=cost(8 * ROWS * ROWS * D, 12000000),
        name="attend",
    )(counts, to_words, to_ents, keys, values)


def normed(value):
    center = value - jnp.mean(value, axis=-1, keepdims=True)
    spread = jnp.mean(center * center, axis=-1, keepdims=True)
    inverse = lax.rsqrt(spread + eps_norm)
    return center * inverse, inverse


def normed_back(unit, inverse, cotangent):
    mean = jnp.mean(cotangent, axis=-1, keepdims=True)
    inner = jnp.mean(cotangent * unit, axis=-1, keepdims=True)
    return inverse * (cotangent - mean - unit * inner)


def column_sum(value):
    return jnp.sum(value, axis=0, keepdims=True)


def feed_kernel(fast, word, ent, context, norms, word_cot, ent_cot, *refs):
    if fast:
        bufs, refs = (refs[0:4], refs[4:8], refs[8:12], refs[12:16]), refs[16:]
    else:
        bufs, refs = refs[0:3], refs[3:]
    (
        word_out,
        ent_out,
        middle_low,
        activated,
        slope,
        d_second,
        d_ffn,
        unit_one,
        inverse_one,
        grads_two,
        out_all,
        exp_all,
        red_all,
        total,
        sem_out,
        sem_exp,
        sem_red,
        sem_save,
    ) = refs
    step = pl.program_id(0)

    @pl.when(step == 0)
    def _():
        if fast:
            start_feed(bufs, out_all, exp_all, red_all, sem_out, sem_exp, sem_red)
        else:
            pltpu.make_async_copy(bufs[0].at[6], out_all, sem_out).start()
            for j in range(4):
                cols = pl.ds(j * D, D)
                pltpu.make_async_copy(bufs[1].at[:, cols], exp_all.at[j], sem_exp.at[j]).start()
                pltpu.make_async_copy(bufs[2].at[:, cols], red_all.at[j], sem_red.at[j]).start()
        drain(out_all, sem_out)
        hidden = jnp.concatenate([word[...], ent[...]], 0)
        unit, inverse = normed(hidden + dot(context[...], out_all[...], NT))
        middle = unit * norms[0:1, :] + norms[1:2, :]
        unit_one[...] = unit
        inverse_one[...] = inverse
        middle_low[...] = middle.astype(bf16)
        total[...] = middle

    for j in range(4):

        @pl.when(step == j)
        def _():
            drain(exp_all.at[j], sem_exp.at[j])
            drain(red_all.at[j], sem_red.at[j])

    inner = dot(middle_low[...], exp_all[step], NN)
    share = 0.5 + 0.5 * lax.erf(inner * 0.7071067811865476)
    slope[...] = share + inner * jnp.exp(-0.5 * inner * inner) * 0.3989422804014327
    active = (inner * share).astype(bf16)
    activated[...] = active
    total[...] += dot(active, red_all[step], NT)

    @pl.when(step == 3)
    def _():
        unit, inverse = normed(total[...])
        result = unit * norms[2:3, :] + norms[3:4, :]
        word_out[...] = result[:WORDS]
        ent_out[...] = result[WORDS:]
        cot = jnp.concatenate([word_cot[...], ent_cot[...]], 0)
        grads_two[0:1, :] = column_sum(cot * unit)
        grads_two[1:2, :] = column_sum(cot)
        back = normed_back(unit, inverse, cot * norms[2:3, :])
        d_second[...] = back
        d_ffn[...] = back.astype(bf16)


def start_feed(bufs, out_all, exp_all, red_all, sem_out, sem_exp, sem_red):
    wide, narrow = coords()
    for block in away_blocks():
        w, n = places(wide, narrow, False, block)
        row = pl.multiple_of(w * 96 + (n % 2) * 48, 16)
        lane = pl.multiple_of((n // 2) * 384, 128)
        src = piece_of(bufs[0], block).at[pl.ds(96, 48)]
        pltpu.make_async_copy(src, out_all.at[pl.ds(row, 48), pl.ds(lane, 384)], sem_out).start()
    for half in range(2):
        for block in away_blocks():
            w, n = places(wide, narrow, False, block)
            src = piece_of(bufs[2 * half], block)
            if half == 0:
                src = src.at[pl.ds(0, 96)]
            row = pl.multiple_of(n * 192 + half * 96, 16)
            lane = pl.multiple_of((w % 2) * 384, 128)
            dst = exp_all.at[w // 2, pl.ds(row, 96), pl.ds(lane, 384)]
            pltpu.make_async_copy(src, dst, sem_exp.at[w // 2]).start()
        for block in away_blocks():
            w, n = places(wide, narrow, True, block)
            src = piece_of(bufs[2 * half + 1], block)
            row = pl.multiple_of(w * 96 + half * 48, 16)
            for part in range(2):
                dst = red_all.at[n, pl.ds(row, 48), pl.ds(part * 384, 384)]
                pltpu.make_async_copy(src.at[pl.ds(part * 48, 48)], dst, sem_red.at[n]).start()


def feed(fast, word, ent, context, norms, word_cot, ent_cot, pieces):
    column = pl.BlockSpec((ROWS, D), lambda i: (0, i))
    return pl.pallas_call(
        functools.partial(feed_kernel, fast),
        grid=(4,),
        in_specs=[VMEM] * 6 + [ANY] * len(pieces),
        out_specs=[VMEM] * 3 + [column, column] + [VMEM] * 8,
        out_shape=[
            shape((WORDS, D), f32),
            shape((ENTS, D), f32),
            shape((ROWS, D), bf16),
            shape((ROWS, FF), bf16),
            shape((ROWS, FF), f32),
            shape((ROWS, D), f32),
            shape((ROWS, D), bf16),
            shape((ROWS, D), f32),
            shape((ROWS, 1), f32),
            shape((2, D), f32),
            shape((D, D), bf16),
            shape((4, D, D), bf16),
            shape((4, D, D), bf16),
        ],
        scratch_shapes=[
            pltpu.VMEM((ROWS, D), f32),
            pltpu.SemaphoreType.DMA,
            pltpu.SemaphoreType.DMA((4,)),
            pltpu.SemaphoreType.DMA((4,)),
            pltpu.SemaphoreType.DMA,
        ],
        compiler_params=PARAMS,
        cost_estimate=cost(2 * ROWS * D * (D + 2 * FF), 40000000),
        name="feed",
    )(word, ent, context, norms, word_cot, ent_cot, *pieces)


def feed_back_kernel(
    d_ffn,
    red_all,
    exp_all,
    slope,
    d_second,
    unit_one,
    inverse_one,
    norms,
    out_all,
    exact,
    d_inner,
    d_first,
    d_out,
    d_context,
    row_inner,
    grads_one,
    total,
):
    step = pl.program_id(0)
    back = (dot(d_ffn[...], red_all[...], NN) * slope[...]).astype(bf16)
    d_inner[...] = back

    @pl.when(step == 0)
    def _():
        total[...] = d_second[...]

    total[...] += dot(back, exp_all[...], NT)

    @pl.when(step == 3)
    def _():
        d_middle = total[...]
        unit = unit_one[...]
        grads_one[0:1, :] = column_sum(d_middle * unit)
        grads_one[1:2, :] = column_sum(d_middle)
        first = normed_back(unit, inverse_one[...], d_middle * norms[0:1, :])
        d_first[...] = first
        d_out[...] = first.astype(bf16)
        context = dot(first.astype(bf16), out_all[...], NN).astype(bf16)
        d_context[...] = context
        product = context.astype(f32) * exact[...]
        head = lax.broadcasted_iota(jnp.int32, (16, D), 1) // HEAD
        pick = jnp.where(head == lax.broadcasted_iota(jnp.int32, (16, D), 0), 1.0, 0.0).astype(bf16)
        high = product.astype(bf16)
        low = (product - high.astype(f32)).astype(bf16)
        sums = dot(pick, high, NT) + dot(pick, low, NT)
        for i in range(HEADS // 2):
            row_inner[i] = sums[2 * i : 2 * i + 2]


def feed_back(d_ffn, red_all, exp_all, slope, d_second, unit_one, inverse_one, norms, out_all, exact):
    column = pl.BlockSpec((ROWS, D), lambda i: (0, i))
    part = pl.BlockSpec((None, D, D), lambda i: (i, 0, 0))
    return pl.pallas_call(
        feed_back_kernel,
        grid=(4,),
        in_specs=[VMEM, part, part, column] + [VMEM] * 6,
        out_specs=[column] + [VMEM] * 5,
        out_shape=[
            shape((ROWS, FF), bf16),
            shape((ROWS, D), f32),
            shape((ROWS, D), bf16),
            shape((ROWS, D), bf16),
            shape((HEADS // 2, 2, ROWS), f32),
            shape((2, D), f32),
        ],
        scratch_shapes=[pltpu.VMEM((ROWS, D), f32)],
        compiler_params=PARAMS,
        cost_estimate=cost(2 * ROWS * D * (D + 2 * FF), 30000000),
        name="feed_back",
    )(d_ffn, red_all, exp_all, slope, d_second, unit_one, inverse_one, norms, out_all, exact)


def attend_back_kernel(
    counts, to_words, to_ents, keys, values, d_context, lse, row_inner, d_to_words, d_to_ents, d_keys, d_values
):
    masks = head_masks(counts)
    scale = HEAD ** (-0.5)
    one, two, three, four = [], [], [], []
    for h in range(2):
        cols = slice(h * HEAD, (h + 1) * HEAD)
        scores = scores_of(masks[h], keys[...], to_words[...], to_ents[...])
        probs = jnp.exp(scores - lse[h : h + 1, :])
        d_probs = dot(values[...] * masks[h][0], d_context[...], NT)
        d_scores = (probs * (d_probs - row_inner[h : h + 1, :])).astype(bf16)
        one.append(dot(keys[:WORDS, cols], d_scores[:WORDS], TN))
        two.append(dot(keys[WORDS:, cols], d_scores[WORDS:], TN))
        three.append(
            jnp.concatenate(
                [
                    dot(d_scores[:WORDS], to_words[:, cols], NN),
                    dot(d_scores[WORDS:], to_ents[:, cols], NN),
                ],
                0,
            )
        )
        four.append(dot(probs.astype(bf16), d_context[:, cols], NN))
    d_to_words[...] = (jnp.concatenate(one, 0).T * scale).astype(bf16)
    d_to_ents[...] = (jnp.concatenate(two, 0).T * scale).astype(bf16)
    d_keys[...] = jnp.concatenate(three, 1).astype(bf16)
    d_values[...] = jnp.concatenate(four, 1).astype(bf16)


def attend_back(counts, to_words, to_ents, keys, values, d_context, lse, row_inner):
    pair = pl.BlockSpec((ROWS, 128), lambda i: (0, i))
    stat = pl.BlockSpec((None, 2, ROWS), lambda i: (i, 0, 0))
    return pl.pallas_call(
        attend_back_kernel,
        grid=(HEADS // 2,),
        in_specs=[SMEM] + [pair] * 5 + [stat] * 2,
        out_specs=[pair] * 4,
        out_shape=[shape((ROWS, D), bf16)] * 4,
        compiler_params=PARAMS,
        cost_estimate=cost(16 * ROWS * ROWS * D, 12000000),
        name="attend_back",
    )(counts, to_words, to_ents, keys, values, d_context, lse, row_inner)


def grad_red_kernel(d_ffn, activated, send, keep, whole):
    wide, narrow = coords()
    for core in range(2):
        out = keep if core == 0 else send
        for x in range(2):
            n = narrow ^ (x * 2 + core)
            lanes = pl.ds(pl.multiple_of(n * D, D), D)
            whole[...] = dot(d_ffn[...], activated[:, lanes], TN)
            for w in range(8):
                away = wide ^ w
                y, low, high = away % 2, (away // 2) % 2, away // 4
                out[0, x, y, low, high] = whole[w * 96 : w * 96 + 48].astype(bf16)
                out[1, y, x, low, high] = whole[w * 96 + 48 : w * 96 + 96].astype(bf16)


def grad_red(d_ffn, activated):
    block = shape((2, 2, 2, 2, 2, 48, D), bf16)
    return pl.pallas_call(
        grad_red_kernel,
        in_specs=[VMEM] * 2,
        out_specs=[VMEM] * 2,
        out_shape=[block, block],
        scratch_shapes=[pltpu.VMEM((D, D), f32)],
        compiler_params=PARAMS,
        cost_estimate=cost(2 * ROWS * D * FF, 10000000),
        name="grad_red",
    )(d_ffn, activated)


def grad_exp_kernel(middle_low, d_inner, d_out, context, send, keep, whole):
    wide, narrow = coords()
    for z in range(4):
        away_z = (wide // 2) ^ z
        low, high = away_z % 2, away_z // 2
        whole[...] = dot(middle_low[...], d_inner[:, z * D : (z + 1) * D], TN)
        for y in range(2):
            w = z * 2 + y
            away_y = (wide ^ w) % 2
            for x in range(2):
                for core in range(2):
                    out = keep if core == 0 else send
                    n = narrow ^ (x * 2 + core)
                    for half in range(2):
                        rows = pl.ds(pl.multiple_of(n * 192 + half * 96, 16), 96)
                        value = whole[rows, y * 384 : (y + 1) * 384].astype(bf16)
                        if half == 0:
                            out[0, x, away_y, low, high, :96] = value
                        else:
                            out[1, away_y, x, low, high, :96] = value
    whole[...] = dot(d_out[...], context[...], TN)
    store_attention(whole, send, keep, 96, (24, 24))


def store_attention(whole, send, keep, at, halves):
    wide, narrow = coords()
    for w in range(8):
        away = wide ^ w
        y, low, high = away % 2, (away // 2) % 2, away // 4
        for x in range(2):
            for core in range(2):
                out = keep if core == 0 else send
                n = narrow ^ (x * 2 + core)
                lanes = pl.ds(pl.multiple_of((n // 2) * 384, 128), 384)
                start = w * 96 + (n % 2) * 48
                for half in range(2):
                    if not halves[half]:
                        continue
                    skip = halves[0] if half else 0
                    rows = pl.ds(pl.multiple_of(start + skip, 8), halves[half])
                    value = whole[rows, lanes].astype(bf16)
                    if half == 0:
                        out[0, x, y, low, high, at : at + halves[0]] = value
                    else:
                        out[1, y, x, low, high, at : at + halves[1]] = value


def grad_exp(middle_low, d_inner, d_out, context):
    block = shape((2, 2, 2, 2, 2, 120, 384), bf16)
    return pl.pallas_call(
        grad_exp_kernel,
        in_specs=[VMEM] * 4,
        out_specs=[VMEM] * 2,
        out_shape=[block, block],
        scratch_shapes=[pltpu.VMEM((D, D), f32)],
        compiler_params=PARAMS,
        cost_estimate=cost(2 * ROWS * D * (FF + D), 12000000),
        name="grad_exp",
    )(middle_low, d_inner, d_out, context)


def grad_att_kernel(low, d_to_words, d_to_ents, d_keys, d_values, send, keep, whole):
    word = low[:WORDS]
    ent = low[WORDS:]
    work = (
        (d_keys, slice(0, ROWS), 0, 0),
        (d_to_words, slice(0, WORDS), 0, 48),
        (d_to_words, slice(WORDS, ROWS), 0, 96),
        (d_values, slice(0, ROWS), 1, 0),
        (d_to_ents, slice(0, WORDS), 1, 48),
        (d_to_ents, slice(WORDS, ROWS), 1, 96),
    )
    for ref, rows, half, at in work:
        whole[...] = dot(ref[rows, :], low[rows, :], TN)
        store_attention(whole, send, keep, at, (48, 0) if half == 0 else (0, 48))


def grad_att(low, d_to_words, d_to_ents, d_keys, d_values):
    block = shape((2, 2, 2, 2, 2, 144, 384), bf16)
    return pl.pallas_call(
        grad_att_kernel,
        in_specs=[VMEM] * 5,
        out_specs=[VMEM] * 2,
        out_shape=[block, block],
        scratch_shapes=[pltpu.VMEM((D, D), f32)],
        compiler_params=PARAMS,
        cost_estimate=cost(2 * ROWS * D * D * 4, 12000000),
        name="grad_att",
    )(low, d_to_words, d_to_ents, d_keys, d_values)


def grad_hidden_kernel(d_first, d_to_words, d_to_ents, d_keys, d_values, kv, q, word, ent):
    shared = d_first[...] + dot(d_keys[...], kv[0], NN) + dot(d_values[...], kv[1], NN)
    word[...] = (
        shared[:WORDS] + dot(d_to_words[:WORDS], q[0], NN) + dot(d_to_ents[:WORDS], q[2], NN)
    )
    ent[...] = (
        shared[WORDS:] + dot(d_to_words[WORDS:], q[1], NN) + dot(d_to_ents[WORDS:], q[3], NN)
    )


def grad_hidden(*args):
    return pl.pallas_call(
        grad_hidden_kernel,
        in_specs=[VMEM] * 7,
        out_specs=[VMEM] * 2,
        out_shape=[shape((WORDS, D), f32), shape((ENTS, D), f32)],
        compiler_params=PARAMS,
        cost_estimate=cost(2 * ROWS * D * D * 4, 16000000),
        name="grad_hidden",
    )(*args)


def flip(axis, bit, value):
    size = lax.axis_size(axis)
    return lax.ppermute(value, axis, [(i, i ^ bit) for i in range(size)])


def over(name, value):
    axis, bit = {
        "core": ("narrow", 1),
        "x": ("narrow", 2),
        "y": ("wide", 1),
        "low": ("wide", 2),
        "high": ("wide", 4),
    }[name]
    return flip(axis, bit, value)


def gather_pair(first, second):
    cut = first.shape[0]
    both = jnp.concatenate([first, second], 0)
    both = jnp.stack([both, over("high", both)], 0)
    got = over("low", both)
    left = jnp.stack([both[:, :cut], got[:, :cut]], 0)
    right = jnp.stack([both[:, cut:], got[:, cut:]], 0)
    left = jnp.stack([left, over("x", left)], 0)
    right = jnp.stack([right, over("y", right)], 0)
    left_far = over("y", left)
    right_far = over("x", right)
    left_core = over("core", left)
    right_core = over("core", right)
    return (
        (left, left_far, left_core, over("core", left_far)),
        (right, right_far, right_core, over("core", right_far)),
    )


def plus(kept, got, at):
    return (kept[at].astype(f32) + got[at].astype(f32)).astype(bf16)


def scatter_pair(send, keep):
    got = over("core", send)
    left = over("x", plus(keep, got, (0, 1)))
    right = over("y", plus(keep, got, (1, 1)))
    keep_left = plus(keep, got, (0, 0))
    keep_right = plus(keep, got, (1, 0))
    left_two = over("y", plus(keep_left, left, 1))
    right_two = over("x", plus(keep_right, right, 1))
    keep_left = plus(keep_left, left, 0)
    keep_right = plus(keep_right, right, 0)
    keep = jnp.stack([plus(keep_left, left_two, ()), plus(keep_right, right_two, ())], 1)
    got = over("low", keep[1])
    keep = (keep[0].astype(f32) + got.astype(f32)).astype(bf16)
    got = over("high", keep[:, 1])
    return keep[:, 0].astype(f32) + got.astype(f32)


def sum_all(value):
    size = lax.axis_size("wide") * lax.axis_size("narrow")
    spread = jnp.broadcast_to(value[None], (size,) + value.shape)
    got = lax.all_to_all(spread, ("wide", "narrow"), 0, 0, tiled=False)
    return jnp.sum(got, axis=0)


def adapt(weight, grad, first, second, decay):
    first = 0.5 * first + 0.5 * grad
    second = 0.5 * second + 0.5 * grad * grad
    fix_first = 1.0 - 0.5**STEP
    fix_second = 1.0 - 0.5**STEP
    update = first / fix_first / (jnp.sqrt(second / fix_second) + adam_eps) + decay * weight
    return (first, second, update)


def shards(
    fast,
    word_states,
    entity_states,
    seq_counts,
    attention_weight,
    expand_weight,
    reduce_weight,
    norm_params,
    moment_attention,
    moment_expand,
    moment_reduce,
    moment_norms,
    square_attention,
    square_expand,
    square_reduce,
    square_norms,
    word_cotangent,
    entity_cotangent,
):
    word, ent, counts = word_states[0], entity_states[0], seq_counts[0]
    core = lax.axis_index("narrow") % 2
    if fast:
        keep, send, exp_low, red_low, weight_local = prep(
            attention_weight, expand_weight, reduce_weight
        )
        got = over("core", send)
        rows = jnp.where(
            core == 0, jnp.concatenate([keep, got], 2), jnp.concatenate([got, keep], 2)
        )
        kv = gather_pair(rows[4], rows[5])
        query = gather_pair(
            jnp.concatenate([rows[0], rows[2]], 0), jnp.concatenate([rows[1], rows[3]], 0)
        )
        feed_one = gather_pair(
            jnp.concatenate([exp_low[:96], rows[6]], 0), red_low[:, :48].reshape(96, 384)
        )
        feed_two = gather_pair(exp_low[96:], red_low[:, 48:].reshape(96, 384))
        kv_pieces = [
            v.reshape(v.shape[:3] + (1, 48, 384)) for half in kv for v in half
        ]
        query_pieces = [
            v.reshape(v.shape[:3] + (2, 48, 384)) for half in query for v in half
        ]
        feed_pieces = [v for pair in (feed_one, feed_two) for half in pair for v in half]
    else:
        weight_local = jnp.concatenate(
            [
                jnp.sum(attention_weight * attention_weight, axis=(1, 2)),
                jnp.sum(expand_weight * expand_weight)[None],
                jnp.sum(reduce_weight * reduce_weight)[None],
            ]
        )
        turned = jnp.swapaxes(attention_weight.astype(bf16), 1, 2)
        turned = lax.all_gather(turned, "wide", axis=1, tiled=True)
        turned = lax.all_gather(turned, "narrow", axis=2, tiled=True)
        exp_all = lax.all_gather(expand_weight.astype(bf16), "wide", axis=1, tiled=True)
        exp_all = lax.all_gather(exp_all, "narrow", axis=0, tiled=True)
        red_all = lax.all_gather(reduce_weight.astype(bf16).T, "wide", axis=0, tiled=True)
        red_all = lax.all_gather(red_all, "narrow", axis=1, tiled=True)
        kv_pieces = query_pieces = [turned]
        feed_pieces = [turned, exp_all, red_all]

    low, keys, values, kv_all = project_kv(fast, word, ent, kv_pieces)
    to_words, to_ents, q_all = project_q(fast, low, query_pieces)
    context, exact, lse = attend(counts, to_words, to_ents, keys, values)
    (
        word_out,
        ent_out,
        middle_low,
        activated,
        slope,
        d_second,
        d_ffn,
        unit_one,
        inverse_one,
        grads_two,
        out_all,
        exp_all,
        red_all,
    ) = feed(
        fast, word, ent, context, norm_params, word_cotangent[0], entity_cotangent[0], feed_pieces
    )
    if fast:
        red_sum = scatter_pair(*grad_red(d_ffn, activated))
    d_inner, d_first, d_out, d_context, row_inner, grads_one = feed_back(
        d_ffn,
        red_all,
        exp_all,
        slope,
        d_second,
        unit_one,
        inverse_one,
        norm_params,
        out_all,
        exact,
    )
    if fast:
        exp_sum = scatter_pair(*grad_exp(middle_low, d_inner, d_out, context))
    d_to_words, d_to_ents, d_keys, d_values = attend_back(
        counts, to_words, to_ents, keys, values, d_context, lse, row_inner
    )
    if fast:
        att_sum = scatter_pair(*grad_att(low, d_to_words, d_to_ents, d_keys, d_values))
    word_grad, ent_grad = grad_hidden(
        d_first, d_to_words, d_to_ents, d_keys, d_values, kv_all, q_all
    )
    early = jnp.concatenate([grads_one, grads_two], 0)
    early = jnp.concatenate([early, jnp.pad(weight_local, (0, D - 9))[None]], 0)
    early = jnp.sum(lax.all_gather(early, ("wide", "narrow"), axis=0, tiled=False), axis=0)
    norm_grads = early[:4]
    weight_total = early[4, :9]

    if fast:
        out_rows = jnp.concatenate([exp_sum[0, 96:], exp_sum[1, 96:]], 0)
        rows = jnp.stack(
            [
                att_sum[0, 48:96],
                att_sum[1, 48:96],
                att_sum[0, 96:],
                att_sum[1, 96:],
                att_sum[0, :48],
                att_sum[1, :48],
                out_rows,
            ]
        ).astype(bf16)
        near, far = rows[:, :, :192], rows[:, :, 192:]
        got = over("core", jnp.where(core == 0, far, near))
        own = jnp.where(core == 0, near, far)
        turned = jnp.where(
            core == 0, jnp.concatenate([own, got], 1), jnp.concatenate([got, own], 1)
        )
        att_grad = jnp.swapaxes(turned.astype(f32), 1, 2)
        exp_grad = jnp.concatenate([exp_sum[0, :96], exp_sum[1, :96]], 0)
        red_grad = jnp.concatenate([red_sum[0], red_sum[1]], 0).T
    else:
        words, ents = low[:WORDS], low[WORDS:]
        turned = jnp.stack(
            [
                dot(d_to_words[:WORDS], words, TN),
                dot(d_to_ents[:WORDS], words, TN),
                dot(d_to_words[WORDS:], ents, TN),
                dot(d_to_ents[WORDS:], ents, TN),
                dot(d_keys, low, TN),
                dot(d_values, low, TN),
                dot(d_out, context, TN),
            ]
        ).astype(bf16)
        turned = lax.psum_scatter(turned, "wide", scatter_dimension=1, tiled=True)
        turned = lax.psum_scatter(turned, "narrow", scatter_dimension=2, tiled=True)
        att_grad = jnp.swapaxes(turned.astype(f32), 1, 2)
        grad = dot(middle_low, d_inner, TN).astype(bf16)
        grad = lax.psum_scatter(grad, "wide", scatter_dimension=1, tiled=True)
        grad = lax.psum_scatter(grad, "narrow", scatter_dimension=0, tiled=True)
        exp_grad = grad.astype(f32)
        grad = dot(d_ffn, activated, TN).astype(bf16)
        grad = lax.psum_scatter(grad, "wide", scatter_dimension=0, tiled=True)
        grad = lax.psum_scatter(grad, "narrow", scatter_dimension=1, tiled=True)
        red_grad = grad.astype(f32).T

    att_first, att_second, att_update = adapt(
        attention_weight, att_grad, moment_attention, square_attention, matrix_decay
    )
    exp_first, exp_second, exp_update = adapt(
        expand_weight, exp_grad, moment_expand, square_expand, matrix_decay
    )
    red_first, red_second, red_update = adapt(
        reduce_weight, red_grad, moment_reduce, square_reduce, matrix_decay
    )
    update_local = jnp.concatenate(
        [
            jnp.sum(att_update * att_update, axis=(1, 2)),
            jnp.sum(exp_update * exp_update)[None],
            jnp.sum(red_update * red_update)[None],
        ]
    )
    update_total = sum_all(update_local)
    nrm_first, nrm_second, nrm_update = adapt(
        norm_params, norm_grads, moment_norms, square_norms, 0.0
    )
    weight_norm = jnp.sqrt(
        jnp.concatenate([weight_total, jnp.sum(norm_params * norm_params, axis=1)])
    )
    update_norm = jnp.sqrt(
        jnp.concatenate([update_total, jnp.sum(nrm_update * nrm_update, axis=1)])
    )
    trust = weight_norm / update_norm
    new_attention = attention_weight - learn_rate * trust[0:7, None, None] * att_update
    new_expand = expand_weight - learn_rate * trust[7] * exp_update
    new_reduce = reduce_weight - learn_rate * trust[8] * red_update
    new_norms = norm_params - learn_rate * trust[9:13, None] * nrm_update
    trust_stats = jnp.stack([jnp.log(weight_norm), jnp.log(update_norm), jnp.log(trust)], 1)
    return (
        word_out[None],
        ent_out[None],
        word_grad[None],
        ent_grad[None],
        new_attention,
        new_expand,
        new_reduce,
        new_norms,
        att_first,
        exp_first,
        red_first,
        nrm_first,
        att_second,
        exp_second,
        red_second,
        nrm_second,
        trust_stats,
    )


def solution(mesh):
    fast = mesh.shape["wide"] == 8 and mesh.shape["narrow"] == 4
    rows = P(("wide", "narrow"), None, None)
    matrix = P("narrow", "wide")
    stack = P(None, "narrow", "wide")
    weights = (stack, matrix, matrix, P())
    return jax.shard_map(
        functools.partial(shards, fast),
        mesh=mesh,
        in_specs=(rows, rows, P(("wide", "narrow"), None)) + weights * 3 + (rows, rows),
        out_specs=(rows,) * 4 + weights * 3 + (P(),),
        check_vma=False,
    )
```

```python
import functools

import jax
import jax.numpy as jnp
from jax import lax
from jax.experimental import pallas as pl
from jax.experimental.pallas import tpu as pltpu
from jax.sharding import PartitionSpec as P

D = 768
FF = 3072
HEADS = 12
HEAD = 64
WORDS = 512
ENTS = 128
ROWS = WORDS + ENTS
STEP = 7

eps_norm = 1e-05
adam_eps = 1e-06
matrix_decay = 0.01
learn_rate = 0.5
masked_score = -1e30

f32 = jnp.float32
bf16 = jnp.bfloat16
NN = (((1,), (0,)), ((), ()))
NT = (((1,), (1,)), ((), ()))
TN = (((0,), (0,)), ((), ()))
VMEM = pl.BlockSpec(memory_space=pltpu.VMEM)
SMEM = pl.BlockSpec(memory_space=pltpu.SMEM)
ANY = pl.BlockSpec(memory_space=pl.ANY)
COST_RATE = 4e9
PARAMS = pltpu.CompilerParams(vmem_limit_bytes=60 * 2**20)


def dot(left, right, dims):
    return lax.dot_general(left, right, dims, preferred_element_type=f32)


def shape(dims, dtype):
    return jax.ShapeDtypeStruct(dims, dtype)


def tokens(values):
    return [v for v in values if v is not None]


def cost(us, rate=COST_RATE):
    return pl.CostEstimate(flops=int(us * rate), bytes_accessed=0, transcendentals=0)


def away_blocks():
    for core in range(2):
        for outer in range(2):
            for lead in range(2):
                for low in range(2):
                    for high in range(2):
                        yield core, outer, lead, low, high


def places(wide, narrow, second, block):
    core, outer, lead, low, high = block
    x_away, y_away = (outer, lead) if second else (lead, outer)
    w = wide ^ (high * 4 + low * 2 + y_away)
    n = narrow ^ (x_away * 2 + core)
    return w, n


def piece_of(bufs, block):
    core, outer, lead, low, high = block
    return bufs[core * 2 + outer].at[lead, low, high]


def coords():
    return lax.axis_index("wide"), lax.axis_index("narrow")


def start_attention(bufs, second, target, slots, sem):
    wide, narrow = coords()
    for block in away_blocks():
        w, n = places(wide, narrow, second, block)
        row = pl.multiple_of(w * 96 + (n % 2) * 48, 16)
        lane = pl.multiple_of((n // 2) * 384, 128)
        src = piece_of(bufs, block)
        pltpu.make_async_copy(src, target.at[slots, pl.ds(row, 48), pl.ds(lane, 384)], sem).start()


def drain(ref, sem):
    pltpu.make_async_copy(ref, ref, sem).wait()


def prep_kernel(att, exp, red, keep, send, exp_low, red_low, sums):
    narrow = lax.axis_index("narrow")
    core = narrow % 2
    total = []
    for i in range(7):
        value = att[i]
        total.append(jnp.sum(value * value))
        turned = value.T.astype(bf16)
        halves = turned.reshape(2, 48, 192)

        @pl.when(core == 0)
        def _():
            keep[i] = halves[0]
            send[i] = halves[1]

        @pl.when(core == 1)
        def _():
            keep[i] = halves[1]
            send[i] = halves[0]

    value = exp[...]
    total.append(jnp.sum(value * value))
    exp_low[...] = value.astype(bf16)
    value = red[...]
    total.append(jnp.sum(value * value))
    red_low[...] = value.astype(bf16)
    for i in range(9):
        sums[i] = total[i]


def prep(att, exp, red):
    return pl.pallas_call(
        prep_kernel,
        in_specs=[VMEM] * 3,
        out_specs=[VMEM] * 4 + [SMEM],
        out_shape=[
            shape((7, 48, 192), bf16),
            shape((7, 48, 192), bf16),
            shape((192, 384), bf16),
            shape((96, D), bf16),
            shape((9,), f32),
        ],
        compiler_params=PARAMS,
        name="prep",
    )(att, exp, red)


def pick_rows(source, mine, other):
    core = lax.axis_index("narrow") % 2
    for c in range(2):

        @pl.when(core == c)
        def _():
            for target, at in ((mine, c * 192), (other, 192 - c * 192)):
                target[:, :192] = source[:, at : at + 192]
                target[:, 192:] = source[:, at + 384 : at + 576]


def pick_tiles(source, mine, other):
    core = lax.axis_index("narrow") % 2
    for c in range(2):

        @pl.when(core == c)
        def _():
            for target, at in ((mine, c * 192), (other, 192 - c * 192)):
                target[:, :128] = source[:, at : at + 128]
                target[:, 128:256] = source[:, at + 384 : at + 512]
                target[:, 256:320] = source[:, at + 128 : at + 192]
                target[:, 320:] = source[:, at + 512 : at + 576]


def project_kv_kernel(fast, n_after, word, ent, *refs):
    if fast:
        first, second, refs = refs[:4], refs[4:8], refs[8:]
    else:
        whole, refs = refs[0], refs[1:]
    low, keys, values, mine, other, saved, target, sem, sem_save = refs[n_after:]
    if fast:
        start_attention(first, False, target, pl.ds(0, 1), sem)
        start_attention(second, True, target, pl.ds(1, 1), sem)
    else:
        pltpu.make_async_copy(whole.at[pl.ds(4, 2)], target, sem).start()
    low[:WORDS] = word[...].astype(bf16)
    low[WORDS:] = ent[...].astype(bf16)
    pick_tiles(low, mine, other)
    drain(target, sem)
    save = pltpu.make_async_copy(target, saved, sem_save)
    save.start()
    keys[...] = dot(low[...], target[0], NT).astype(bf16)
    values[...] = dot(low[...], target[1], NT).astype(bf16)
    save.wait()


def project_kv(fast, word, ent, pieces, after=()):
    after = tokens(after)
    return pl.pallas_call(
        functools.partial(project_kv_kernel, fast, len(after)),
        in_specs=[VMEM, VMEM] + [ANY] * (len(pieces) + len(after)),
        out_specs=[VMEM] * 5 + [ANY],
        out_shape=[shape((ROWS, D), bf16)] * 3
        + [shape((ROWS, D // 2), bf16)] * 2
        + [shape((2, D, D), bf16)],
        scratch_shapes=[
            pltpu.VMEM((2, D, D), bf16),
            pltpu.SemaphoreType.DMA,
            pltpu.SemaphoreType.DMA,
        ],
        compiler_params=PARAMS,
        cost_estimate=cost(6, 4e8),
        name="project_kv",
    )(word, ent, *pieces, *after)


def project_q_kernel(fast, n_after, low, *refs):
    if fast:
        first, second, refs = refs[:4], refs[4:8], refs[8:]
    else:
        whole, refs = refs[0], refs[1:]
    to_words, to_ents, saved, target, sem, sem_save = refs[n_after:]
    if fast:
        start_attention(first, False, target, pl.ds(0, 2), sem)
        start_attention(second, True, target, pl.ds(2, 2), sem)
    else:
        for slot, k in enumerate((0, 2, 1, 3)):
            pltpu.make_async_copy(whole.at[k], target.at[slot], sem).start()
    drain(target, sem)
    save = pltpu.make_async_copy(target, saved, sem_save)
    save.start()
    scale = HEAD ** (-0.5)
    word = low[:WORDS]
    ent = low[WORDS:]
    to_words[:WORDS] = (dot(word, target[0], NT) * scale).astype(bf16)
    to_words[WORDS:] = (dot(ent, target[1], NT) * scale).astype(bf16)
    to_ents[:WORDS] = (dot(word, target[2], NT) * scale).astype(bf16)
    to_ents[WORDS:] = (dot(ent, target[3], NT) * scale).astype(bf16)
    save.wait()


def project_q(fast, low, pieces, after=()):
    after = tokens(after)
    return pl.pallas_call(
        functools.partial(project_q_kernel, fast, len(after)),
        in_specs=[VMEM] + [ANY] * (len(pieces) + len(after)),
        out_specs=[VMEM] * 2 + [ANY],
        out_shape=[shape((ROWS, D), bf16)] * 2 + [shape((4, D, D), bf16)],
        scratch_shapes=[
            pltpu.VMEM((4, D, D), bf16),
            pltpu.SemaphoreType.DMA,
            pltpu.SemaphoreType.DMA,
        ],
        compiler_params=PARAMS,
        cost_estimate=cost(7, 4e8),
        name="project_q",
    )(low, *pieces, *after)


def head_masks(counts):
    lane = lax.broadcasted_iota(jnp.int32, (ROWS, 128), 1)
    row = lax.broadcasted_iota(jnp.int32, (ROWS, 128), 0)
    edge = jnp.where(row < WORDS, counts[0], counts[1] + WORDS)
    bias = jnp.where(row < edge, 0.0, masked_score)
    out = []
    for h in range(2):
        own = jnp.where((lane < HEAD) if h == 0 else (lane >= HEAD), 1.0, 0.0).astype(bf16)
        mark = jnp.where(lane == (HEAD if h == 0 else 0), 1.0, 0.0)
        rest = (1.0 - mark).astype(bf16)
        tag = (bias * mark).astype(bf16)
        out.append((own, mark.astype(bf16), rest, tag))
    return out


def scores_of(masks, keys, to_words, to_ents):
    own, mark, rest, tag = masks
    tagged = keys * own + tag
    upper = dot(tagged[:WORDS], to_words * rest + mark, NT)
    lower = dot(tagged[WORDS:], to_ents * rest + mark, NT)
    return jnp.concatenate([upper, lower], 0)


def attend_kernel(n_after, counts, to_words, to_ents, keys, values, *refs):
    context, exact, lse = refs[n_after:]
    masks = head_masks(counts)
    outs = []
    for h in range(2):
        scores = scores_of(masks[h], keys[...], to_words[...], to_ents[...])
        top = jnp.max(scores, axis=0, keepdims=True)
        expd = jnp.exp(scores - top)
        total = jnp.sum(expd, axis=0, keepdims=True)
        lse[h : h + 1, :] = top + jnp.log(total)
        mixed = dot(values[:, h * HEAD : (h + 1) * HEAD], expd.astype(bf16), TN)
        outs.append(mixed * (1.0 / total))
    joined = jnp.concatenate(outs, 0).T
    exact[...] = joined
    context[...] = joined.astype(bf16)


def attend(counts, to_words, to_ents, keys, values, after=()):
    after = tokens(after)
    pair = pl.BlockSpec((ROWS, 128), lambda i: (0, i))
    stat = pl.BlockSpec((None, 2, ROWS), lambda i: (i, 0, 0))
    return pl.pallas_call(
        functools.partial(attend_kernel, len(after)),
        grid=(HEADS // 2,),
        in_specs=[SMEM, pair, pair, pair, pair] + [ANY] * len(after),
        out_specs=[pair, pair, stat],
        out_shape=[
            shape((ROWS, D), bf16),
            shape((ROWS, D), f32),
            shape((HEADS // 2, 2, ROWS), f32),
        ],
        compiler_params=PARAMS,
        cost_estimate=cost(12, 4e8),
        name="attend",
    )(counts, to_words, to_ents, keys, values, *after)


def normed(value):
    center = value - jnp.mean(value, axis=-1, keepdims=True)
    spread = jnp.mean(center * center, axis=-1, keepdims=True)
    inverse = lax.rsqrt(spread + eps_norm)
    return center * inverse, inverse


def normed_back(unit, inverse, cotangent):
    mean = jnp.mean(cotangent, axis=-1, keepdims=True)
    inner = jnp.mean(cotangent * unit, axis=-1, keepdims=True)
    return inverse * (cotangent - mean - unit * inner)


def column_sum(value):
    return jnp.sum(value, axis=0, keepdims=True)


def feed_in_kernel(fast, n_after, word, ent, context, norms, *refs):
    if fast:
        bufs, refs = (refs[0:4], refs[4:8]), refs[8:]
    else:
        bufs, refs = refs[0:2], refs[2:]
    (
        middle,
        middle_low,
        activated,
        slope,
        unit_one,
        inverse_one,
        middle_mine,
        middle_other,
        context_mine,
        context_other,
        out_saved,
        exp_saved,
        out_all,
        exp_all,
        sem_out,
        sem_exp,
        sem_save,
    ) = refs[n_after:]
    step = pl.program_id(0)
    save_out = pltpu.make_async_copy(out_all, out_saved, sem_save.at[0])
    save_exp = pltpu.make_async_copy(exp_all, exp_saved, sem_save.at[1])

    @pl.when(step == 0)
    def _():
        if fast:
            start_feed_in(bufs, out_all, exp_all, sem_out, sem_exp)
        else:
            pltpu.make_async_copy(bufs[0].at[6], out_all, sem_out).start()
            for j in range(4):
                cols = pl.ds(j * D, D)
                pltpu.make_async_copy(bufs[1].at[:, cols], exp_all.at[j], sem_exp).start()
        drain(out_all, sem_out)
        save_out.start()
        hidden = jnp.concatenate([word[...], ent[...]], 0)
        unit, inverse = normed(hidden + dot(context[...], out_all[...], NT))
        value = unit * norms[0:1, :] + norms[1:2, :]
        unit_one[...] = unit
        inverse_one[...] = inverse
        middle_low[...] = value.astype(bf16)
        middle[...] = value
        pick_rows(middle_low, middle_mine, middle_other)
        pick_tiles(context, context_mine, context_other)
        drain(exp_all, sem_exp)
        save_exp.start()

    inner = dot(middle_low[...], exp_all[step], NN)
    share = 0.5 + 0.5 * lax.erf(inner * 0.7071067811865476)
    bell = jnp.exp(-0.5 * inner * inner) * 0.3989422804014327
    slope[...] = (share + inner * bell).astype(bf16)
    activated[...] = (inner * share).astype(bf16)

    @pl.when(step == 3)
    def _():
        save_out.wait()
        save_exp.wait()


def start_feed_in(bufs, out_all, exp_all, sem_out, sem_exp):
    wide, narrow = coords()
    for block in away_blocks():
        w, n = places(wide, narrow, False, block)
        row = pl.multiple_of(w * 96 + (n % 2) * 48, 16)
        lane = pl.multiple_of((n // 2) * 384, 128)
        src = piece_of(bufs[0], block).at[pl.ds(96, 48)]
        pltpu.make_async_copy(src, out_all.at[pl.ds(row, 48), pl.ds(lane, 384)], sem_out).start()
    for half in range(2):
        for block in away_blocks():
            w, n = places(wide, narrow, half == 1, block)
            src = piece_of(bufs[half], block)
            if half == 0:
                src = src.at[pl.ds(0, 96)]
            row = pl.multiple_of(n * 192 + half * 96, 16)
            lane = pl.multiple_of((w % 2) * 384, 128)
            dst = exp_all.at[w // 2, pl.ds(row, 96), pl.ds(lane, 384)]
            pltpu.make_async_copy(src, dst, sem_exp).start()


def feed_in(fast, word, ent, context, norms, pieces, after=()):
    after = tokens(after)
    column = pl.BlockSpec((ROWS, D), lambda i: (0, i))
    return pl.pallas_call(
        functools.partial(feed_in_kernel, fast, len(after)),
        grid=(4,),
        in_specs=[VMEM] * 4 + [ANY] * (len(pieces) + len(after)),
        out_specs=[VMEM] * 2 + [column, column] + [VMEM] * 6 + [ANY] * 2,
        out_shape=[
            shape((ROWS, D), f32),
            shape((ROWS, D), bf16),
            shape((ROWS, FF), bf16),
            shape((ROWS, FF), bf16),
            shape((ROWS, D), f32),
            shape((ROWS, 1), f32),
            shape((ROWS, D // 2), bf16),
            shape((ROWS, D // 2), bf16),
            shape((ROWS, D // 2), bf16),
            shape((ROWS, D // 2), bf16),
            shape((D, D), bf16),
            shape((4, D, D), bf16),
        ],
        scratch_shapes=[
            pltpu.VMEM((D, D), bf16),
            pltpu.VMEM((4, D, D), bf16),
            pltpu.SemaphoreType.DMA,
            pltpu.SemaphoreType.DMA,
            pltpu.SemaphoreType.DMA((2,)),
        ],
        compiler_params=PARAMS,
        cost_estimate=cost(15),
        name="feed_in",
    )(word, ent, context, norms, *pieces, *after)


def feed_out_kernel(fast, n_after, activated, middle, norms, word_cot, ent_cot, *refs):
    if fast:
        bufs, refs = (refs[0:4], refs[4:8]), refs[8:]
    else:
        bufs, refs = refs[0:1], refs[1:]
    (
        word_out,
        ent_out,
        d_second,
        d_ffn,
        grads_two,
        red_saved,
        total,
        red_all,
        sem_red,
        sem_save,
    ) = refs[n_after:]
    step = pl.program_id(0)
    save = pltpu.make_async_copy(red_all, red_saved, sem_save)

    @pl.when(step == 0)
    def _():
        if fast:
            start_feed_out(bufs, red_all, sem_red)
        else:
            for j in range(4):
                cols = pl.ds(j * D, D)
                pltpu.make_async_copy(bufs[0].at[:, cols], red_all.at[j], sem_red).start()
        total[...] = middle[...]
        drain(red_all, sem_red)
        save.start()

    total[...] += dot(activated[...], red_all[step], NT)

    @pl.when(step == 3)
    def _():
        unit, inverse = normed(total[...])
        result = unit * norms[2:3, :] + norms[3:4, :]
        word_out[...] = result[:WORDS]
        ent_out[...] = result[WORDS:]
        cot = jnp.concatenate([word_cot[...], ent_cot[...]], 0)
        grads_two[0:1, :] = column_sum(cot * unit)
        grads_two[1:2, :] = column_sum(cot)
        back = normed_back(unit, inverse, cot * norms[2:3, :])
        d_second[...] = back
        d_ffn[...] = back.astype(bf16)
        save.wait()


def start_feed_out(bufs, red_all, sem_red):
    wide, narrow = coords()
    for half in range(2):
        for block in away_blocks():
            w, n = places(wide, narrow, half == 1, block)
            src = piece_of(bufs[half], block)
            row = pl.multiple_of(w * 96 + half * 48, 16)
            pltpu.make_async_copy(src, red_all.at[n, pl.ds(row, 48)], sem_red).start()


def feed_out(fast, activated, middle, norms, word_cot, ent_cot, pieces, after=()):
    after = tokens(after)
    column = pl.BlockSpec((ROWS, D), lambda i: (0, i))
    return pl.pallas_call(
        functools.partial(feed_out_kernel, fast, len(after)),
        grid=(4,),
        in_specs=[column] + [VMEM] * 4 + [ANY] * (len(pieces) + len(after)),
        out_specs=[VMEM] * 5 + [ANY],
        out_shape=[
            shape((WORDS, D), f32),
            shape((ENTS, D), f32),
            shape((ROWS, D), f32),
            shape((ROWS, D), bf16),
            shape((2, D), f32),
            shape((4, D, D), bf16),
        ],
        scratch_shapes=[
            pltpu.VMEM((ROWS, D), f32),
            pltpu.VMEM((4, D, D), bf16),
            pltpu.SemaphoreType.DMA,
            pltpu.SemaphoreType.DMA,
        ],
        compiler_params=PARAMS,
        cost_estimate=cost(13),
        name="feed_out",
    )(activated, middle, norms, word_cot, ent_cot, *pieces, *after)


def feed_back_one_kernel(n_after, d_ffn, red_all, exp_all, slope, d_second, *refs):
    d_inner, total = refs[n_after:]
    step = pl.program_id(0)
    back = (dot(d_ffn[...], red_all[...], NN) * slope[...].astype(f32)).astype(bf16)
    d_inner[...] = back

    @pl.when(step == 0)
    def _():
        total[...] = d_second[...]

    total[...] += dot(back, exp_all[...], NT)


def feed_back_one(first, d_ffn, red_all, exp_all, slope, d_second, after=()):
    after = tokens(after)
    wide = pl.BlockSpec((ROWS, D), lambda i: (0, i + first))
    column = pl.BlockSpec((ROWS, D), lambda i: (0, i))
    part = pl.BlockSpec((None, D, D), lambda i: (i + first, 0, 0))
    return pl.pallas_call(
        functools.partial(feed_back_one_kernel, len(after)),
        grid=(2,),
        in_specs=[VMEM, part, part, wide, VMEM] + [ANY] * len(after),
        out_specs=[column, VMEM],
        out_shape=[shape((ROWS, FF // 2), bf16), shape((ROWS, D), f32)],
        compiler_params=PARAMS,
        cost_estimate=cost(10),
        name="feed_back_one",
    )(d_ffn, red_all, exp_all, slope, d_second, *after)


def feed_back_two_kernel(
    n_after, d_ffn, red_all, exp_all, slope, d_second, unit_one, inverse_one, norms, out_all, exact, *refs
):
    d_inner, d_first, d_out, d_context, row_inner, grads_one, total = refs[n_after:]
    step = pl.program_id(0)
    back = (dot(d_ffn[...], red_all[...], NN) * slope[...].astype(f32)).astype(bf16)
    d_inner[...] = back

    @pl.when(step == 0)
    def _():
        total[...] = d_second[...]

    total[...] += dot(back, exp_all[...], NT)

    @pl.when(step == 1)
    def _():
        d_middle = total[...]
        unit = unit_one[...]
        grads_one[0:1, :] = column_sum(d_middle * unit)
        grads_one[1:2, :] = column_sum(d_middle)
        first = normed_back(unit, inverse_one[...], d_middle * norms[0:1, :])
        d_first[...] = first
        d_out[...] = first.astype(bf16)
        context = dot(first.astype(bf16), out_all[...], NN).astype(bf16)
        d_context[...] = context
        product = context.astype(f32) * exact[...]
        head = lax.broadcasted_iota(jnp.int32, (16, D), 1) // HEAD
        pick = jnp.where(head == lax.broadcasted_iota(jnp.int32, (16, D), 0), 1.0, 0.0).astype(bf16)
        high = product.astype(bf16)
        low = (product - high.astype(f32)).astype(bf16)
        sums = dot(pick, high, NT) + dot(pick, low, NT)
        for i in range(HEADS // 2):
            row_inner[i] = sums[2 * i : 2 * i + 2]


def feed_back_two(
    first, d_ffn, red_all, exp_all, slope, d_second, unit_one, inverse_one, norms, out_all, exact, after=()
):
    after = tokens(after)
    wide = pl.BlockSpec((ROWS, D), lambda i: (0, i + first))
    column = pl.BlockSpec((ROWS, D), lambda i: (0, i))
    part = pl.BlockSpec((None, D, D), lambda i: (i + first, 0, 0))
    return pl.pallas_call(
        functools.partial(feed_back_two_kernel, len(after)),
        grid=(2,),
        in_specs=[VMEM, part, part, wide] + [VMEM] * 6 + [ANY] * len(after),
        out_specs=[column] + [VMEM] * 5,
        out_shape=[
            shape((ROWS, FF // 2), bf16),
            shape((ROWS, D), f32),
            shape((ROWS, D), bf16),
            shape((ROWS, D), bf16),
            shape((HEADS // 2, 2, ROWS), f32),
            shape((2, D), f32),
        ],
        scratch_shapes=[pltpu.VMEM((ROWS, D), f32)],
        compiler_params=PARAMS,
        cost_estimate=cost(15),
        name="feed_back_two",
    )(d_ffn, red_all, exp_all, slope, d_second, unit_one, inverse_one, norms, out_all, exact, *after)


def attend_back_kernel(
    n_after, counts, to_words, to_ents, keys, values, d_context, lse, row_inner, *refs
):
    d_to_words, d_to_ents, d_keys, d_values = refs[n_after:]
    masks = head_masks(counts)
    scale = HEAD ** (-0.5)
    one, two, three, four = [], [], [], []
    for h in range(2):
        cols = slice(h * HEAD, (h + 1) * HEAD)
        scores = scores_of(masks[h], keys[...], to_words[...], to_ents[...])
        probs = jnp.exp(scores - lse[h : h + 1, :])
        d_probs = dot(values[...] * masks[h][0], d_context[...], NT)
        d_scores = (probs * (d_probs - row_inner[h : h + 1, :])).astype(bf16)
        one.append(dot(keys[:WORDS, cols], d_scores[:WORDS], TN))
        two.append(dot(keys[WORDS:, cols], d_scores[WORDS:], TN))
        three.append(
            jnp.concatenate(
                [
                    dot(d_scores[:WORDS], to_words[:, cols], NN),
                    dot(d_scores[WORDS:], to_ents[:, cols], NN),
                ],
                0,
            )
        )
        four.append(dot(probs.astype(bf16), d_context[:, cols], NN))
    d_to_words[...] = (jnp.concatenate(one, 0).T * scale).astype(bf16)
    d_to_ents[...] = (jnp.concatenate(two, 0).T * scale).astype(bf16)
    d_keys[...] = jnp.concatenate(three, 1).astype(bf16)
    d_values[...] = jnp.concatenate(four, 1).astype(bf16)


def attend_back(first, counts, to_words, to_ents, keys, values, d_context, lse, row_inner, after=()):
    after = tokens(after)
    pair = pl.BlockSpec((ROWS, 128), lambda i: (0, i + first))
    column = pl.BlockSpec((ROWS, 128), lambda i: (0, i))
    stat = pl.BlockSpec((None, 2, ROWS), lambda i: (i + first, 0, 0))
    return pl.pallas_call(
        functools.partial(attend_back_kernel, len(after)),
        grid=(HEADS // 4,),
        in_specs=[SMEM] + [pair] * 5 + [stat] * 2 + [ANY] * len(after),
        out_specs=[column] * 4,
        out_shape=[shape((ROWS, D // 2), bf16)] * 4,
        compiler_params=PARAMS,
        cost_estimate=cost(10),
        name="attend_back",
    )(counts, to_words, to_ents, keys, values, d_context, lse, row_inner, *after)


def relative():
    for x in range(2):
        for y in range(2):
            for low in range(2):
                for high in range(2):
                    yield x, y, low, high


def emit(mine, got, outs, half, first, rest, rows, value):
    if not mine:
        outs[0][(half, first) + rest + (rows,)] = value.astype(bf16)
        return
    value = (value + got[(half, first) + rest + (rows,)].astype(f32)).astype(bf16)
    if first:
        outs[half][rest + (rows,)] = value
    else:
        outs[2][(half,) + rest + (rows,)] = value


def grad_call(kernel, name, mine, operands, got, dims, extra, after):
    after = tokens(after)
    zs, rows, lanes = dims
    if mine:
        outs = [shape((2,) + zs + (rows, lanes), bf16)] * 2
        outs += [shape((2, 2) + zs + (rows, lanes), bf16)]
        operands = list(operands) + [got]
    else:
        outs = [shape((2, 2, 2) + zs + (rows, lanes), bf16)]
    return pl.pallas_call(
        functools.partial(kernel, mine, len(after), len(outs)),
        in_specs=[VMEM] * len(operands) + [ANY] * len(after),
        out_specs=[VMEM] * len(outs),
        out_shape=outs,
        scratch_shapes=extra,
        compiler_params=PARAMS,
        cost_estimate=cost(7),
        name=name,
    )(*operands, *after)


def split_refs(mine, n_after, n_outs, refs):
    got, refs = (refs[0], refs[1:]) if mine else (None, refs)
    refs = refs[n_after:]
    return got, refs[:n_outs], refs[n_outs:]


def grad_red_kernel(mine, n_after, n_outs, d_ffn, activated, *refs):
    got, outs, (whole,) = split_refs(mine, n_after, n_outs, refs)
    wide, narrow = coords()
    core = 0 if mine else 1
    for x in range(2):
        n = narrow ^ (x * 2 + core)
        lanes = pl.ds(pl.multiple_of(n * D, D), D)
        whole[...] = dot(d_ffn[...], activated[:, lanes], TN)
        for y in range(2):
            for low in range(2):
                for high in range(2):
                    w = wide ^ (high * 4 + low * 2 + y)
                    for half in range(2):
                        rows = pl.ds(pl.multiple_of(w * 96 + half * 48, 16), 48)
                        first, second = (x, y) if half == 0 else (y, x)
                        emit(
                            mine, got, outs, half, first, (second, low, high), slice(0, 48), whole[rows, :]
                        )


def grad_red(mine, d_ffn, activated, got=None, after=()):
    return grad_call(
        grad_red_kernel,
        "grad_red",
        mine,
        (d_ffn, activated),
        got,
        ((2, 2), 48, D),
        [pltpu.VMEM((D, D), f32)],
        after,
    )


def grad_exp_kernel(mine, n_after, n_outs, middle, d_inner_one, d_inner_two, d_out, context, *refs):
    got, outs, (whole, turned) = split_refs(mine, n_after, n_outs, refs)
    wide, narrow = coords()
    for z in range(4):
        d_inner = d_inner_one if z < 2 else d_inner_two
        whole[z] = dot(middle[...], d_inner[:, (z % 2) * D : (z % 2 + 1) * D], TN)
    for x, y, low, high in relative():
        z = (wide // 2) ^ (high * 2 + low)
        lanes = pl.ds(pl.multiple_of(((wide % 2) ^ y) * 384, 128), 384)
        for half in range(2):
            rows = pl.ds(pl.multiple_of((narrow // 2 ^ x) * 192 + half * 96, 16), 96)
            first, second = (x, y) if half == 0 else (y, x)
            emit(
                mine, got, outs, half, first, (second, low, high), slice(0, 96), whole[z, rows, lanes]
            )
    turned[...] = dot(d_out[...], context[...], TN)
    for y in range(2):
        for low in range(2):
            for high in range(2):
                w = wide ^ (high * 4 + low * 2 + y)
                blocks = packed(turned, w * 96, narrow)
                for x in range(2):
                    for half in range(2):
                        first, second = (x, y) if half == 0 else (y, x)
                        value = blocks[x][half * 16 : half * 16 + 32]
                        emit(
                            mine, got, outs, half, first, (second, low, high), slice(96, 128), value
                        )


def packed(turned, start, narrow):
    upper = pl.ds(pl.multiple_of(start, 16), 48)
    lower = pl.ds(pl.multiple_of(start + 48, 16), 48)
    tail_upper = turned[upper, 256:]
    tail_lower = turned[lower, 256:]
    tails = (
        jnp.concatenate([tail_upper[:, :64], tail_lower[:, :64]], 1),
        jnp.concatenate([tail_upper[:, 64:], tail_lower[:, 64:]], 1),
    )
    x_own = narrow // 2
    out = []
    for x in range(2):
        lanes = pl.ds(pl.multiple_of((x_own ^ x) * 128, 128), 128)
        tail = jnp.where(x_own == x, tails[0], tails[1])
        out.append(jnp.concatenate([turned[upper, lanes], turned[lower, lanes], tail], 1))
    return out


def unpacked(block):
    upper = jnp.concatenate([block[..., :128], block[..., 256:320]], -1)
    lower = jnp.concatenate([block[..., 128:256], block[..., 320:]], -1)
    return jnp.concatenate([upper, lower], -2)


def grad_exp(mine, middle, d_inner_one, d_inner_two, d_out, context, got=None, after=()):
    return grad_call(
        grad_exp_kernel,
        "grad_exp",
        mine,
        (middle, d_inner_one, d_inner_two, d_out, context),
        got,
        ((2, 2), 128, 384),
        [pltpu.VMEM((4, 384, D), f32), pltpu.VMEM((D, 384), f32)],
        after,
    )


def grad_att_kernel(part, mine, n_after, n_outs, picked, d_to_words, d_to_ents, d_keys, d_values, *refs):
    got, outs, (turned,) = split_refs(mine, n_after, n_outs, refs)
    wide, narrow = coords()
    work = (
        (d_keys, slice(0, ROWS), 0, 0),
        (d_to_words, slice(0, WORDS), 0, 1),
        (d_to_words, slice(WORDS, ROWS), 0, 2),
        (d_values, slice(0, ROWS), 1, 0),
        (d_to_ents, slice(0, WORDS), 1, 1),
        (d_to_ents, slice(WORDS, ROWS), 1, 2),
    )
    for ref, rows, half, at in work:
        turned[...] = dot(ref[rows, :], picked[rows, :], TN)
        for y in range(2):
            for low in range(2):
                w = (wide % 4) ^ (low * 2 + y)
                blocks = packed(turned, w * 96, narrow)
                for x in range(2):
                    first, second = (x, y) if half == 0 else (y, x)
                    where = slice(at * 48, at * 48 + 48)
                    emit(mine, got, outs, half, first, (second, low), where, blocks[x])


def grad_att(part, mine, picked, grads, got=None, after=()):
    return grad_call(
        functools.partial(grad_att_kernel, part),
        "grad_att",
        mine,
        (picked,) + tuple(grads),
        got,
        ((2,), 144, 384),
        [pltpu.VMEM((D // 2, 384), f32)],
        after,
    )


def grad_hidden_kernel(n_after, d_first, *refs):
    grads, (kv, q), (word, ent) = refs[:8], refs[8:10], refs[10 + n_after :]
    d_to_words, d_to_ents, d_keys, d_values = [
        jnp.concatenate([grads[i][...], grads[4 + i][...]], 1) for i in range(4)
    ]
    shared = d_first[...] + dot(d_keys, kv[0], NN) + dot(d_values, kv[1], NN)
    word[...] = (
        shared[:WORDS] + dot(d_to_words[:WORDS], q[0], NN) + dot(d_to_ents[:WORDS], q[2], NN)
    )
    ent[...] = (
        shared[WORDS:] + dot(d_to_words[WORDS:], q[1], NN) + dot(d_to_ents[WORDS:], q[3], NN)
    )


def grad_hidden(d_first, grads, kv, q, after=()):
    after = tokens(after)
    return pl.pallas_call(
        functools.partial(grad_hidden_kernel, len(after)),
        in_specs=[VMEM] * 11 + [ANY] * len(after),
        out_specs=[VMEM] * 2,
        out_shape=[shape((WORDS, D), f32), shape((ENTS, D), f32)],
        compiler_params=PARAMS,
        cost_estimate=cost(9),
        name="grad_hidden",
    )(d_first, *grads, kv, q, *after)


def flip(axis, bit, value):
    size = lax.axis_size(axis)
    return lax.ppermute(value, axis, [(i, i ^ bit) for i in range(size)])


def over(name, value):
    axis, bit = {
        "core": ("narrow", 1),
        "x": ("narrow", 2),
        "y": ("wide", 1),
        "low": ("wide", 2),
        "high": ("wide", 4),
    }[name]
    return flip(axis, bit, value)


class Links:
    def __init__(self):
        self.past = {}

    def send(self, name, value):
        kind = "z" if name in ("low", "high") else name
        past = self.past.setdefault(kind, [])
        if len(past) > 1:
            value, unused = lax.optimization_barrier((value, past[-2]))
        got = over(name, value)
        past.append(got)
        return got


def later(values, token):
    return lax.optimization_barrier((tuple(values), token))[0]


def gather_high(links, first, second):
    both = jnp.concatenate([first, second], 0)
    return both, links.send("high", both)


def gather_low(links, cut, both):
    both = jnp.stack(both, 0)
    got = links.send("low", both)
    left = jnp.stack([both[:, :cut], got[:, :cut]], 0)
    right = jnp.stack([both[:, cut:], got[:, cut:]], 0)
    return left, right


def gather_near(links, left, right):
    got_left = links.send("x", left)
    got_right = links.send("y", right)
    left = jnp.stack([left, got_left], 0)
    right = jnp.stack([right, got_right], 0)
    return left, right


def gather_far(links, left, right):
    return gather_core(left, right, links.send("y", left), links.send("x", right))


def gather_core(left, right, left_far, right_far, token=None):
    left_core = over("core", left)
    right_core = over("core", right)
    if token is not None:
        left_far, right_far = later((left_far, right_far), token)
    return (
        left,
        left_far,
        left_core,
        over("core", left_far),
        right,
        right_far,
        right_core,
        over("core", right_far),
    )


def plus(kept, got):
    return (kept.astype(f32) + got.astype(f32)).astype(bf16)


class Sum:
    def __init__(self, send_left, send_right, keep):
        self.keep = keep
        self.got = over("x", send_left), over("y", send_right)

    def wait(self, token):
        self.got = later(self.got, token) if isinstance(self.got, tuple) else later((self.got,), token)[0]
        return self

    def second(self):
        left, right = self.got
        keep = self.keep
        self.got = (
            over("y", plus(keep[0, 1], left[1])),
            over("x", plus(keep[1, 1], right[1])),
        )
        self.keep = plus(keep[0, 0], left[0]), plus(keep[1, 0], right[0])
        return self.got

    def third(self):
        left, right = self.got
        keep = jnp.stack([plus(self.keep[0], left), plus(self.keep[1], right)], 1)
        self.keep = keep[0]
        self.got = over("low", keep[1])
        return self.got

    def low(self):
        return plus(self.keep, self.got)

    def fourth(self):
        keep = self.low()
        self.keep = keep[:, 0]
        self.got = over("high", keep[:, 1])
        return self.got

    def result(self):
        return self.keep.astype(f32) + self.got.astype(f32)


def sum_all(value):
    size = lax.axis_size("wide") * lax.axis_size("narrow")
    spread = jnp.broadcast_to(value[None], (size,) + value.shape)
    got = lax.all_to_all(spread, ("wide", "narrow"), 0, 0, tiled=False)
    return jnp.sum(got, axis=0)


def adapt(weight, grad, first, second, decay):
    first = 0.5 * first + 0.5 * grad
    second = 0.5 * second + 0.5 * grad * grad
    fix_first = 1.0 - 0.5**STEP
    fix_second = 1.0 - 0.5**STEP
    update = first / fix_first / (jnp.sqrt(second / fix_second) + adam_eps) + decay * weight
    return (first, second, update)


def shards(
    fast,
    word_states,
    entity_states,
    seq_counts,
    attention_weight,
    expand_weight,
    reduce_weight,
    norm_params,
    moment_attention,
    moment_expand,
    moment_reduce,
    moment_norms,
    square_attention,
    square_expand,
    square_reduce,
    square_norms,
    word_cotangent,
    entity_cotangent,
):
    word, ent, counts = word_states[0], entity_states[0], seq_counts[0]
    core = lax.axis_index("narrow") % 2
    high = lax.axis_index("wide") // 4
    if fast:
        keep, send, exp_low, red_low, weight_local = prep(
            attention_weight, expand_weight, reduce_weight.T
        )
        got = over("core", send)
        rows = jnp.where(
            core == 0, jnp.concatenate([keep, got], 2), jnp.concatenate([got, keep], 2)
        )
        links = Links()
        kv = gather_high(links, rows[4], rows[5])
        query = gather_high(
            links,
            jnp.concatenate([rows[0], rows[2]], 0),
            jnp.concatenate([rows[1], rows[3]], 0),
        )
        kv = gather_low(links, 48, kv)
        query = gather_low(links, 96, query)
        kv = gather_near(links, *kv)
        kv_pieces = gather_far(links, *kv)
        query = gather_near(links, *query)
        query_pieces = gather_far(links, *query)
        one = gather_high(links, jnp.concatenate([exp_low[:96], rows[6]], 0), exp_low[96:])
        kv_pieces = [v.reshape(v.shape[:3] + (1, 48, 384)) for v in kv_pieces]
        query_pieces = [v.reshape(v.shape[:3] + (2, 48, 384)) for v in query_pieces]
    else:
        weight_local = jnp.concatenate(
            [
                jnp.sum(attention_weight * attention_weight, axis=(1, 2)),
                jnp.sum(expand_weight * expand_weight)[None],
                jnp.sum(reduce_weight * reduce_weight)[None],
            ]
        )
        turned = jnp.swapaxes(attention_weight.astype(bf16), 1, 2)
        turned = lax.all_gather(turned, "wide", axis=1, tiled=True)
        turned = lax.all_gather(turned, "narrow", axis=2, tiled=True)
        exp_all = lax.all_gather(expand_weight.astype(bf16), "wide", axis=1, tiled=True)
        exp_all = lax.all_gather(exp_all, "narrow", axis=0, tiled=True)
        red_all = lax.all_gather(reduce_weight.astype(bf16).T, "wide", axis=0, tiled=True)
        red_all = lax.all_gather(red_all, "narrow", axis=1, tiled=True)
        kv_pieces = query_pieces = [turned]
        one_pieces = [turned, exp_all]
        two_pieces = [red_all]
        one = two = (None, None)

    low, keys, values, low_mine, low_other, kv_all = project_kv(fast, word, ent, kv_pieces)
    if fast:
        one = gather_low(links, 144, later(one, keys))
        two = gather_high(links, *later((red_low[:48], red_low[48:]), keys))
        one = gather_near(links, *one)
        one_pieces = gather_far(links, *one)
    to_words, to_ents, q_all = project_q(fast, low, query_pieces)
    context, exact, lse = attend(counts, to_words, to_ents, keys, values, after=one)
    if fast:
        two = gather_low(links, 48, later(two, to_words))
        two = gather_near(links, *later(two, context))
        two_far = links.send("y", two[0]), links.send("x", two[1])
    (
        middle,
        middle_low,
        activated,
        slope,
        unit_one,
        inverse_one,
        middle_mine,
        middle_other,
        context_mine,
        context_other,
        out_all,
        exp_all,
    ) = feed_in(fast, word, ent, context, norm_params, one_pieces, after=two)
    if fast:
        two_pieces = gather_core(*two, *two_far, token=activated)
    word_out, ent_out, d_second, d_ffn, grads_two, red_all = feed_out(
        fast, activated, middle, norm_params, word_cotangent[0], entity_cotangent[0], two_pieces
    )
    got = red = exp = att_one = att_two = None
    if fast:
        got = over("core", grad_red(False, d_ffn, activated)[0])
    d_inner_one, partial = feed_back_one(0, d_ffn, red_all, exp_all, slope, d_second)
    if fast:
        red = Sum(*grad_red(True, d_ffn, activated, got, after=(partial,)))
    d_inner_two, d_first, d_out, d_context, row_inner, grads_one = feed_back_two(
        2,
        d_ffn,
        red_all,
        exp_all,
        slope,
        partial,
        unit_one,
        inverse_one,
        norm_params,
        out_all,
        exact,
        after=(red.keep,) if fast else (),
    )
    early = jnp.concatenate([grads_one, grads_two], 0)
    early = jnp.concatenate([early, jnp.pad(weight_local, (0, D - 9))[None]], 0)
    early = jnp.pad(early, ((0, 11), (0, 0)))
    early = lax.all_gather(early, ("wide", "narrow"))
    exp_args = (d_inner_one, d_inner_two, d_out)
    att_args = (counts, to_words, to_ents, keys, values, d_context, lse, row_inner)
    if fast:
        sent = grad_exp(False, middle_other, *exp_args, context_other)[0]
        got = over("core", sent)
        red.wait(sent).second()
    grads = attend_back(0, *att_args, after=(red.keep + (sent,)) if fast else ())
    if fast:
        exp = Sum(*grad_exp(True, middle_mine, *exp_args, context_mine, got, after=(grads[0],)))
        red.wait(exp.keep).third()
        sent = grad_att(0, False, low_other, grads, after=(exp.keep, red.keep))[0]
        got = over("core", sent)
    more = attend_back(3, *att_args, after=(sent, red.keep) if fast else ())
    if fast:
        exp.wait(more[0]).second()
        red.wait(more[0]).fourth()
        att_one = Sum(*grad_att(0, True, low_mine, grads, got, after=exp.keep + (more[0], red.keep)))
        sent = grad_att(1, False, low_other, more, after=(att_one.keep,))[0]
        got = over("core", sent)
        exp.wait(sent).third()
        att_two = Sum(*grad_att(1, True, low_mine, more, got, after=(sent,)))
    word_grad, ent_grad = grad_hidden(
        d_first, grads + more, kv_all, q_all, after=(att_two.keep,) if fast else ()
    )
    early = jnp.sum(later((early,), word_grad)[0], axis=0)
    norm_grads = early[:4]
    weight_total = early[4, :9]

    if fast:
        att_one.wait(att_two.keep).second()
        exp.wait(word_grad).fourth()
        att_two.wait(word_grad).second()
        att_one.wait(word_grad).third()
        att_two.third()
        red_sum = red.result()
        exp_sum = exp.result()
        first, second = att_one.low(), att_two.low()
        got = over("high", jnp.where(high == 0, second, first))
        att_sum = jnp.where(high == 0, first, second).astype(f32) + got.astype(f32)
        out_rows = jnp.concatenate([exp_sum[0, 96:], exp_sum[1, 112:]], 0)
        turned = jnp.stack(
            [
                att_sum[0, 48:96],
                att_sum[1, 48:96],
                att_sum[0, 96:],
                att_sum[1, 96:],
                att_sum[0, :48],
                att_sum[1, :48],
                out_rows,
            ]
        )
        att_grad = jnp.swapaxes(unpacked(turned), 1, 2)
        exp_grad = jnp.concatenate([exp_sum[0, :96], exp_sum[1, :96]], 0)
        red_grad = jnp.concatenate([red_sum[0], red_sum[1]], 0)
    else:
        d_to_words, d_to_ents, d_keys, d_values = [
            jnp.concatenate([a, b], 1) for a, b in zip(grads, more)
        ]
        d_inner = jnp.concatenate([d_inner_one, d_inner_two], 1)
        words, ents = low[:WORDS], low[WORDS:]
        turned = jnp.stack(
            [
                dot(d_to_words[:WORDS], words, TN),
                dot(d_to_ents[:WORDS], words, TN),
                dot(d_to_words[WORDS:], ents, TN),
                dot(d_to_ents[WORDS:], ents, TN),
                dot(d_keys, low, TN),
                dot(d_values, low, TN),
                dot(d_out, context, TN),
            ]
        ).astype(bf16)
        turned = lax.psum_scatter(turned, "wide", scatter_dimension=1, tiled=True)
        turned = lax.psum_scatter(turned, "narrow", scatter_dimension=2, tiled=True)
        att_grad = jnp.swapaxes(turned.astype(f32), 1, 2)
        grad = dot(middle_low, d_inner, TN).astype(bf16)
        grad = lax.psum_scatter(grad, "wide", scatter_dimension=1, tiled=True)
        grad = lax.psum_scatter(grad, "narrow", scatter_dimension=0, tiled=True)
        exp_grad = grad.astype(f32)
        grad = dot(d_ffn, activated, TN).astype(bf16)
        grad = lax.psum_scatter(grad, "wide", scatter_dimension=0, tiled=True)
        grad = lax.psum_scatter(grad, "narrow", scatter_dimension=1, tiled=True)
        red_grad = grad.astype(f32)

    att_first, att_second, att_update = adapt(
        attention_weight, att_grad, moment_attention, square_attention, matrix_decay
    )
    exp_first, exp_second, exp_update = adapt(
        expand_weight, exp_grad, moment_expand, square_expand, matrix_decay
    )
    red_first, red_second, red_update = adapt(
        reduce_weight.T, red_grad, moment_reduce.T, square_reduce.T, matrix_decay
    )
    update_local = jnp.concatenate(
        [
            jnp.sum(att_update * att_update, axis=(1, 2)),
            jnp.sum(exp_update * exp_update)[None],
            jnp.sum(red_update * red_update)[None],
        ]
    )
    update_total = sum_all(update_local)
    nrm_first, nrm_second, nrm_update = adapt(
        norm_params, norm_grads, moment_norms, square_norms, 0.0
    )
    weight_norm = jnp.sqrt(
        jnp.concatenate([weight_total, jnp.sum(norm_params * norm_params, axis=1)])
    )
    update_norm = jnp.sqrt(
        jnp.concatenate([update_total, jnp.sum(nrm_update * nrm_update, axis=1)])
    )
    trust = weight_norm / update_norm
    new_attention = attention_weight - learn_rate * trust[0:7, None, None] * att_update
    new_expand = expand_weight - learn_rate * trust[7] * exp_update
    new_reduce = reduce_weight - learn_rate * trust[8] * red_update.T
    new_norms = norm_params - learn_rate * trust[9:13, None] * nrm_update
    trust_stats = jnp.stack([jnp.log(weight_norm), jnp.log(update_norm), jnp.log(trust)], 1)
    return (
        word_out[None],
        ent_out[None],
        word_grad[None],
        ent_grad[None],
        new_attention,
        new_expand,
        new_reduce,
        new_norms,
        att_first,
        exp_first,
        red_first.T,
        nrm_first,
        att_second,
        exp_second,
        red_second.T,
        nrm_second,
        trust_stats,
    )


def solution(mesh):
    fast = mesh.shape["wide"] == 8 and mesh.shape["narrow"] == 4
    rows = P(("wide", "narrow"), None, None)
    matrix = P("narrow", "wide")
    stack = P(None, "narrow", "wide")
    weights = (stack, matrix, matrix, P())
    return jax.shard_map(
        functools.partial(shards, fast),
        mesh=mesh,
        in_specs=(rows, rows, P(("wide", "narrow"), None)) + weights * 3 + (rows, rows),
        out_specs=(rows,) * 4 + weights * 3 + (P(),),
        check_vma=False,
    )
```

```python
import functools

import jax
import jax.numpy as jnp
from jax import lax
from jax.experimental import pallas as pl
from jax.experimental.pallas import tpu as pltpu
from jax.sharding import PartitionSpec as P

D = 768
FF = 3072
HEADS = 12
HEAD = 64
WORDS = 512
ENTS = 128
ROWS = WORDS + ENTS
STEP = 7

eps_norm = 1e-05
adam_eps = 1e-06
matrix_decay = 0.01
learn_rate = 0.5
masked_score = -1e30

f32 = jnp.float32
bf16 = jnp.bfloat16
NN = (((1,), (0,)), ((), ()))
NT = (((1,), (1,)), ((), ()))
TN = (((0,), (0,)), ((), ()))
VMEM = pl.BlockSpec(memory_space=pltpu.VMEM)
SMEM = pl.BlockSpec(memory_space=pltpu.SMEM)
ANY = pl.BlockSpec(memory_space=pl.ANY)
COST_RATE = 4e9
PARAMS = pltpu.CompilerParams(vmem_limit_bytes=60 * 2**20)


def dot(left, right, dims):
    return lax.dot_general(left, right, dims, preferred_element_type=f32)


def shape(dims, dtype):
    return jax.ShapeDtypeStruct(dims, dtype)


def tokens(values):
    return [v for v in values if v is not None]


def cost(us, rate=COST_RATE):
    return pl.CostEstimate(flops=int(us * rate), bytes_accessed=0, transcendentals=0)


def away_blocks():
    for core in range(2):
        for outer in range(2):
            for lead in range(2):
                for low in range(2):
                    for high in range(2):
                        yield core, outer, lead, low, high


def places(wide, narrow, second, block):
    core, outer, lead, low, high = block
    x_away, y_away = (outer, lead) if second else (lead, outer)
    w = wide ^ (high * 4 + low * 2 + y_away)
    n = narrow ^ (x_away * 2 + core)
    return w, n


def piece_of(bufs, block):
    core, outer, lead, low, high = block
    return bufs[core].at[outer, lead, low, high]


def coords():
    return lax.axis_index("wide"), lax.axis_index("narrow")


def start_attention(bufs, second, target, slots, sem):
    wide, narrow = coords()
    for block in away_blocks():
        w, n = places(wide, narrow, second, block)
        row = pl.multiple_of(w * 96 + (n % 2) * 48, 16)
        lane = pl.multiple_of((n // 2) * 384, 128)
        src = piece_of(bufs, block)
        pltpu.make_async_copy(src, target.at[slots, pl.ds(row, 48), pl.ds(lane, 384)], sem).start()


def drain(ref, sem):
    pltpu.make_async_copy(ref, ref, sem).wait()


def prep_kernel(att, exp, red, keep, send, exp_low, red_low, sums):
    narrow = lax.axis_index("narrow")
    core = narrow % 2
    total = []
    for i in range(7):
        value = att[i]
        total.append(jnp.sum(value * value))
        turned = value.T.astype(bf16)
        halves = turned.reshape(2, 48, 192)

        @pl.when(core == 0)
        def _():
            keep[i] = halves[0]
            send[i] = halves[1]

        @pl.when(core == 1)
        def _():
            keep[i] = halves[1]
            send[i] = halves[0]

    value = exp[...]
    total.append(jnp.sum(value * value))
    exp_low[...] = value.astype(bf16)
    value = red[...]
    total.append(jnp.sum(value * value))
    red_low[...] = value.astype(bf16)
    for i in range(9):
        sums[i] = total[i]


def prep(att, exp, red):
    return pl.pallas_call(
        prep_kernel,
        in_specs=[VMEM] * 3,
        out_specs=[VMEM] * 4 + [SMEM],
        out_shape=[
            shape((7, 48, 192), bf16),
            shape((7, 48, 192), bf16),
            shape((192, 384), bf16),
            shape((96, D), bf16),
            shape((9,), f32),
        ],
        compiler_params=PARAMS,
        name="prep",
    )(att, exp, red)


def pick_rows(source, mine, other):
    core = lax.axis_index("narrow") % 2
    for c in range(2):

        @pl.when(core == c)
        def _():
            for target, at in ((mine, c * 192), (other, 192 - c * 192)):
                target[:, :192] = source[:, at : at + 192]
                target[:, 192:] = source[:, at + 384 : at + 576]


def pick_tiles(source, mine, other):
    core = lax.axis_index("narrow") % 2
    for c in range(2):

        @pl.when(core == c)
        def _():
            for target, at in ((mine, c * 192), (other, 192 - c * 192)):
                target[:, :128] = source[:, at : at + 128]
                target[:, 128:256] = source[:, at + 384 : at + 512]
                target[:, 256:320] = source[:, at + 128 : at + 192]
                target[:, 320:] = source[:, at + 512 : at + 576]


def project_kv_kernel(fast, n_after, word, ent, *refs):
    if fast:
        first, second, refs = refs[:2], refs[2:4], refs[4:]
    else:
        whole, refs = refs[0], refs[1:]
    low, keys, values, mine, other, saved, target, sem, sem_save = refs[n_after:]
    if fast:
        start_attention(first, False, target, pl.ds(0, 1), sem)
        start_attention(second, True, target, pl.ds(1, 1), sem)
    else:
        pltpu.make_async_copy(whole.at[pl.ds(4, 2)], target, sem).start()
    low[:WORDS] = word[...].astype(bf16)
    low[WORDS:] = ent[...].astype(bf16)
    pick_tiles(low, mine, other)
    drain(target, sem)
    save = pltpu.make_async_copy(target, saved, sem_save)
    save.start()
    keys[...] = dot(low[...], target[0], NT).astype(bf16)
    values[...] = dot(low[...], target[1], NT).astype(bf16)
    save.wait()


def project_kv(fast, word, ent, pieces, after=()):
    after = tokens(after)
    return pl.pallas_call(
        functools.partial(project_kv_kernel, fast, len(after)),
        in_specs=[VMEM, VMEM] + [ANY] * (len(pieces) + len(after)),
        out_specs=[VMEM] * 5 + [ANY],
        out_shape=[shape((ROWS, D), bf16)] * 3
        + [shape((ROWS, D // 2), bf16)] * 2
        + [shape((2, D, D), bf16)],
        scratch_shapes=[
            pltpu.VMEM((2, D, D), bf16),
            pltpu.SemaphoreType.DMA,
            pltpu.SemaphoreType.DMA,
        ],
        compiler_params=PARAMS,
        cost_estimate=cost(6, 4e8),
        name="project_kv",
    )(word, ent, *pieces, *after)


def project_q_kernel(fast, n_after, low, *refs):
    if fast:
        first, second, refs = refs[:2], refs[2:4], refs[4:]
    else:
        whole, refs = refs[0], refs[1:]
    to_words, to_ents, saved, target, sem, sem_save = refs[n_after:]
    if fast:
        start_attention(first, False, target, pl.ds(0, 2), sem)
        start_attention(second, True, target, pl.ds(2, 2), sem)
    else:
        for slot, k in enumerate((0, 2, 1, 3)):
            pltpu.make_async_copy(whole.at[k], target.at[slot], sem).start()
    drain(target, sem)
    save = pltpu.make_async_copy(target, saved, sem_save)
    save.start()
    scale = HEAD ** (-0.5)
    word = low[:WORDS]
    ent = low[WORDS:]
    to_words[:WORDS] = (dot(word, target[0], NT) * scale).astype(bf16)
    to_words[WORDS:] = (dot(ent, target[1], NT) * scale).astype(bf16)
    to_ents[:WORDS] = (dot(word, target[2], NT) * scale).astype(bf16)
    to_ents[WORDS:] = (dot(ent, target[3], NT) * scale).astype(bf16)
    save.wait()


def project_q(fast, low, pieces, after=()):
    after = tokens(after)
    return pl.pallas_call(
        functools.partial(project_q_kernel, fast, len(after)),
        in_specs=[VMEM] + [ANY] * (len(pieces) + len(after)),
        out_specs=[VMEM] * 2 + [ANY],
        out_shape=[shape((ROWS, D), bf16)] * 2 + [shape((4, D, D), bf16)],
        scratch_shapes=[
            pltpu.VMEM((4, D, D), bf16),
            pltpu.SemaphoreType.DMA,
            pltpu.SemaphoreType.DMA,
        ],
        compiler_params=PARAMS,
        cost_estimate=cost(7, 4e8),
        name="project_q",
    )(low, *pieces, *after)


def head_masks(counts):
    lane = lax.broadcasted_iota(jnp.int32, (ROWS, 128), 1)
    row = lax.broadcasted_iota(jnp.int32, (ROWS, 128), 0)
    edge = jnp.where(row < WORDS, counts[0], counts[1] + WORDS)
    bias = jnp.where(row < edge, 0.0, masked_score)
    out = []
    for h in range(2):
        own = jnp.where((lane < HEAD) if h == 0 else (lane >= HEAD), 1.0, 0.0).astype(bf16)
        mark = jnp.where(lane == (HEAD if h == 0 else 0), 1.0, 0.0)
        rest = (1.0 - mark).astype(bf16)
        tag = (bias * mark).astype(bf16)
        out.append((own, mark.astype(bf16), rest, tag))
    return out


def scores_of(masks, keys, to_words, to_ents):
    own, mark, rest, tag = masks
    tagged = keys * own + tag
    upper = dot(tagged[:WORDS], to_words * rest + mark, NT)
    lower = dot(tagged[WORDS:], to_ents * rest + mark, NT)
    return jnp.concatenate([upper, lower], 0)


def attend_kernel(n_after, counts, to_words, to_ents, keys, values, *refs):
    context, exact, lse = refs[n_after:]
    masks = head_masks(counts)
    outs = []
    for h in range(2):
        scores = scores_of(masks[h], keys[...], to_words[...], to_ents[...])
        top = jnp.max(scores, axis=0, keepdims=True)
        expd = jnp.exp(scores - top)
        total = jnp.sum(expd, axis=0, keepdims=True)
        lse[h : h + 1, :] = top + jnp.log(total)
        mixed = dot(values[:, h * HEAD : (h + 1) * HEAD], expd.astype(bf16), TN)
        outs.append(mixed * (1.0 / total))
    joined = jnp.concatenate(outs, 0).T
    exact[...] = joined
    context[...] = joined.astype(bf16)


def attend(counts, to_words, to_ents, keys, values, after=()):
    after = tokens(after)
    pair = pl.BlockSpec((ROWS, 128), lambda i: (0, i))
    stat = pl.BlockSpec((None, 2, ROWS), lambda i: (i, 0, 0))
    return pl.pallas_call(
        functools.partial(attend_kernel, len(after)),
        grid=(HEADS // 2,),
        in_specs=[SMEM, pair, pair, pair, pair] + [ANY] * len(after),
        out_specs=[pair, pair, stat],
        out_shape=[
            shape((ROWS, D), bf16),
            shape((ROWS, D), f32),
            shape((HEADS // 2, 2, ROWS), f32),
        ],
        compiler_params=PARAMS,
        cost_estimate=cost(12, 4e8),
        name="attend",
    )(counts, to_words, to_ents, keys, values, *after)


def normed(value):
    center = value - jnp.mean(value, axis=-1, keepdims=True)
    spread = jnp.mean(center * center, axis=-1, keepdims=True)
    inverse = lax.rsqrt(spread + eps_norm)
    return center * inverse, inverse


def normed_back(unit, inverse, cotangent):
    mean = jnp.mean(cotangent, axis=-1, keepdims=True)
    inner = jnp.mean(cotangent * unit, axis=-1, keepdims=True)
    return inverse * (cotangent - mean - unit * inner)


def column_sum(value):
    return jnp.sum(value, axis=0, keepdims=True)


def feed_in_kernel(fast, n_after, word, ent, context, norms, *refs):
    if fast:
        bufs, refs = (refs[0:2], refs[2:4]), refs[4:]
    else:
        bufs, refs = refs[0:2], refs[2:]
    (
        middle,
        middle_low,
        activated,
        slope,
        unit_one,
        inverse_one,
        middle_mine,
        middle_other,
        context_mine,
        context_other,
        out_saved,
        exp_saved,
        out_all,
        exp_all,
        sem_out,
        sem_exp,
        sem_save,
    ) = refs[n_after:]
    step = pl.program_id(0)
    save_out = pltpu.make_async_copy(out_all, out_saved, sem_save.at[0])
    save_exp = pltpu.make_async_copy(exp_all, exp_saved, sem_save.at[1])

    @pl.when(step == 0)
    def _():
        if fast:
            start_feed_in(bufs, out_all, exp_all, sem_out, sem_exp)
        else:
            pltpu.make_async_copy(bufs[0].at[6], out_all, sem_out).start()
            for j in range(4):
                cols = pl.ds(j * D, D)
                pltpu.make_async_copy(bufs[1].at[:, cols], exp_all.at[j], sem_exp).start()
        drain(out_all, sem_out)
        save_out.start()
        hidden = jnp.concatenate([word[...], ent[...]], 0)
        unit, inverse = normed(hidden + dot(context[...], out_all[...], NT))
        value = unit * norms[0:1, :] + norms[1:2, :]
        unit_one[...] = unit
        inverse_one[...] = inverse
        middle_low[...] = value.astype(bf16)
        middle[...] = value
        pick_rows(middle_low, middle_mine, middle_other)
        pick_tiles(context, context_mine, context_other)
        drain(exp_all, sem_exp)
        save_exp.start()

    inner = dot(middle_low[...], exp_all[step], NN)
    share = 0.5 + 0.5 * lax.erf(inner * 0.7071067811865476)
    bell = jnp.exp(-0.5 * inner * inner) * 0.3989422804014327
    slope[...] = (share + inner * bell).astype(bf16)
    activated[...] = (inner * share).astype(bf16)

    @pl.when(step == 3)
    def _():
        save_out.wait()
        save_exp.wait()


def start_feed_in(bufs, out_all, exp_all, sem_out, sem_exp):
    wide, narrow = coords()
    for block in away_blocks():
        w, n = places(wide, narrow, False, block)
        row = pl.multiple_of(w * 96 + (n % 2) * 48, 16)
        lane = pl.multiple_of((n // 2) * 384, 128)
        src = piece_of(bufs[0], block).at[pl.ds(96, 48)]
        pltpu.make_async_copy(src, out_all.at[pl.ds(row, 48), pl.ds(lane, 384)], sem_out).start()
    for half in range(2):
        for block in away_blocks():
            w, n = places(wide, narrow, half == 1, block)
            src = piece_of(bufs[half], block)
            if half == 0:
                src = src.at[pl.ds(0, 96)]
            row = pl.multiple_of(n * 192 + half * 96, 16)
            lane = pl.multiple_of((w % 2) * 384, 128)
            dst = exp_all.at[w // 2, pl.ds(row, 96), pl.ds(lane, 384)]
            pltpu.make_async_copy(src, dst, sem_exp).start()


def feed_in(fast, word, ent, context, norms, pieces, after=()):
    after = tokens(after)
    column = pl.BlockSpec((ROWS, D), lambda i: (0, i))
    return pl.pallas_call(
        functools.partial(feed_in_kernel, fast, len(after)),
        grid=(4,),
        in_specs=[VMEM] * 4 + [ANY] * (len(pieces) + len(after)),
        out_specs=[VMEM] * 2 + [column, column] + [VMEM] * 6 + [ANY] * 2,
        out_shape=[
            shape((ROWS, D), f32),
            shape((ROWS, D), bf16),
            shape((ROWS, FF), bf16),
            shape((ROWS, FF), bf16),
            shape((ROWS, D), f32),
            shape((ROWS, 1), f32),
            shape((ROWS, D // 2), bf16),
            shape((ROWS, D // 2), bf16),
            shape((ROWS, D // 2), bf16),
            shape((ROWS, D // 2), bf16),
            shape((D, D), bf16),
            shape((4, D, D), bf16),
        ],
        scratch_shapes=[
            pltpu.VMEM((D, D), bf16),
            pltpu.VMEM((4, D, D), bf16),
            pltpu.SemaphoreType.DMA,
            pltpu.SemaphoreType.DMA,
            pltpu.SemaphoreType.DMA((2,)),
        ],
        compiler_params=PARAMS,
        cost_estimate=cost(15),
        name="feed_in",
    )(word, ent, context, norms, *pieces, *after)


def feed_out_kernel(fast, n_after, activated, middle, norms, word_cot, ent_cot, *refs):
    if fast:
        bufs, refs = (refs[0:2], refs[2:4], refs[4:6], refs[6:8]), refs[8:]
    else:
        bufs, refs = refs[0:1], refs[1:]
    (
        word_out,
        ent_out,
        d_second,
        d_ffn,
        grads_two,
        red_saved,
        total,
        red_all,
        sem_red,
        sem_save,
    ) = refs[n_after:]
    step = pl.program_id(0)
    save = pltpu.make_async_copy(red_all, red_saved, sem_save)

    @pl.when(step == 0)
    def _():
        if fast:
            start_feed_out(bufs, red_all, sem_red)
        else:
            for j in range(4):
                cols = pl.ds(j * D, D)
                pltpu.make_async_copy(bufs[0].at[:, cols], red_all.at[j], sem_red).start()
        total[...] = middle[...]
        drain(red_all, sem_red)
        save.start()

    total[...] += dot(activated[...], red_all[step], NT)

    @pl.when(step == 3)
    def _():
        unit, inverse = normed(total[...])
        result = unit * norms[2:3, :] + norms[3:4, :]
        word_out[...] = result[:WORDS]
        ent_out[...] = result[WORDS:]
        cot = jnp.concatenate([word_cot[...], ent_cot[...]], 0)
        grads_two[0:1, :] = column_sum(cot * unit)
        grads_two[1:2, :] = column_sum(cot)
        back = normed_back(unit, inverse, cot * norms[2:3, :])
        d_second[...] = back
        d_ffn[...] = back.astype(bf16)
        save.wait()


def start_feed_out(bufs, red_all, sem_red):
    wide, narrow = coords()
    for half in range(2):
        for block in away_blocks():
            w, n = places(wide, narrow, half == 1, block)
            core, outer, lead, low, high = block
            src = bufs[half + 2 * outer][core].at[lead, low, high]
            row = pl.multiple_of(w * 96 + half * 48, 16)
            pltpu.make_async_copy(src, red_all.at[n, pl.ds(row, 48)], sem_red).start()


def feed_out(fast, activated, middle, norms, word_cot, ent_cot, pieces, after=()):
    after = tokens(after)
    column = pl.BlockSpec((ROWS, D), lambda i: (0, i))
    return pl.pallas_call(
        functools.partial(feed_out_kernel, fast, len(after)),
        grid=(4,),
        in_specs=[column] + [VMEM] * 4 + [ANY] * (len(pieces) + len(after)),
        out_specs=[VMEM] * 5 + [ANY],
        out_shape=[
            shape((WORDS, D), f32),
            shape((ENTS, D), f32),
            shape((ROWS, D), f32),
            shape((ROWS, D), bf16),
            shape((2, D), f32),
            shape((4, D, D), bf16),
        ],
        scratch_shapes=[
            pltpu.VMEM((ROWS, D), f32),
            pltpu.VMEM((4, D, D), bf16),
            pltpu.SemaphoreType.DMA,
            pltpu.SemaphoreType.DMA,
        ],
        compiler_params=PARAMS,
        cost_estimate=cost(13),
        name="feed_out",
    )(activated, middle, norms, word_cot, ent_cot, *pieces, *after)


def feed_back_one_kernel(n_after, d_ffn, red_all, exp_all, slope, d_second, *refs):
    d_inner, total = refs[n_after:]
    step = pl.program_id(0)
    back = (dot(d_ffn[...], red_all[...], NN) * slope[...].astype(f32)).astype(bf16)
    d_inner[...] = back

    @pl.when(step == 0)
    def _():
        total[...] = d_second[...]

    total[...] += dot(back, exp_all[...], NT)


def feed_back_one(first, d_ffn, red_all, exp_all, slope, d_second, after=()):
    after = tokens(after)
    wide = pl.BlockSpec((ROWS, D), lambda i: (0, i + first))
    column = pl.BlockSpec((ROWS, D), lambda i: (0, i))
    part = pl.BlockSpec((None, D, D), lambda i: (i + first, 0, 0))
    return pl.pallas_call(
        functools.partial(feed_back_one_kernel, len(after)),
        grid=(2,),
        in_specs=[VMEM, part, part, wide, VMEM] + [ANY] * len(after),
        out_specs=[column, VMEM],
        out_shape=[shape((ROWS, FF // 2), bf16), shape((ROWS, D), f32)],
        compiler_params=PARAMS,
        cost_estimate=cost(10),
        name="feed_back_one",
    )(d_ffn, red_all, exp_all, slope, d_second, *after)


def feed_back_two_kernel(
    n_after, d_ffn, red_all, exp_all, slope, d_second, unit_one, inverse_one, norms, out_all, exact, *refs
):
    d_inner, d_first, d_out, d_context, row_inner, grads_one, total = refs[n_after:]
    step = pl.program_id(0)
    back = (dot(d_ffn[...], red_all[...], NN) * slope[...].astype(f32)).astype(bf16)
    d_inner[...] = back

    @pl.when(step == 0)
    def _():
        total[...] = d_second[...]

    total[...] += dot(back, exp_all[...], NT)

    @pl.when(step == 1)
    def _():
        d_middle = total[...]
        unit = unit_one[...]
        grads_one[0:1, :] = column_sum(d_middle * unit)
        grads_one[1:2, :] = column_sum(d_middle)
        first = normed_back(unit, inverse_one[...], d_middle * norms[0:1, :])
        d_first[...] = first
        d_out[...] = first.astype(bf16)
        context = dot(first.astype(bf16), out_all[...], NN).astype(bf16)
        d_context[...] = context
        product = context.astype(f32) * exact[...]
        head = lax.broadcasted_iota(jnp.int32, (16, D), 1) // HEAD
        pick = jnp.where(head == lax.broadcasted_iota(jnp.int32, (16, D), 0), 1.0, 0.0).astype(bf16)
        high = product.astype(bf16)
        low = (product - high.astype(f32)).astype(bf16)
        sums = dot(pick, high, NT) + dot(pick, low, NT)
        for i in range(HEADS // 2):
            row_inner[i] = sums[2 * i : 2 * i + 2]


def feed_back_two(
    first, d_ffn, red_all, exp_all, slope, d_second, unit_one, inverse_one, norms, out_all, exact, after=()
):
    after = tokens(after)
    wide = pl.BlockSpec((ROWS, D), lambda i: (0, i + first))
    column = pl.BlockSpec((ROWS, D), lambda i: (0, i))
    part = pl.BlockSpec((None, D, D), lambda i: (i + first, 0, 0))
    return pl.pallas_call(
        functools.partial(feed_back_two_kernel, len(after)),
        grid=(2,),
        in_specs=[VMEM, part, part, wide] + [VMEM] * 6 + [ANY] * len(after),
        out_specs=[column] + [VMEM] * 5,
        out_shape=[
            shape((ROWS, FF // 2), bf16),
            shape((ROWS, D), f32),
            shape((ROWS, D), bf16),
            shape((ROWS, D), bf16),
            shape((HEADS // 2, 2, ROWS), f32),
            shape((2, D), f32),
        ],
        scratch_shapes=[pltpu.VMEM((ROWS, D), f32)],
        compiler_params=PARAMS,
        cost_estimate=cost(15),
        name="feed_back_two",
    )(d_ffn, red_all, exp_all, slope, d_second, unit_one, inverse_one, norms, out_all, exact, *after)


def attend_back_kernel(
    n_after, counts, to_words, to_ents, keys, values, d_context, lse, row_inner, *refs
):
    d_to_words, d_to_ents, d_keys, d_values = refs[n_after:]
    masks = head_masks(counts)
    scale = HEAD ** (-0.5)
    one, two, three, four = [], [], [], []
    for h in range(2):
        cols = slice(h * HEAD, (h + 1) * HEAD)
        scores = scores_of(masks[h], keys[...], to_words[...], to_ents[...])
        probs = jnp.exp(scores - lse[h : h + 1, :])
        d_probs = dot(values[...] * masks[h][0], d_context[...], NT)
        d_scores = (probs * (d_probs - row_inner[h : h + 1, :])).astype(bf16)
        one.append(dot(keys[:WORDS, cols], d_scores[:WORDS], TN))
        two.append(dot(keys[WORDS:, cols], d_scores[WORDS:], TN))
        three.append(
            jnp.concatenate(
                [
                    dot(d_scores[:WORDS], to_words[:, cols], NN),
                    dot(d_scores[WORDS:], to_ents[:, cols], NN),
                ],
                0,
            )
        )
        four.append(dot(probs.astype(bf16), d_context[:, cols], NN))
    d_to_words[...] = (jnp.concatenate(one, 0).T * scale).astype(bf16)
    d_to_ents[...] = (jnp.concatenate(two, 0).T * scale).astype(bf16)
    d_keys[...] = jnp.concatenate(three, 1).astype(bf16)
    d_values[...] = jnp.concatenate(four, 1).astype(bf16)


def attend_back(first, counts, to_words, to_ents, keys, values, d_context, lse, row_inner, after=()):
    after = tokens(after)
    pair = pl.BlockSpec((ROWS, 128), lambda i: (0, i + first))
    column = pl.BlockSpec((ROWS, 128), lambda i: (0, i))
    stat = pl.BlockSpec((None, 2, ROWS), lambda i: (i + first, 0, 0))
    return pl.pallas_call(
        functools.partial(attend_back_kernel, len(after)),
        grid=(HEADS // 4,),
        in_specs=[SMEM] + [pair] * 5 + [stat] * 2 + [ANY] * len(after),
        out_specs=[column] * 4,
        out_shape=[shape((ROWS, D // 2), bf16)] * 4,
        compiler_params=PARAMS,
        cost_estimate=cost(10),
        name="attend_back",
    )(counts, to_words, to_ents, keys, values, d_context, lse, row_inner, *after)


def relative():
    for x in range(2):
        for y in range(2):
            for low in range(2):
                for high in range(2):
                    yield x, y, low, high


def emit(mine, got, outs, half, first, rest, rows, value):
    if not mine:
        outs[0][(half, first) + rest + (rows,)] = value.astype(bf16)
        return
    value = (value + got[(half, first) + rest + (rows,)].astype(f32)).astype(bf16)
    if first:
        outs[half][rest + (rows,)] = value
    else:
        outs[2][(half,) + rest + (rows,)] = value


def grad_call(kernel, name, mine, operands, got, dims, extra, after):
    after = tokens(after)
    zs, rows, lanes = dims
    if mine:
        outs = [shape((2,) + zs + (rows, lanes), bf16)] * 2
        outs += [shape((2, 2) + zs + (rows, lanes), bf16)]
        operands = list(operands) + [got]
    else:
        outs = [shape((2, 2, 2) + zs + (rows, lanes), bf16)]
    return pl.pallas_call(
        functools.partial(kernel, mine, len(after), len(outs)),
        in_specs=[VMEM] * len(operands) + [ANY] * len(after),
        out_specs=[VMEM] * len(outs),
        out_shape=outs,
        scratch_shapes=extra,
        compiler_params=PARAMS,
        cost_estimate=cost(7),
        name=name,
    )(*operands, *after)


def split_refs(mine, n_after, n_outs, refs):
    got, refs = (refs[0], refs[1:]) if mine else (None, refs)
    refs = refs[n_after:]
    return got, refs[:n_outs], refs[n_outs:]


def grad_red_kernel(mine, n_after, n_outs, d_ffn, activated, *refs):
    got, outs, (whole,) = split_refs(mine, n_after, n_outs, refs)
    wide, narrow = coords()
    core = 0 if mine else 1
    for x in range(2):
        n = narrow ^ (x * 2 + core)
        lanes = pl.ds(pl.multiple_of(n * D, D), D)
        whole[...] = dot(d_ffn[...], activated[:, lanes], TN)
        for y in range(2):
            for low in range(2):
                for high in range(2):
                    w = wide ^ (high * 4 + low * 2 + y)
                    for half in range(2):
                        rows = pl.ds(pl.multiple_of(w * 96 + half * 48, 16), 48)
                        first, second = (x, y) if half == 0 else (y, x)
                        emit(
                            mine, got, outs, half, first, (second, low, high), slice(0, 48), whole[rows, :]
                        )


def grad_red(mine, d_ffn, activated, got=None, after=()):
    return grad_call(
        grad_red_kernel,
        "grad_red",
        mine,
        (d_ffn, activated),
        got,
        ((2, 2), 48, D),
        [pltpu.VMEM((D, D), f32)],
        after,
    )


def grad_exp_kernel(
    mine, n_after, n_outs, middle, d_inner_one, d_inner_two, d_out, context, norms_one, norms_two, *refs
):
    got, outs, (whole, turned, norms) = split_refs(mine, n_after, n_outs, refs)
    norms[0:2] = norms_one[...]
    norms[2:4] = norms_two[...]
    wide, narrow = coords()
    for z in range(4):
        d_inner = d_inner_one if z < 2 else d_inner_two
        whole[z] = dot(middle[...], d_inner[:, (z % 2) * D : (z % 2 + 1) * D], TN)
    for x, y, low, high in relative():
        z = (wide // 2) ^ (high * 2 + low)
        lanes = pl.ds(pl.multiple_of(((wide % 2) ^ y) * 384, 128), 384)
        for half in range(2):
            rows = pl.ds(pl.multiple_of((narrow // 2 ^ x) * 192 + half * 96, 16), 96)
            first, second = (x, y) if half == 0 else (y, x)
            emit(
                mine, got, outs, half, first, (second, low, high), slice(0, 96), whole[z, rows, lanes]
            )
    turned[...] = dot(d_out[...], context[...], TN)
    for y in range(2):
        for low in range(2):
            for high in range(2):
                w = wide ^ (high * 4 + low * 2 + y)
                blocks = packed(turned, w * 96, narrow)
                lanes = pl.ds(pl.multiple_of(jnp.minimum(w, 5) * 128, 128), 128)
                for x in range(2):
                    n = narrow ^ (x * 2 + (0 if mine else 1))
                    here = lax.broadcasted_iota(jnp.int32, (8, 128), 0) == n
                    norm = jnp.sum(jnp.where(here, norms[:, lanes], 0.0), axis=0, keepdims=True)
                    norm = jnp.broadcast_to(norm, (16, 128))
                    norm = jnp.concatenate([norm] * 3, 1)
                    lower = jnp.concatenate([norm, blocks[x][32:]], 0)
                    emit(mine, got, outs, 0, x, (y, low, high), slice(96, 128), blocks[x][:32])
                    emit(mine, got, outs, 1, y, (x, low, high), slice(96, 128), lower)


def packed(turned, start, narrow):
    upper = pl.ds(pl.multiple_of(start, 16), 48)
    lower = pl.ds(pl.multiple_of(start + 48, 16), 48)
    tail_upper = turned[upper, 256:]
    tail_lower = turned[lower, 256:]
    tails = (
        jnp.concatenate([tail_upper[:, :64], tail_lower[:, :64]], 1),
        jnp.concatenate([tail_upper[:, 64:], tail_lower[:, 64:]], 1),
    )
    x_own = narrow // 2
    out = []
    for x in range(2):
        lanes = pl.ds(pl.multiple_of((x_own ^ x) * 128, 128), 128)
        tail = jnp.where(x_own == x, tails[0], tails[1])
        out.append(jnp.concatenate([turned[upper, lanes], turned[lower, lanes], tail], 1))
    return out


def unpacked(block):
    upper = jnp.concatenate([block[..., :128], block[..., 256:320]], -1)
    lower = jnp.concatenate([block[..., 128:256], block[..., 320:]], -1)
    return jnp.concatenate([upper, lower], -2)


def grad_exp(mine, middle, d_inner_one, d_inner_two, d_out, context, norms, got=None, after=()):
    return grad_call(
        grad_exp_kernel,
        "grad_exp",
        mine,
        (middle, d_inner_one, d_inner_two, d_out, context) + norms,
        got,
        ((2, 2), 128, 384),
        [pltpu.VMEM((4, 384, D), f32), pltpu.VMEM((D, 384), f32), pltpu.VMEM((8, D), f32)],
        after,
    )


def grad_att_kernel(part, mine, n_after, n_outs, picked, d_to_words, d_to_ents, d_keys, d_values, *refs):
    got, outs, (turned,) = split_refs(mine, n_after, n_outs, refs)
    wide, narrow = coords()
    work = (
        (d_keys, slice(0, ROWS), 0, 0),
        (d_to_words, slice(0, WORDS), 0, 1),
        (d_to_words, slice(WORDS, ROWS), 0, 2),
        (d_values, slice(0, ROWS), 1, 0),
        (d_to_ents, slice(0, WORDS), 1, 1),
        (d_to_ents, slice(WORDS, ROWS), 1, 2),
    )
    for ref, rows, half, at in work:
        turned[...] = dot(ref[rows, :], picked[rows, :], TN)
        for y in range(2):
            for low in range(2):
                w = (wide % 4) ^ (low * 2 + y)
                blocks = packed(turned, w * 96, narrow)
                for x in range(2):
                    first, second = (x, y) if half == 0 else (y, x)
                    where = slice(at * 48, at * 48 + 48)
                    emit(mine, got, outs, half, first, (second, low), where, blocks[x])


def grad_att(part, mine, picked, grads, got=None, after=()):
    return grad_call(
        functools.partial(grad_att_kernel, part),
        "grad_att",
        mine,
        (picked,) + tuple(grads),
        got,
        ((2,), 144, 384),
        [pltpu.VMEM((D // 2, 384), f32)],
        after,
    )


def grad_hidden_kernel(n_after, d_first, *refs):
    grads, (kv, q), (word, ent) = refs[:8], refs[8:10], refs[10 + n_after :]
    d_to_words, d_to_ents, d_keys, d_values = [
        jnp.concatenate([grads[i][...], grads[4 + i][...]], 1) for i in range(4)
    ]
    shared = d_first[...] + dot(d_keys, kv[0], NN) + dot(d_values, kv[1], NN)
    word[...] = (
        shared[:WORDS] + dot(d_to_words[:WORDS], q[0], NN) + dot(d_to_ents[:WORDS], q[2], NN)
    )
    ent[...] = (
        shared[WORDS:] + dot(d_to_words[WORDS:], q[1], NN) + dot(d_to_ents[WORDS:], q[3], NN)
    )


def grad_hidden(d_first, grads, kv, q, after=()):
    after = tokens(after)
    return pl.pallas_call(
        functools.partial(grad_hidden_kernel, len(after)),
        in_specs=[VMEM] * 11 + [ANY] * len(after),
        out_specs=[VMEM] * 2,
        out_shape=[shape((WORDS, D), f32), shape((ENTS, D), f32)],
        compiler_params=PARAMS,
        cost_estimate=cost(9),
        name="grad_hidden",
    )(d_first, *grads, kv, q, *after)


def flip(axis, bit, value):
    size = lax.axis_size(axis)
    return lax.ppermute(value, axis, [(i, i ^ bit) for i in range(size)])


def over(name, value):
    axis, bit = {
        "core": ("narrow", 1),
        "x": ("narrow", 2),
        "y": ("wide", 1),
        "low": ("wide", 2),
        "high": ("wide", 4),
    }[name]
    return flip(axis, bit, value)


class Links:
    def __init__(self):
        self.past = {}

    def send(self, name, value):
        kind = "z" if name in ("low", "high") else name
        past = self.past.setdefault(kind, [])
        if len(past) > 1:
            value, unused = lax.optimization_barrier((value, past[-2]))
        got = over(name, value)
        past.append(got)
        return got


def later(values, token):
    return lax.optimization_barrier((values, token))[0]


def gather_high(links, first, second):
    both = jnp.concatenate([first, second], 0)
    return both, links.send("high", both)


def gather_low(links, cut, both):
    both = jnp.stack(both, 0)
    got = links.send("low", both)
    left = jnp.stack([both[:, :cut], got[:, :cut]], 0)
    right = jnp.stack([both[:, cut:], got[:, cut:]], 0)
    return left, right


def gather_near(links, left, right, token=None):
    got_left = links.send("x", left)
    got_right = links.send("y", right)
    if token is not None:
        got_left, got_right = later((got_left, got_right), token)
    left = jnp.stack([left, got_left], 0)
    right = jnp.stack([right, got_right], 0)
    return left, right


def gather_far(links, left, right):
    return gather_core(left, right, links.send("y", left), links.send("x", right))


def gather_core(left, right, left_far, right_far):
    left = jnp.stack([left, left_far], 0)
    right = jnp.stack([right, right_far], 0)
    return left, over("core", left), right, over("core", right)


def plus(kept, got):
    return (kept.astype(f32) + got.astype(f32)).astype(bf16)


class Sum:
    def __init__(self, send_left, send_right, keep):
        self.keep = keep
        self.got = over("x", send_left), over("y", send_right)

    def wait(self, token):
        self.got = later(self.got, token) if isinstance(self.got, tuple) else later((self.got,), token)[0]
        return self

    def parts(self):
        left, right = self.got
        keep = self.keep
        return (
            plus(keep[0, 1], left[1]),
            plus(keep[1, 1], right[1]),
            (plus(keep[0, 0], left[0]), plus(keep[1, 0], right[0])),
        )

    def second(self):
        left, right, self.keep = self.parts()
        self.got = over("y", left), over("x", right)

    def near(self):
        left, right = self.got
        return plus(self.keep[0], left), plus(self.keep[1], right)


def flat(blocks, leading):
    return jnp.concatenate([v.reshape(v.shape[:leading] + (-1, 384)) for v in blocks], leading)


def gather_all(value):
    size = lax.axis_size("wide") * lax.axis_size("narrow")
    spread = jnp.broadcast_to(value[None], (size,) + value.shape)
    return lax.all_to_all(spread, ("wide", "narrow"), 0, 0, tiled=False)


def sum_all(value):
    return jnp.sum(gather_all(value), axis=0)


def adapt(weight, grad, first, second, decay):
    first = 0.5 * first + 0.5 * grad
    second = 0.5 * second + 0.5 * grad * grad
    fix_first = 1.0 - 0.5**STEP
    fix_second = 1.0 - 0.5**STEP
    update = first / fix_first / (jnp.sqrt(second / fix_second) + adam_eps) + decay * weight
    return (first, second, update)


def shards(
    fast,
    word_states,
    entity_states,
    seq_counts,
    attention_weight,
    expand_weight,
    reduce_weight,
    norm_params,
    moment_attention,
    moment_expand,
    moment_reduce,
    moment_norms,
    square_attention,
    square_expand,
    square_reduce,
    square_norms,
    word_cotangent,
    entity_cotangent,
):
    word, ent, counts = word_states[0], entity_states[0], seq_counts[0]
    core = lax.axis_index("narrow") % 2
    high = lax.axis_index("wide") // 4
    if fast:
        keep, send, exp_low, red_low, weight_local = prep(
            attention_weight, expand_weight, reduce_weight.T
        )
        got = over("core", send)
        rows = jnp.where(
            core == 0, jnp.concatenate([keep, got], 2), jnp.concatenate([got, keep], 2)
        )
        links = Links()
        kv = gather_high(links, rows[4], rows[5])
        query = gather_high(
            links,
            jnp.concatenate([rows[0], rows[2]], 0),
            jnp.concatenate([rows[1], rows[3]], 0),
        )
        kv = gather_low(links, 48, kv)
        query = gather_low(links, 96, query)
        kv = gather_near(links, *kv)
        kv_pieces = gather_far(links, *kv)
        query = gather_near(links, *query)
        query_far = links.send("y", query[0]), links.send("x", query[1])
        one = gather_high(links, jnp.concatenate([exp_low[:96], rows[6]], 0), exp_low[96:])
        one = gather_low(links, 144, one)
        kv_pieces = [v.reshape(v.shape[:4] + (1, 48, 384)) for v in kv_pieces]
    else:
        weight_local = jnp.concatenate(
            [
                jnp.sum(attention_weight * attention_weight, axis=(1, 2)),
                jnp.sum(expand_weight * expand_weight)[None],
                jnp.sum(reduce_weight * reduce_weight)[None],
            ]
        )
        turned = jnp.swapaxes(attention_weight.astype(bf16), 1, 2)
        turned = lax.all_gather(turned, "wide", axis=1, tiled=True)
        turned = lax.all_gather(turned, "narrow", axis=2, tiled=True)
        exp_all = lax.all_gather(expand_weight.astype(bf16), "wide", axis=1, tiled=True)
        exp_all = lax.all_gather(exp_all, "narrow", axis=0, tiled=True)
        red_all = lax.all_gather(reduce_weight.astype(bf16).T, "wide", axis=0, tiled=True)
        red_all = lax.all_gather(red_all, "narrow", axis=1, tiled=True)
        kv_pieces = query_pieces = [turned]
        one_pieces = [turned, exp_all]
        two_pieces = [red_all]
        one = two = (None, None)

    low, keys, values, low_mine, low_other, kv_all = project_kv(fast, word, ent, kv_pieces)
    if fast:
        query_pieces = gather_core(*query, *later(query_far, keys))
        query_pieces = [v.reshape(v.shape[:4] + (2, 48, 384)) for v in query_pieces]
        two = gather_high(links, *later((red_low[:48], red_low[48:]), keys))
        one = gather_near(links, *later(one, keys))
        one_far = links.send("y", one[0]), links.send("x", one[1])
    to_words, to_ents, q_all = project_q(fast, low, query_pieces, after=two)
    if fast:
        two = gather_low(links, 48, two)
    context, exact, lse = attend(counts, to_words, to_ents, keys, values, after=one + two)
    if fast:
        two = gather_near(links, *two, token=context)
        one_pieces = gather_core(*one, *later(one_far, two))
        two_far = links.send("y", two[0]), links.send("x", two[1])
        two_core = over("core", two[0]), over("core", two[1])
    (
        middle,
        middle_low,
        activated,
        slope,
        unit_one,
        inverse_one,
        middle_mine,
        middle_other,
        context_mine,
        context_other,
        out_all,
        exp_all,
    ) = feed_in(fast, word, ent, context, norm_params, one_pieces, after=two)
    if fast:
        two_far = later(two_far, activated)
        two_pieces = (two[0], two_core[0], two[1], two_core[1])
        two_pieces += (two_far[0], over("core", two_far[0]), two_far[1], over("core", two_far[1]))
    word_out, ent_out, d_second, d_ffn, grads_two, red_all = feed_out(
        fast, activated, middle, norm_params, word_cotangent[0], entity_cotangent[0], two_pieces
    )
    got = red = exp = att_one = att_two = None
    if fast:
        got = over("core", grad_red(False, d_ffn, activated)[0])
    d_inner_one, partial = feed_back_one(0, d_ffn, red_all, exp_all, slope, d_second)
    if fast:
        red = Sum(*grad_red(True, d_ffn, activated, got, after=(partial,)))
    d_inner_two, d_first, d_out, d_context, row_inner, grads_one = feed_back_two(
        2,
        d_ffn,
        red_all,
        exp_all,
        slope,
        partial,
        unit_one,
        inverse_one,
        norm_params,
        out_all,
        exact,
        after=(red.keep,) if fast else (),
    )
    exp_args = (d_inner_one, d_inner_two, d_out)
    norm_args = (grads_one, grads_two)
    att_args = (counts, to_words, to_ents, keys, values, d_context, lse, row_inner)
    if fast:
        sent = grad_exp(False, middle_other, *exp_args, context_other, norm_args)[0]
        got = over("core", sent)
        red.wait(sent).second()
    grads = attend_back(0, *att_args, after=(red.keep + (sent,)) if fast else ())
    if fast:
        exp = Sum(*grad_exp(True, middle_mine, *exp_args, context_mine, norm_args, got, after=(grads[0],)))
        sent = grad_att(0, False, low_other, grads, after=(exp.keep,))[0]
        got = over("core", sent)
    more = attend_back(3, *att_args, after=(sent,) if fast else ())
    if fast:
        red_near = red.wait(more[0]).near()
        exp.wait(more[0]).second()
        att_one = Sum(
            *grad_att(0, True, low_mine, grads, got, after=exp.keep + red_near + (more[0],))
        )
        sent = grad_att(1, False, low_other, more, after=(att_one.keep,))[0]
        got = over("core", sent)
        exp_near = exp.wait(sent).near()
        near = flat(red_near + exp_near, 2)
        low_got = over("low", near[1])
    word_grad, ent_grad = grad_hidden(
        d_first, grads + more, kv_all, q_all, after=(sent, near) if fast else ()
    )

    if fast:
        near = plus(near[0], later((low_got,), word_grad)[0])
        high_got = over("high", near[1])
        att_two = Sum(*grad_att(1, True, low_mine, more, got, after=(word_grad, near)))
        one_left, one_right, one_keep = att_one.wait(att_two.keep).parts()
        two_left, two_right, two_keep = att_two.parts()
        left_got = over("y", jnp.concatenate([one_left, two_left], 1))
        right_got = over("x", jnp.concatenate([one_right, two_right], 1))
        high_got = later(high_got, (two_left, two_right))
        near = near[0].astype(f32) + high_got.astype(f32)
        left = plus(jnp.concatenate([one_keep[0], two_keep[0]], 1), left_got)
        right = plus(jnp.concatenate([one_keep[1], two_keep[1]], 1), right_got)
        got = over("low", jnp.concatenate([left[1], right[1]], 0))
        att_low = plus(jnp.concatenate([left[0], right[0]], 0), got).reshape(2, 2, 144, 384)
        att_low = jnp.swapaxes(att_low, 0, 1).reshape(2, 288, 384)
        red_sum = near[:192].reshape(2, 48, D)
        exp_sum = near[192:].reshape(2, 128, 384)
        norm_row = jnp.concatenate([exp_sum[1, 96, :128], jnp.pad(weight_local, (0, 119))])
        norm_rows = gather_all(norm_row)
        weight_total = jnp.sum(norm_rows[:, 128:137], axis=0)
        norm_grads = norm_rows[:, :128].reshape(8, 4, 128)[:6]
        norm_grads = jnp.swapaxes(norm_grads, 0, 1).reshape(4, D)
        first, second = att_low[0], att_low[1]
        got = over("high", jnp.where(high == 0, second, first))
        att_sum = jnp.where(high == 0, first, second).astype(f32) + got.astype(f32)
        att_sum = att_sum.reshape(2, 144, 384)
        out_rows = jnp.concatenate([exp_sum[0, 96:], exp_sum[1, 112:]], 0)
        turned = jnp.stack(
            [
                att_sum[0, 48:96],
                att_sum[1, 48:96],
                att_sum[0, 96:],
                att_sum[1, 96:],
                att_sum[0, :48],
                att_sum[1, :48],
                out_rows,
            ]
        )
        att_grad = jnp.swapaxes(unpacked(turned), 1, 2)
        exp_grad = jnp.concatenate([exp_sum[0, :96], exp_sum[1, :96]], 0)
        red_grad = jnp.concatenate([red_sum[0], red_sum[1]], 0)
    else:
        d_to_words, d_to_ents, d_keys, d_values = [
            jnp.concatenate([a, b], 1) for a, b in zip(grads, more)
        ]
        d_inner = jnp.concatenate([d_inner_one, d_inner_two], 1)
        norm_grads = sum_all(jnp.concatenate([grads_one, grads_two], 0))
        weight_total = sum_all(weight_local)
        words, ents = low[:WORDS], low[WORDS:]
        turned = jnp.stack(
            [
                dot(d_to_words[:WORDS], words, TN),
                dot(d_to_ents[:WORDS], words, TN),
                dot(d_to_words[WORDS:], ents, TN),
                dot(d_to_ents[WORDS:], ents, TN),
                dot(d_keys, low, TN),
                dot(d_values, low, TN),
                dot(d_out, context, TN),
            ]
        ).astype(bf16)
        turned = lax.psum_scatter(turned, "wide", scatter_dimension=1, tiled=True)
        turned = lax.psum_scatter(turned, "narrow", scatter_dimension=2, tiled=True)
        att_grad = jnp.swapaxes(turned.astype(f32), 1, 2)
        grad = dot(middle_low, d_inner, TN).astype(bf16)
        grad = lax.psum_scatter(grad, "wide", scatter_dimension=1, tiled=True)
        grad = lax.psum_scatter(grad, "narrow", scatter_dimension=0, tiled=True)
        exp_grad = grad.astype(f32)
        grad = dot(d_ffn, activated, TN).astype(bf16)
        grad = lax.psum_scatter(grad, "wide", scatter_dimension=0, tiled=True)
        grad = lax.psum_scatter(grad, "narrow", scatter_dimension=1, tiled=True)
        red_grad = grad.astype(f32)

    att_first, att_second, att_update = adapt(
        attention_weight, att_grad, moment_attention, square_attention, matrix_decay
    )
    exp_first, exp_second, exp_update = adapt(
        expand_weight, exp_grad, moment_expand, square_expand, matrix_decay
    )
    red_first, red_second, red_update = adapt(
        reduce_weight.T, red_grad, moment_reduce.T, square_reduce.T, matrix_decay
    )
    update_local = jnp.concatenate(
        [
            jnp.sum(att_update * att_update, axis=(1, 2)),
            jnp.sum(exp_update * exp_update)[None],
            jnp.sum(red_update * red_update)[None],
        ]
    )
    update_total = sum_all(update_local)
    nrm_first, nrm_second, nrm_update = adapt(
        norm_params, norm_grads, moment_norms, square_norms, 0.0
    )
    weight_norm = jnp.sqrt(
        jnp.concatenate([weight_total, jnp.sum(norm_params * norm_params, axis=1)])
    )
    update_norm = jnp.sqrt(
        jnp.concatenate([update_total, jnp.sum(nrm_update * nrm_update, axis=1)])
    )
    trust = weight_norm / update_norm
    new_attention = attention_weight - learn_rate * trust[0:7, None, None] * att_update
    new_expand = expand_weight - learn_rate * trust[7] * exp_update
    new_reduce = reduce_weight - learn_rate * trust[8] * red_update.T
    new_norms = norm_params - learn_rate * trust[9:13, None] * nrm_update
    trust_stats = jnp.stack([jnp.log(weight_norm), jnp.log(update_norm), jnp.log(trust)], 1)
    return (
        word_out[None],
        ent_out[None],
        word_grad[None],
        ent_grad[None],
        new_attention,
        new_expand,
        new_reduce,
        new_norms,
        att_first,
        exp_first,
        red_first.T,
        nrm_first,
        att_second,
        exp_second,
        red_second.T,
        nrm_second,
        trust_stats,
    )


def solution(mesh):
    fast = mesh.shape["wide"] == 8 and mesh.shape["narrow"] == 4
    rows = P(("wide", "narrow"), None, None)
    matrix = P("narrow", "wide")
    stack = P(None, "narrow", "wide")
    weights = (stack, matrix, matrix, P())
    return jax.shard_map(
        functools.partial(shards, fast),
        mesh=mesh,
        in_specs=(rows, rows, P(("wide", "narrow"), None)) + weights * 3 + (rows, rows),
        out_specs=(rows,) * 4 + weights * 3 + (P(),),
        check_vma=False,
    )
```

```python
import functools

import jax
import jax.numpy as jnp
from jax import lax
from jax.experimental import pallas as pl
from jax.experimental.layout import Layout, with_layout_constraint
from jax.experimental.pallas import tpu as pltpu
from jax.sharding import PartitionSpec as P

D = 768
FF = 3072
HEADS = 12
HEAD = 64
WORDS = 512
ENTS = 128
ROWS = WORDS + ENTS
STEP = 7

eps_norm = 1e-05
adam_eps = 1e-06
matrix_decay = 0.01
learn_rate = 0.5
masked_score = -1e30

f32 = jnp.float32
bf16 = jnp.bfloat16
NN = (((1,), (0,)), ((), ()))
NT = (((1,), (1,)), ((), ()))
TN = (((0,), (0,)), ((), ()))
VMEM = pl.BlockSpec(memory_space=pltpu.VMEM)
SMEM = pl.BlockSpec(memory_space=pltpu.SMEM)
ANY = pl.BlockSpec(memory_space=pl.ANY)
HBM = pl.BlockSpec(memory_space=pltpu.HBM)
COST_RATE = 4e9
PARAMS = pltpu.CompilerParams(vmem_limit_bytes=12 * 2**20)
WIDE = pltpu.CompilerParams(vmem_limit_bytes=28 * 2**20)


def dot(left, right, dims):
    return lax.dot_general(left, right, dims, preferred_element_type=f32)


def shape(dims, dtype):
    return jax.ShapeDtypeStruct(dims, dtype)


def kept(dims, dtype):
    return pltpu.VMEM(dims, dtype)


def stored(dims, dtype):
    return pltpu.HBM(dims, dtype)


def tokens(values):
    return [v for v in values if v is not None]


def cost(us, rate=COST_RATE):
    return pl.CostEstimate(flops=int(us * rate), bytes_accessed=0, transcendentals=0)


def away_blocks():
    for core in range(2):
        for outer in range(2):
            for lead in range(2):
                for low in range(2):
                    for high in range(2):
                        yield core, outer, lead, low, high


def places(wide, narrow, second, block):
    core, outer, lead, low, high = block
    x_away, y_away = (outer, lead) if second else (lead, outer)
    w = wide ^ (high * 4 + low * 2 + y_away)
    n = narrow ^ (x_away * 2 + core)
    return w, n


def piece_of(bufs, block):
    core, outer, lead, low, high = block
    return bufs[core].at[outer, lead, low, high]


def coords():
    return lax.axis_index("wide"), lax.axis_index("narrow")


def start_attention(bufs, second, target, slots, sem):
    wide, narrow = coords()
    for block in away_blocks():
        w, n = places(wide, narrow, second, block)
        row = pl.multiple_of(w * 96 + (n % 2) * 48, 16)
        lane = pl.multiple_of((n // 2) * 384, 128)
        src = piece_of(bufs, block)
        pltpu.make_async_copy(src, target.at[slots, pl.ds(row, 48), pl.ds(lane, 384)], sem).start()


def drain(ref, sem):
    pltpu.make_async_copy(ref, ref, sem).wait()


def prep_kernel(att, exp, red, keep, send, exp_low, red_low, sums):
    narrow = lax.axis_index("narrow")
    core = narrow % 2
    total = []
    for i in range(7):
        value = att[i]
        total.append(jnp.sum(value * value))
        turned = value.T.astype(bf16)
        halves = turned.reshape(2, 48, 192)

        @pl.when(core == 0)
        def _():
            keep[i] = halves[0]
            send[i] = halves[1]

        @pl.when(core == 1)
        def _():
            keep[i] = halves[1]
            send[i] = halves[0]

    value = exp[...]
    total.append(jnp.sum(value * value))
    exp_low[...] = value.astype(bf16)
    value = red[...]
    total.append(jnp.sum(value * value))
    red_low[...] = value.astype(bf16)
    for i in range(9):
        sums[i] = total[i]


def prep(att, exp, red):
    return pl.pallas_call(
        prep_kernel,
        in_specs=[VMEM] * 3,
        out_specs=[VMEM] * 4 + [SMEM],
        out_shape=[
            shape((7, 48, 192), bf16),
            shape((7, 48, 192), bf16),
            shape((192, 384), bf16),
            shape((96, D), bf16),
            shape((9,), f32),
        ],
        compiler_params=PARAMS,
        name="prep",
    )(att, exp, red)


def pick_rows(source, mine, other):
    core = lax.axis_index("narrow") % 2
    for c in range(2):

        @pl.when(core == c)
        def _():
            for target, at in ((mine, c * 192), (other, 192 - c * 192)):
                target[:, :192] = source[:, at : at + 192]
                target[:, 192:] = source[:, at + 384 : at + 576]


def pick_tiles(source, mine, other):
    core = lax.axis_index("narrow") % 2
    for c in range(2):

        @pl.when(core == c)
        def _():
            for target, at in ((mine, c * 192), (other, 192 - c * 192)):
                target[:, :128] = source[:, at : at + 128]
                target[:, 128:256] = source[:, at + 384 : at + 512]
                target[:, 256:320] = source[:, at + 128 : at + 192]
                target[:, 320:] = source[:, at + 512 : at + 576]


def project_kv_kernel(fast, n_after, word, ent, *refs):
    if fast:
        first, second, refs = refs[:2], refs[2:4], refs[4:]
    else:
        whole, refs = refs[0], refs[1:]
    low, keys, values, mine, other, saved, target, sem, sem_save = refs[n_after:]
    if fast:
        start_attention(first, False, target, pl.ds(0, 1), sem)
        start_attention(second, True, target, pl.ds(1, 1), sem)
    else:
        pltpu.make_async_copy(whole.at[pl.ds(4, 2)], target, sem).start()
    low[:WORDS] = word[...].astype(bf16)
    low[WORDS:] = ent[...].astype(bf16)
    pick_tiles(low, mine, other)
    drain(target, sem)
    save = pltpu.make_async_copy(target, saved, sem_save)
    save.start()
    keys[...] = dot(low[...], target[0], NT).astype(bf16)
    values[...] = dot(low[...], target[1], NT).astype(bf16)
    save.wait()


def project_kv(fast, word, ent, pieces, after=()):
    after = tokens(after)
    return pl.pallas_call(
        functools.partial(project_kv_kernel, fast, len(after)),
        in_specs=[VMEM, VMEM] + [ANY] * (len(pieces) + len(after)),
        out_specs=[VMEM] * 5 + [HBM],
        out_shape=[kept((ROWS, D), bf16)] * 3
        + [stored((ROWS, D // 2), bf16)] * 2
        + [stored((2, D, D), bf16)],
        scratch_shapes=[
            pltpu.VMEM((2, D, D), bf16),
            pltpu.SemaphoreType.DMA,
            pltpu.SemaphoreType.DMA,
        ],
        compiler_params=PARAMS,
        cost_estimate=cost(6, 4e8),
        name="project_kv",
    )(word, ent, *pieces, *after)


def project_q_kernel(fast, n_after, low, *refs):
    if fast:
        first, second, refs = refs[:2], refs[2:4], refs[4:]
    else:
        whole, refs = refs[0], refs[1:]
    to_words, to_ents, saved, target, sem, sem_save = refs[n_after:]
    if fast:
        start_attention(first, False, target, pl.ds(0, 2), sem)
        start_attention(second, True, target, pl.ds(2, 2), sem)
    else:
        for slot, k in enumerate((0, 2, 1, 3)):
            pltpu.make_async_copy(whole.at[k], target.at[slot], sem).start()
    drain(target, sem)
    save = pltpu.make_async_copy(target, saved, sem_save)
    save.start()
    scale = HEAD ** (-0.5)
    word = low[:WORDS]
    ent = low[WORDS:]
    to_words[:WORDS] = (dot(word, target[0], NT) * scale).astype(bf16)
    to_words[WORDS:] = (dot(ent, target[1], NT) * scale).astype(bf16)
    to_ents[:WORDS] = (dot(word, target[2], NT) * scale).astype(bf16)
    to_ents[WORDS:] = (dot(ent, target[3], NT) * scale).astype(bf16)
    save.wait()


def project_q(fast, low, pieces, after=()):
    after = tokens(after)
    return pl.pallas_call(
        functools.partial(project_q_kernel, fast, len(after)),
        in_specs=[VMEM] + [ANY] * (len(pieces) + len(after)),
        out_specs=[VMEM] * 2 + [HBM],
        out_shape=[kept((ROWS, D), bf16)] * 2 + [stored((4, D, D), bf16)],
        scratch_shapes=[
            pltpu.VMEM((4, D, D), bf16),
            pltpu.SemaphoreType.DMA,
            pltpu.SemaphoreType.DMA,
        ],
        compiler_params=PARAMS,
        cost_estimate=cost(7, 4e8),
        name="project_q",
    )(low, *pieces, *after)


def head_masks(counts):
    lane = lax.broadcasted_iota(jnp.int32, (ROWS, 128), 1)
    row = lax.broadcasted_iota(jnp.int32, (ROWS, 128), 0)
    edge = jnp.where(row < WORDS, counts[0], counts[1] + WORDS)
    bias = jnp.where(row < edge, 0.0, masked_score)
    out = []
    for h in range(2):
        own = jnp.where((lane < HEAD) if h == 0 else (lane >= HEAD), 1.0, 0.0).astype(bf16)
        mark = jnp.where(lane == (HEAD if h == 0 else 0), 1.0, 0.0)
        rest = (1.0 - mark).astype(bf16)
        tag = (bias * mark).astype(bf16)
        out.append((own, mark.astype(bf16), rest, tag))
    return out


def scores_of(masks, keys, to_words, to_ents):
    own, mark, rest, tag = masks
    tagged = keys * own + tag
    upper = dot(tagged[:WORDS], to_words * rest + mark, NT)
    lower = dot(tagged[WORDS:], to_ents * rest + mark, NT)
    return jnp.concatenate([upper, lower], 0)


def attend_kernel(n_after, counts, to_words, to_ents, keys, values, *refs):
    context, exact, lse = refs[n_after:]
    masks = head_masks(counts)
    pair = pl.program_id(0)
    lanes = pl.ds(pl.multiple_of(pair * 128, 128), 128)
    key, value = keys[:, lanes], values[:, lanes]
    outs = []
    for h in range(2):
        scores = scores_of(masks[h], key, to_words[:, lanes], to_ents[:, lanes])
        top = jnp.max(scores, axis=0, keepdims=True)
        expd = jnp.exp(scores - top)
        total = jnp.sum(expd, axis=0, keepdims=True)
        lse[pair, h : h + 1, :] = top + jnp.log(total)
        mixed = dot(value[:, h * HEAD : (h + 1) * HEAD], expd.astype(bf16), TN)
        outs.append(mixed * (1.0 / total))
    joined = jnp.concatenate(outs, 0).T
    exact[...] = joined
    context[:, lanes] = joined.astype(bf16)


def attend(counts, to_words, to_ents, keys, values, after=()):
    after = tokens(after)
    return pl.pallas_call(
        functools.partial(attend_kernel, len(after)),
        grid=(HEADS // 2,),
        in_specs=[SMEM] + [VMEM] * 4 + [ANY] * len(after),
        out_specs=[VMEM, pl.BlockSpec((ROWS, 128), lambda i: (0, i)), VMEM],
        out_shape=[
            kept((ROWS, D), bf16),
            stored((ROWS, D), f32),
            kept((HEADS // 2, 2, ROWS), f32),
        ],
        compiler_params=PARAMS,
        cost_estimate=cost(12, 4e8),
        name="attend",
    )(counts, to_words, to_ents, keys, values, *after)


def normed(value):
    center = value - jnp.mean(value, axis=-1, keepdims=True)
    spread = jnp.mean(center * center, axis=-1, keepdims=True)
    inverse = lax.rsqrt(spread + eps_norm)
    return center * inverse, inverse


def normed_back(unit, inverse, cotangent):
    mean = jnp.mean(cotangent, axis=-1, keepdims=True)
    inner = jnp.mean(cotangent * unit, axis=-1, keepdims=True)
    return inverse * (cotangent - mean - unit * inner)


def column_sum(value):
    return jnp.sum(value, axis=0, keepdims=True)


def feed_in_kernel(fast, n_after, word, ent, context, norms, *refs):
    if fast:
        bufs, refs = (refs[0:2], refs[2:4]), refs[4:]
    else:
        bufs, refs = refs[0:2], refs[2:]
    (
        middle_saved,
        middle_low,
        act_saved,
        slope_saved,
        unit_saved,
        picks_saved,
        out_saved,
        exp_saved,
        middle,
        activated,
        slope,
        unit_here,
        picks,
        out_all,
        exp_all,
        sem_out,
        sem_exp,
        sem_save,
    ) = refs[n_after:]
    step = pl.program_id(0)
    pairs = (
        (unit_here, unit_saved),
        (picks, picks_saved),
        (out_all, out_saved),
        (middle, middle_saved),
    )
    saves = [pltpu.make_async_copy(*pair, sem_save.at[i]) for i, pair in enumerate(pairs)]

    @pl.when(step == 0)
    def _():
        if fast:
            start_feed_in(bufs, out_all, exp_all, sem_out, sem_exp)
        else:
            pltpu.make_async_copy(bufs[0].at[6], out_all, sem_out).start()
            for j in range(4):
                cols = pl.ds(j * D, D)
                pltpu.make_async_copy(bufs[1].at[:, cols], exp_all.at[j], sem_exp.at[j]).start()
        drain(out_all, sem_out)
        saves[2].start()
        hidden = jnp.concatenate([word[...], ent[...]], 0)
        unit, inverse = normed(hidden + dot(context[...], out_all[...], NT))
        value = unit * norms[0:1, :] + norms[1:2, :]
        unit_here[:, :D] = unit
        unit_here[:, D:] = jnp.broadcast_to(inverse, (ROWS, 128))
        saves[0].start()
        middle_low[...] = value.astype(bf16)
        middle[...] = value
        saves[3].start()
        pick_rows(middle_low, picks.at[0], picks.at[1])
        pick_tiles(context, picks.at[2], picks.at[3])
        saves[1].start()

    drain(exp_all.at[step], sem_exp.at[step])
    pltpu.make_async_copy(exp_all.at[step], exp_saved.at[step], sem_save.at[4 + step]).start()
    inner = dot(middle_low[...], exp_all[step], NN)
    share = 0.5 + 0.5 * lax.erf(inner * 0.7071067811865476)
    bell = jnp.exp(-0.5 * inner * inner) * 0.3989422804014327
    slope[step] = (share + inner * bell).astype(bf16)
    activated[step] = (inner * share).astype(bf16)
    pltpu.make_async_copy(slope.at[step], slope_saved.at[step], sem_save.at[8 + step]).start()
    pltpu.make_async_copy(activated.at[step], act_saved.at[step], sem_save.at[12 + step]).start()

    @pl.when(step == 3)
    def _():
        for save in saves:
            save.wait()
        for j in range(4):
            pltpu.make_async_copy(exp_all.at[j], exp_saved.at[j], sem_save.at[4 + j]).wait()
            pltpu.make_async_copy(slope.at[j], slope_saved.at[j], sem_save.at[8 + j]).wait()
            pltpu.make_async_copy(activated.at[j], act_saved.at[j], sem_save.at[12 + j]).wait()


def start_feed_in(bufs, out_all, exp_all, sem_out, sem_exp):
    wide, narrow = coords()
    for block in away_blocks():
        w, n = places(wide, narrow, False, block)
        row = pl.multiple_of(w * 96 + (n % 2) * 48, 16)
        lane = pl.multiple_of((n // 2) * 384, 128)
        src = piece_of(bufs[0], block).at[pl.ds(96, 48)]
        pltpu.make_async_copy(src, out_all.at[pl.ds(row, 48), pl.ds(lane, 384)], sem_out).start()
    for half in range(2):
        for block in away_blocks():
            w, n = places(wide, narrow, half == 1, block)
            src = piece_of(bufs[half], block)
            if half == 0:
                src = src.at[pl.ds(0, 96)]
            row = pl.multiple_of(n * 192 + half * 96, 16)
            lane = pl.multiple_of((w % 2) * 384, 128)
            dst = exp_all.at[w // 2, pl.ds(row, 96), pl.ds(lane, 384)]
            pltpu.make_async_copy(src, dst, sem_exp.at[w // 2]).start()


def feed_in(fast, word, ent, context, norms, pieces, after=()):
    after = tokens(after)
    return pl.pallas_call(
        functools.partial(feed_in_kernel, fast, len(after)),
        grid=(4,),
        in_specs=[VMEM] * 4 + [ANY] * (len(pieces) + len(after)),
        out_specs=[HBM, VMEM] + [HBM] * 6,
        out_shape=[
            stored((ROWS, D), f32),
            kept((ROWS, D), bf16),
            stored((4, ROWS, D), bf16),
            stored((4, ROWS, D), bf16),
            stored((ROWS, D + 128), f32),
            stored((4, ROWS, D // 2), bf16),
            stored((D, D), bf16),
            stored((4, D, D), bf16),
        ],
        scratch_shapes=[
            pltpu.VMEM((ROWS, D), f32),
            pltpu.VMEM((4, ROWS, D), bf16),
            pltpu.VMEM((4, ROWS, D), bf16),
            pltpu.VMEM((ROWS, D + 128), f32),
            pltpu.VMEM((4, ROWS, D // 2), bf16),
            pltpu.VMEM((D, D), bf16),
            pltpu.VMEM((4, D, D), bf16),
            pltpu.SemaphoreType.DMA,
            pltpu.SemaphoreType.DMA((4,)),
            pltpu.SemaphoreType.DMA((16,)),
        ],
        compiler_params=pltpu.CompilerParams(vmem_limit_bytes=28 * 2**20),
        cost_estimate=cost(12),
        name="feed_in",
    )(word, ent, context, norms, *pieces, *after)


def feed_out_kernel(fast, n_after, norms, activated, middle, word_cot, ent_cot, *refs):
    if fast:
        bufs, refs = (refs[0:2], refs[2:4], refs[4:6], refs[6:8]), refs[8:]
    else:
        bufs, refs = refs[0:1], refs[1:]
    (
        word_out,
        ent_out,
        second_saved,
        d_ffn,
        grads_two,
        red_saved,
        total,
        cot_here,
        middle_here,
        d_second,
        act_here,
        red_all,
        sem_red,
        sem_act,
        sem_save,
        sem_late,
    ) = refs[n_after:]
    step = pl.program_id(0)
    upper, lower = pl.ds(0, WORDS), pl.ds(WORDS, ENTS)
    late = (
        pltpu.make_async_copy(word_cot, cot_here.at[upper], sem_late.at[0]),
        pltpu.make_async_copy(ent_cot, cot_here.at[lower], sem_late.at[1]),
        pltpu.make_async_copy(middle, middle_here, sem_late.at[2]),
    )
    saves = (
        pltpu.make_async_copy(total.at[upper], word_out, sem_save.at[0]),
        pltpu.make_async_copy(total.at[lower], ent_out, sem_save.at[1]),
        pltpu.make_async_copy(d_second, second_saved, sem_save.at[2]),
    )

    @pl.when(step == 0)
    def _():
        for j in range(4):
            pltpu.make_async_copy(activated.at[j], act_here.at[j], sem_act.at[j]).start()
        if fast:
            start_feed_out(bufs, red_all, sem_red)
        else:
            for j in range(4):
                cols = pl.ds(j * D, D)
                pltpu.make_async_copy(bufs[0].at[:, cols], red_all.at[j], sem_red.at[j]).start()
        for copy in late:
            copy.start()

    drain(act_here.at[step], sem_act.at[step])
    drain(red_all.at[step], sem_red.at[step])
    pltpu.make_async_copy(red_all.at[step], red_saved.at[step], sem_save.at[3 + step]).start()
    part = dot(act_here[step], red_all[step], NT)

    @pl.when(step == 0)
    def _():
        total[...] = part

    @pl.when(step > 0)
    def _():
        total[...] += part

    @pl.when(step == 3)
    def _():
        for copy in late:
            copy.wait()
        unit, inverse = normed(total[...] + middle_here[...])
        total[...] = unit * norms[2:3, :] + norms[3:4, :]
        saves[0].start()
        saves[1].start()
        cot = cot_here[...]
        back = normed_back(unit, inverse, cot * norms[2:3, :])
        d_second[...] = back
        saves[2].start()
        d_ffn[...] = back.astype(bf16)
        grads_two[0:1, :] = column_sum(cot * unit)
        grads_two[1:2, :] = column_sum(cot)
        for save in saves:
            save.wait()
        for j in range(4):
            pltpu.make_async_copy(red_all.at[j], red_saved.at[j], sem_save.at[3 + j]).wait()


def start_feed_out(bufs, red_all, sem_red):
    wide, narrow = coords()
    for half in range(2):
        for block in away_blocks():
            w, n = places(wide, narrow, half == 1, block)
            core, outer, lead, low, high = block
            src = bufs[half + 2 * outer][core].at[lead, low, high]
            row = pl.multiple_of(w * 96 + half * 48, 16)
            pltpu.make_async_copy(src, red_all.at[n, pl.ds(row, 48)], sem_red.at[n]).start()


def feed_out(fast, activated, middle, norms, word_cot, ent_cot, pieces, after=()):
    after = tokens(after)
    return pl.pallas_call(
        functools.partial(feed_out_kernel, fast, len(after)),
        grid=(4,),
        in_specs=[VMEM] + [HBM] * 4 + [ANY] * (len(pieces) + len(after)),
        out_specs=[HBM] * 3 + [VMEM] * 2 + [HBM],
        out_shape=[
            stored((WORDS, D), f32),
            stored((ENTS, D), f32),
            stored((ROWS, D), f32),
            kept((ROWS, D), bf16),
            kept((2, D), f32),
            stored((4, D, D), bf16),
        ],
        scratch_shapes=[
            pltpu.VMEM((ROWS, D), f32),
            pltpu.VMEM((ROWS, D), f32),
            pltpu.VMEM((ROWS, D), f32),
            pltpu.VMEM((ROWS, D), f32),
            pltpu.VMEM((4, ROWS, D), bf16),
            pltpu.VMEM((4, D, D), bf16),
            pltpu.SemaphoreType.DMA((4,)),
            pltpu.SemaphoreType.DMA((4,)),
            pltpu.SemaphoreType.DMA((7,)),
            pltpu.SemaphoreType.DMA((3,)),
        ],
        compiler_params=pltpu.CompilerParams(vmem_limit_bytes=56 * 2**20),
        cost_estimate=cost(12),
        name="feed_out",
    )(norms, activated, middle, word_cot, ent_cot, *pieces, *after)


def feed_back_kernel(
    n_after, d_ffn, norms, red_all, exp_all, slope, d_second, unit_one, out_all, exact, *refs
):
    (
        d_inner,
        d_first,
        d_out,
        d_context,
        row_inner,
        grads_one,
        total,
        red_here,
        exp_here,
        slope_here,
        second_here,
        unit_here,
        out_here,
        exact_here,
        sem_step,
        sem_late,
        sem_save,
    ) = refs[n_after:]
    step = pl.program_id(0)
    pairs = (
        (d_second, second_here),
        (unit_one, unit_here),
        (out_all, out_here),
        (exact, exact_here),
    )
    late = [pltpu.make_async_copy(*pair, sem_late.at[i]) for i, pair in enumerate(pairs)]
    save = pltpu.make_async_copy(total, d_first, sem_save)
    parts = ((red_all, red_here), (slope, slope_here), (exp_all, exp_here))

    @pl.when(step == 0)
    def _():
        for j in range(4):
            for k, (there, here) in enumerate(parts):
                pltpu.make_async_copy(there.at[j], here.at[j], sem_step.at[k, j]).start()
        for copy in late:
            copy.start()

    drain(red_here.at[step], sem_step.at[0, step])
    drain(slope_here.at[step], sem_step.at[1, step])
    drain(exp_here.at[step], sem_step.at[2, step])
    lanes = pl.ds(pl.multiple_of(step * D, D), D)
    back = (dot(d_ffn[...], red_here[step], NN) * slope_here[step].astype(f32)).astype(bf16)
    d_inner[:, lanes] = back
    part = dot(back, exp_here[step], NT)

    @pl.when(step == 0)
    def _():
        total[...] = part

    @pl.when(step > 0)
    def _():
        total[...] += part

    @pl.when(step == 3)
    def _():
        for copy in late:
            copy.wait()
        d_middle = total[...] + second_here[...]
        unit = unit_here[:, :D]
        grads_one[0:1, :] = column_sum(d_middle * unit)
        grads_one[1:2, :] = column_sum(d_middle)
        first = normed_back(unit, unit_here[:, D : D + 1], d_middle * norms[0:1, :])
        total[...] = first
        save.start()
        low_first = first.astype(bf16)
        d_out[...] = low_first
        context = dot(low_first, out_here[...], NN).astype(bf16)
        d_context[...] = context
        product = context.astype(f32) * exact_here[...]
        head = lax.broadcasted_iota(jnp.int32, (16, D), 1) // HEAD
        pick = jnp.where(head == lax.broadcasted_iota(jnp.int32, (16, D), 0), 1.0, 0.0).astype(bf16)
        high = product.astype(bf16)
        low = (product - high.astype(f32)).astype(bf16)
        sums = dot(pick, high, NT) + dot(pick, low, NT)
        for i in range(HEADS // 2):
            row_inner[i] = sums[2 * i : 2 * i + 2]
        save.wait()


def feed_back(d_ffn, red_all, exp_all, slope, norms, d_second, unit_one, out_all, exact, after=()):
    after = tokens(after)
    return pl.pallas_call(
        functools.partial(feed_back_kernel, len(after)),
        grid=(4,),
        in_specs=[VMEM, VMEM] + [HBM] * 7 + [ANY] * len(after),
        out_specs=[VMEM, HBM] + [VMEM] * 4,
        out_shape=[
            kept((ROWS, FF), bf16),
            stored((ROWS, D), f32),
            kept((ROWS, D), bf16),
            kept((ROWS, D), bf16),
            kept((HEADS // 2, 2, ROWS), f32),
            kept((2, D), f32),
        ],
        scratch_shapes=[
            pltpu.VMEM((ROWS, D), f32),
            pltpu.VMEM((4, D, D), bf16),
            pltpu.VMEM((4, D, D), bf16),
            pltpu.VMEM((4, ROWS, D), bf16),
            pltpu.VMEM((ROWS, D), f32),
            pltpu.VMEM((ROWS, D + 128), f32),
            pltpu.VMEM((D, D), bf16),
            pltpu.VMEM((ROWS, D), f32),
            pltpu.SemaphoreType.DMA((3, 4)),
            pltpu.SemaphoreType.DMA((4,)),
            pltpu.SemaphoreType.DMA,
        ],
        compiler_params=pltpu.CompilerParams(vmem_limit_bytes=36 * 2**20),
        cost_estimate=cost(14),
        name="feed_back",
    )(d_ffn, norms, red_all, exp_all, slope, d_second, unit_one, out_all, exact, *after)


def attend_back_kernel(
    first, n_after, counts, to_words, to_ents, keys, values, d_context, lse, row_inner, *refs
):
    d_to_words, d_to_ents, d_keys, d_values = refs[n_after:]
    masks = head_masks(counts)
    scale = HEAD ** (-0.5)
    step = pl.program_id(0)
    pair = step + first
    lanes = pl.ds(pl.multiple_of(pair * 128, 128), 128)
    here = pl.ds(pl.multiple_of(step * 128, 128), 128)
    word_query, ent_query = to_words[...], to_ents[...]
    key, value, d_mixed = keys[...], values[...], d_context[:, lanes]
    one, two, three, four = [], [], [], []
    for h in range(2):
        cols = slice(h * HEAD, (h + 1) * HEAD)
        scores = scores_of(masks[h], key, word_query, ent_query)
        probs = jnp.exp(scores - lse[pair, h : h + 1, :])
        d_probs = dot(value * masks[h][0], d_mixed, NT)
        d_scores = (probs * (d_probs - row_inner[pair, h : h + 1, :])).astype(bf16)
        one.append(dot(key[:WORDS, cols], d_scores[:WORDS], TN))
        two.append(dot(key[WORDS:, cols], d_scores[WORDS:], TN))
        three.append(
            jnp.concatenate(
                [
                    dot(d_scores[:WORDS], word_query[:, cols], NN),
                    dot(d_scores[WORDS:], ent_query[:, cols], NN),
                ],
                0,
            )
        )
        four.append(dot(probs.astype(bf16), d_mixed[:, cols], NN))
    d_to_words[:, here] = (jnp.concatenate(one, 0).T * scale).astype(bf16)
    d_to_ents[:, here] = (jnp.concatenate(two, 0).T * scale).astype(bf16)
    d_keys[:, here] = jnp.concatenate(three, 1).astype(bf16)
    d_values[:, here] = jnp.concatenate(four, 1).astype(bf16)


def attend_back(first, counts, to_words, to_ents, keys, values, d_context, lse, row_inner, after=()):
    after = tokens(after)
    pair = pl.BlockSpec((ROWS, 128), lambda i: (0, i + first))
    return pl.pallas_call(
        functools.partial(attend_back_kernel, first, len(after)),
        grid=(HEADS // 4,),
        in_specs=[SMEM] + [pair] * 4 + [VMEM] * 3 + [ANY] * len(after),
        out_specs=[VMEM] * 4,
        out_shape=[kept((ROWS, D // 2), bf16)] * 4,
        compiler_params=PARAMS,
        cost_estimate=cost(10),
        name="attend_back",
    )(counts, to_words, to_ents, keys, values, d_context, lse, row_inner, *after)


def relative():
    for x in range(2):
        for y in range(2):
            for low in range(2):
                for high in range(2):
                    yield x, y, low, high


def emit(mine, got, outs, half, first, rest, rows, value):
    if not mine:
        outs[0][(half, first) + rest + (rows,)] = value.astype(bf16)
        return
    value = (value + got[(half, first) + rest + (rows,)].astype(f32)).astype(bf16)
    if first:
        outs[half][rest + (rows,)] = value
    else:
        outs[2][(half,) + rest + (rows,)] = value


def grad_call(kernel, name, mine, operands, got, steps, dims, extra, after, specs=(), limit=12):
    after = tokens(after)
    if mine:
        outs = [kept((2,) + dims, bf16)] * 2 + [kept((2, 2) + dims, bf16)]
        operands = list(operands) + [got]
    else:
        outs = [kept((2, 2, 2) + dims, bf16)]
    return pl.pallas_call(
        functools.partial(kernel, mine, len(after), len(outs)),
        grid=(steps,),
        in_specs=list(specs)
        + [VMEM] * (len(operands) - len(specs))
        + [ANY] * len(after),
        out_specs=[VMEM] * len(outs),
        out_shape=outs,
        scratch_shapes=extra,
        compiler_params=pltpu.CompilerParams(vmem_limit_bytes=limit * 2**20),
        cost_estimate=cost(7),
        name=name,
    )(*operands, *after)


def split_refs(mine, n_after, n_outs, refs):
    got, refs = (refs[0], refs[1:]) if mine else (None, refs)
    refs = refs[n_after:]
    return got, refs[:n_outs], refs[n_outs:]


def grad_red_kernel(mine, n_after, n_outs, d_ffn, activated, *refs):
    got, outs, (whole, act, sem) = split_refs(mine, n_after, n_outs, refs)
    wide, narrow = coords()
    for x in range(2):
        n = narrow ^ (x * 2 + (0 if mine else 1))
        pltpu.make_async_copy(activated.at[n], act.at[x], sem.at[x]).start()
    for x in range(2):
        drain(act.at[x], sem.at[x])
        whole[...] = dot(d_ffn[...], act[x], TN)
        for y in range(2):
            for low in range(2):
                for high in range(2):
                    w = wide ^ (high * 4 + low * 2 + y)
                    for half in range(2):
                        rows = pl.ds(pl.multiple_of(w * 96 + half * 48, 16), 48)
                        first, second = (x, y) if half == 0 else (y, x)
                        rest = (second, low, high)
                        emit(mine, got, outs, half, first, rest, slice(0, 48), whole[rows, :])


def grad_red(mine, d_ffn, activated, got=None, after=()):
    scratch = [
        pltpu.VMEM((D, D), f32),
        pltpu.VMEM((2, ROWS, D), bf16),
        pltpu.SemaphoreType.DMA((2,)),
    ]
    operands, specs = (d_ffn, activated), [VMEM, HBM]
    return grad_call(
        grad_red_kernel, "grad_red", mine, operands, got, 1, (2, 2, 48, D), scratch, after, specs, 24
    )


def grad_exp_kernel(
    mine, n_after, n_outs, picks, d_inner, d_out, norms_one, norms_two, *refs
):
    got, outs, (whole, turned, norms, middle, context, sem) = split_refs(
        mine, n_after, n_outs, refs
    )
    wide, narrow = coords()
    step = pl.program_id(0)

    @pl.when(step == 0)
    def _():
        at = 0 if mine else 1
        pltpu.make_async_copy(picks.at[at], middle, sem.at[0]).start()
        pltpu.make_async_copy(picks.at[at + 2], context, sem.at[1]).start()
        drain(middle, sem.at[0])
        drain(context, sem.at[1])
        norms[0:2] = norms_one[...]
        norms[2:4] = norms_two[...]
        turned[...] = dot(d_out[...], context[...], TN)

    z = (wide // 2) ^ step
    whole[...] = dot(middle[...], d_inner[:, pl.ds(pl.multiple_of(z * D, D), D)], TN)
    low, high = step % 2, step // 2
    for y in range(2):
        w = wide ^ (step * 2 + y)
        lanes = pl.ds(pl.multiple_of((w % 2) * 384, 128), 384)
        blocks = packed(turned, w * 96, narrow)
        norm_lanes = pl.ds(pl.multiple_of(jnp.minimum(w, 5) * 128, 128), 128)
        for x in range(2):
            n = narrow ^ (x * 2 + (0 if mine else 1))
            for half in range(2):
                rows = pl.ds(pl.multiple_of((n // 2) * 192 + half * 96, 16), 96)
                first, second = (x, y) if half == 0 else (y, x)
                rest = (second, low, high)
                emit(mine, got, outs, half, first, rest, slice(0, 96), whole[rows, lanes])
            here = lax.broadcasted_iota(jnp.int32, (8, 128), 0) == n
            norm = jnp.sum(jnp.where(here, norms[:, norm_lanes], 0.0), axis=0, keepdims=True)
            norm = jnp.broadcast_to(norm, (16, 128))
            norm = jnp.concatenate([norm] * 3, 1)
            lower = jnp.concatenate([norm, blocks[x][32:]], 0)
            emit(mine, got, outs, 0, x, (y, low, high), slice(96, 128), blocks[x][:32])
            emit(mine, got, outs, 1, y, (x, low, high), slice(96, 128), lower)


def packed(turned, start, narrow):
    upper = pl.ds(pl.multiple_of(start, 16), 48)
    lower = pl.ds(pl.multiple_of(start + 48, 16), 48)
    tail_upper = turned[upper, 256:]
    tail_lower = turned[lower, 256:]
    tails = (
        jnp.concatenate([tail_upper[:, :64], tail_lower[:, :64]], 1),
        jnp.concatenate([tail_upper[:, 64:], tail_lower[:, 64:]], 1),
    )
    x_own = narrow // 2
    out = []
    for x in range(2):
        lanes = pl.ds(pl.multiple_of((x_own ^ x) * 128, 128), 128)
        tail = jnp.where(x_own == x, tails[0], tails[1])
        out.append(jnp.concatenate([turned[upper, lanes], turned[lower, lanes], tail], 1))
    return out


def unpacked(block):
    upper = jnp.concatenate([block[..., :128], block[..., 256:320]], -1)
    lower = jnp.concatenate([block[..., 128:256], block[..., 320:]], -1)
    return jnp.concatenate([upper, lower], -2)


def grad_exp(mine, picks, d_inner, d_out, norms, got=None, after=()):
    operands, specs = (picks, d_inner, d_out) + norms, [HBM]
    scratch = [
        pltpu.VMEM((384, D), f32),
        pltpu.VMEM((D, 384), f32),
        pltpu.VMEM((8, D), f32),
        pltpu.VMEM((ROWS, D // 2), bf16),
        pltpu.VMEM((ROWS, D // 2), bf16),
        pltpu.SemaphoreType.DMA((2,)),
    ]
    return grad_call(
        grad_exp_kernel, "grad_exp", mine, operands, got, 4, (2, 2, 128, 384), scratch, after, specs
    )


def grad_att_kernel(
    part, mine, n_after, n_outs, picked, d_to_words, d_to_ents, d_keys, d_values, *refs
):
    got, outs, (turned,) = split_refs(mine, n_after, n_outs, refs)
    wide, narrow = coords()
    work = (
        (d_keys, slice(0, ROWS), 0, 0),
        (d_to_words, slice(0, WORDS), 0, 1),
        (d_to_words, slice(WORDS, ROWS), 0, 2),
        (d_values, slice(0, ROWS), 1, 0),
        (d_to_ents, slice(0, WORDS), 1, 1),
        (d_to_ents, slice(WORDS, ROWS), 1, 2),
    )
    for ref, rows, half, at in work:
        turned[...] = dot(ref[rows, :], picked[rows, :], TN)
        for y in range(2):
            for low in range(2):
                w = (wide % 4) ^ (low * 2 + y)
                blocks = packed(turned, w * 96, narrow)
                for x in range(2):
                    first, second = (x, y) if half == 0 else (y, x)
                    where = slice(at * 48, at * 48 + 48)
                    emit(mine, got, outs, half, first, (second, low), where, blocks[x])


def grad_att(part, mine, picked, grads, got=None, after=()):
    kernel = functools.partial(grad_att_kernel, part)
    operands = (picked,) + tuple(grads)
    scratch = [pltpu.VMEM((D // 2, 384), f32)]
    return grad_call(
        kernel, "grad_att", mine, operands, got, 1, (2, 144, 384), scratch, after
    )


def grad_hidden_kernel(n_after, kv, q, *refs):
    grads, d_first = refs[:8], refs[8]
    word, ent, joined, first_here, sem = refs[9 + n_after :]
    step = pl.program_id(0)
    upper, lower = slice(0, WORDS), slice(WORDS, ROWS)
    late = pltpu.make_async_copy(d_first, first_here, sem)

    def both(kind):
        joined[:, : D // 2] = grads[kind][...]
        joined[:, D // 2 :] = grads[4 + kind][...]

    @pl.when(step == 0)
    def _():
        late.start()
        both(2)
        word[...] = dot(joined[upper], kv[...], NN)
        ent[...] = dot(joined[lower], kv[...], NN)

    @pl.when(step == 1)
    def _():
        both(3)
        word[...] += dot(joined[upper], kv[...], NN)
        ent[...] += dot(joined[lower], kv[...], NN)

    @pl.when(step == 2)
    def _():
        both(0)
        word[...] += dot(joined[upper], q[...], NN)

    @pl.when(step == 3)
    def _():
        ent[...] += dot(joined[lower], q[...], NN)

    @pl.when(step == 4)
    def _():
        both(1)
        late.wait()
        word[...] += first_here[upper] + dot(joined[upper], q[...], NN)

    @pl.when(step == 5)
    def _():
        ent[...] += first_here[lower] + dot(joined[lower], q[...], NN)


def grad_hidden(d_first, grads, kv, q, after=()):
    after = tokens(after)
    return pl.pallas_call(
        functools.partial(grad_hidden_kernel, len(after)),
        grid=(6,),
        in_specs=[
            pl.BlockSpec((None, D, D), lambda i: (jnp.minimum(i, 1), 0, 0)),
            pl.BlockSpec((None, D, D), lambda i: (jnp.maximum(i - 2, 0), 0, 0)),
        ]
        + [VMEM] * 8
        + [HBM]
        + [ANY] * len(after),
        out_specs=[VMEM] * 2,
        out_shape=[stored((WORDS, D), f32), stored((ENTS, D), f32)],
        scratch_shapes=[
            pltpu.VMEM((ROWS, D), bf16),
            pltpu.VMEM((ROWS, D), f32),
            pltpu.SemaphoreType.DMA,
        ],
        compiler_params=PARAMS,
        cost_estimate=cost(9),
        name="grad_hidden",
    )(kv, q, *grads, d_first, *after)


def flip(axis, bit, value):
    size = lax.axis_size(axis)
    return lax.ppermute(value, axis, [(i, i ^ bit) for i in range(size)])


def over(name, value):
    axis, bit = {
        "core": ("narrow", 1),
        "x": ("narrow", 2),
        "y": ("wide", 1),
        "low": ("wide", 2),
        "high": ("wide", 4),
    }[name]
    return flip(axis, bit, value)


class Links:
    def __init__(self):
        self.past = {}

    def send(self, name, value):
        kind = "z" if name in ("low", "high") else name
        past = self.past.setdefault(kind, [])
        if len(past) > 1:
            value, unused = lax.optimization_barrier((value, past[-2]))
        got = over(name, value)
        past.append(got)
        return got


def later(values, token):
    return lax.optimization_barrier((values, token))[0]


def gather_high(links, first, second):
    both = jnp.concatenate([first, second], 0)
    return both, links.send("high", both)


def gather_low(links, cut, both):
    both = jnp.stack(both, 0)
    got = links.send("low", both)
    left = jnp.stack([both[:, :cut], got[:, :cut]], 0)
    right = jnp.stack([both[:, cut:], got[:, cut:]], 0)
    return left, right


def gather_near(links, left, right, token=None):
    got_left = links.send("x", left)
    got_right = links.send("y", right)
    if token is not None:
        got_left, got_right = later((got_left, got_right), token)
    left = jnp.stack([left, got_left], 0)
    right = jnp.stack([right, got_right], 0)
    return left, right


def gather_far(links, left, right):
    return gather_core(left, right, links.send("y", left), links.send("x", right))


def gather_core(left, right, left_far, right_far):
    left = jnp.stack([left, left_far], 0)
    right = jnp.stack([right, right_far], 0)
    return left, over("core", left), right, over("core", right)


def plus(kept, got):
    return (kept.astype(f32) + got.astype(f32)).astype(bf16)


class Sum:
    def __init__(self, send_left, send_right, keep):
        self.keep = keep
        self.got = over("x", send_left), over("y", send_right)

    def wait(self, token):
        self.got = later(self.got, token) if isinstance(self.got, tuple) else later((self.got,), token)[0]
        return self

    def parts(self):
        left, right = self.got
        keep = self.keep
        return (
            plus(keep[0, 1], left[1]),
            plus(keep[1, 1], right[1]),
            (plus(keep[0, 0], left[0]), plus(keep[1, 0], right[0])),
        )

    def second(self):
        left, right, self.keep = self.parts()
        self.got = over("y", left), over("x", right)

    def near(self):
        left, right = self.got
        return plus(self.keep[0], left), plus(self.keep[1], right)


def flat(blocks, leading):
    return jnp.concatenate([v.reshape(v.shape[:leading] + (-1, 384)) for v in blocks], leading)


def gather_all(value):
    size = lax.axis_size("wide") * lax.axis_size("narrow")
    spread = jnp.broadcast_to(value[None], (size,) + value.shape)
    return lax.all_to_all(spread, ("wide", "narrow"), 0, 0, tiled=False)


def sum_all(value):
    return jnp.sum(gather_all(value), axis=0)


def adapt(weight, grad, first, second, decay):
    first = 0.5 * first + 0.5 * grad
    second = 0.5 * second + 0.5 * grad * grad
    fix_first = 1.0 - 0.5**STEP
    fix_second = 1.0 - 0.5**STEP
    update = first / fix_first / (jnp.sqrt(second / fix_second) + adam_eps) + decay * weight
    return (first, second, update)


def shards(
    fast,
    word_states,
    entity_states,
    seq_counts,
    attention_weight,
    expand_weight,
    reduce_weight,
    norm_params,
    moment_attention,
    moment_expand,
    moment_reduce,
    moment_norms,
    square_attention,
    square_expand,
    square_reduce,
    square_norms,
    word_cotangent,
    entity_cotangent,
):
    word, ent, counts = word_states[0], entity_states[0], seq_counts[0]
    core = lax.axis_index("narrow") % 2
    high = lax.axis_index("wide") // 4
    if fast:
        keep, send, exp_low, red_low, weight_local = prep(
            attention_weight, expand_weight, reduce_weight.T
        )
        got = over("core", send)
        rows = jnp.where(
            core == 0, jnp.concatenate([keep, got], 2), jnp.concatenate([got, keep], 2)
        )
        links = Links()
        kv = gather_high(links, rows[4], rows[5])
        query = gather_high(
            links,
            jnp.concatenate([rows[0], rows[2]], 0),
            jnp.concatenate([rows[1], rows[3]], 0),
        )
        kv = gather_low(links, 48, kv)
        query = gather_low(links, 96, query)
        kv = gather_near(links, *kv)
        kv_pieces = gather_far(links, *kv)
        query = gather_near(links, *query)
        query_far = links.send("y", query[0]), links.send("x", query[1])
        one = gather_high(links, jnp.concatenate([exp_low[:96], rows[6]], 0), exp_low[96:])
        one = gather_low(links, 144, one)
        kv_pieces = [v.reshape(v.shape[:4] + (1, 48, 384)) for v in kv_pieces]
    else:
        weight_local = jnp.concatenate(
            [
                jnp.sum(attention_weight * attention_weight, axis=(1, 2)),
                jnp.sum(expand_weight * expand_weight)[None],
                jnp.sum(reduce_weight * reduce_weight)[None],
            ]
        )
        turned = jnp.swapaxes(attention_weight.astype(bf16), 1, 2)
        turned = lax.all_gather(turned, "wide", axis=1, tiled=True)
        turned = lax.all_gather(turned, "narrow", axis=2, tiled=True)
        exp_all = lax.all_gather(expand_weight.astype(bf16), "wide", axis=1, tiled=True)
        exp_all = lax.all_gather(exp_all, "narrow", axis=0, tiled=True)
        red_all = lax.all_gather(reduce_weight.astype(bf16).T, "wide", axis=0, tiled=True)
        red_all = lax.all_gather(red_all, "narrow", axis=1, tiled=True)
        kv_pieces = query_pieces = [turned]
        one_pieces = [turned, exp_all]
        two_pieces = [red_all]
        one = two = (None, None)

    low, keys, values, low_mine, low_other, kv_all = project_kv(fast, word, ent, kv_pieces)
    if fast:
        query_pieces = gather_core(*query, *later(query_far, keys))
        query_pieces = [v.reshape(v.shape[:4] + (2, 48, 384)) for v in query_pieces]
        two = gather_high(links, *later((red_low[:48], red_low[48:]), keys))
        one = gather_near(links, *later(one, keys))
        one_far = links.send("y", one[0]), links.send("x", one[1])
    to_words, to_ents, q_all = project_q(fast, low, query_pieces, after=two)
    if fast:
        two = gather_low(links, 48, two)
    context, exact, lse = attend(counts, to_words, to_ents, keys, values, after=one + two)
    if fast:
        two = gather_near(links, *two, token=context)
        one_pieces = gather_core(*one, *later(one_far, two))
        two_far = links.send("y", two[0]), links.send("x", two[1])
        two_core = over("core", two[0]), over("core", two[1])
    (
        middle,
        middle_low,
        activated,
        slope,
        unit_one,
        picks,
        out_all,
        exp_all,
    ) = feed_in(fast, word, ent, context, norm_params, one_pieces, after=two)
    if fast:
        two_far = later(two_far, activated)
        two_pieces = (two[0], two_core[0], two[1], two_core[1])
        two_pieces += (two_far[0], over("core", two_far[0]), two_far[1], over("core", two_far[1]))
    word_out, ent_out, d_second, d_ffn, grads_two, red_all = feed_out(
        fast, activated, middle, norm_params, word_cotangent[0], entity_cotangent[0], two_pieces
    )
    got = red = exp = att_one = att_two = None
    if fast:
        got = over("core", grad_red(False, d_ffn, activated)[0])
    d_inner, d_first, d_out, d_context, row_inner, grads_one = feed_back(
        d_ffn, red_all, exp_all, slope, norm_params, d_second, unit_one, out_all, exact
    )
    if fast:
        red = Sum(*grad_red(True, d_ffn, activated, got, after=(d_first,)))
    exp_args = (d_inner, d_out)
    norm_args = (grads_one, grads_two)
    att_args = (counts, to_words, to_ents, keys, values, d_context, lse, row_inner)
    if fast:
        sent = grad_exp(False, picks, *exp_args, norm_args, after=(red.keep,))[0]
        got = over("core", sent)
    grads = attend_back(0, *att_args, after=(sent,) if fast else ())
    if fast:
        red.wait(grads[0]).second()
        exp = Sum(
            *grad_exp(True, picks, *exp_args, norm_args, got, after=red.keep)
        )
        sent = grad_att(0, False, low_other, grads, after=(exp.keep,))[0]
        got = over("core", sent)
    more = attend_back(3, *att_args, after=(sent,) if fast else ())
    if fast:
        red_near = red.wait(more[0]).near()
        exp.wait(more[0]).second()
        sent = grad_att(1, False, low_other, more, after=exp.keep + red_near)[0]
        got_two = over("core", sent)
        att_one = Sum(*grad_att(0, True, low_mine, grads, got, after=(sent,)))
        att_two = Sum(*grad_att(1, True, low_mine, more, got_two, after=(att_one.keep,)))
        exp_near = exp.wait(att_two.keep).near()
        near = flat(red_near + exp_near, 2)
        low_got = over("low", near[1])
    word_grad, ent_grad = grad_hidden(
        d_first, grads + more, kv_all, q_all, after=(att_two.keep,) if fast else ()
    )

    if fast:
        one_left, one_right, one_keep = att_one.wait(word_grad).parts()
        two_left, two_right, two_keep = att_two.wait(word_grad).parts()
        left_got = over("y", jnp.concatenate([one_left, two_left], 1))
        right_got = over("x", jnp.concatenate([one_right, two_right], 1))
        near = plus(near[0], later(low_got, (two_left, two_right)))
        high_got = over("high", near[1])
        left = plus(jnp.concatenate([one_keep[0], two_keep[0]], 1), left_got)
        right = plus(jnp.concatenate([one_keep[1], two_keep[1]], 1), right_got)
        got = over("low", jnp.concatenate([left[1], right[1]], 0))
        high_got = later(high_got, (left, right))
        near = near[0].astype(f32) + high_got.astype(f32)
        att_low = plus(jnp.concatenate([left[0], right[0]], 0), got).reshape(2, 2, 144, 384)
        att_low = jnp.swapaxes(att_low, 0, 1).reshape(2, 288, 384)
        red_sum = near[:192].reshape(2, 48, D)
        exp_sum = near[192:].reshape(2, 128, 384)
        norm_row = jnp.concatenate([exp_sum[1, 96, :128], jnp.pad(weight_local, (0, 119))])
        norm_rows = gather_all(norm_row)
        weight_total = jnp.sum(norm_rows[:, 128:137], axis=0)
        norm_grads = norm_rows[:, :128].reshape(8, 4, 128)[:6]
        norm_grads = jnp.swapaxes(norm_grads, 0, 1).reshape(4, D)
        first, second = att_low[0], att_low[1]
        got = over("high", jnp.where(high == 0, second, first))
        att_sum = jnp.where(high == 0, first, second).astype(f32) + got.astype(f32)
        att_sum = att_sum.reshape(2, 144, 384)
        out_rows = jnp.concatenate([exp_sum[0, 96:], exp_sum[1, 112:]], 0)
        turned = jnp.stack(
            [
                att_sum[0, 48:96],
                att_sum[1, 48:96],
                att_sum[0, 96:],
                att_sum[1, 96:],
                att_sum[0, :48],
                att_sum[1, :48],
                out_rows,
            ]
        )
        att_grad = with_layout_constraint(
            jnp.swapaxes(unpacked(turned), 1, 2), Layout((0, 1, 2))
        )
        exp_grad = jnp.concatenate([exp_sum[0, :96], exp_sum[1, :96]], 0)
        red_grad = jnp.concatenate([red_sum[0], red_sum[1]], 0)
    else:
        d_to_words, d_to_ents, d_keys, d_values = [
            jnp.concatenate([a, b], 1) for a, b in zip(grads, more)
        ]
        norm_grads = sum_all(jnp.concatenate([grads_one, grads_two], 0))
        weight_total = sum_all(weight_local)
        words, ents = low[:WORDS], low[WORDS:]
        turned = jnp.stack(
            [
                dot(d_to_words[:WORDS], words, TN),
                dot(d_to_ents[:WORDS], words, TN),
                dot(d_to_words[WORDS:], ents, TN),
                dot(d_to_ents[WORDS:], ents, TN),
                dot(d_keys, low, TN),
                dot(d_values, low, TN),
                dot(d_out, context, TN),
            ]
        ).astype(bf16)
        turned = lax.psum_scatter(turned, "wide", scatter_dimension=1, tiled=True)
        turned = lax.psum_scatter(turned, "narrow", scatter_dimension=2, tiled=True)
        att_grad = jnp.swapaxes(turned.astype(f32), 1, 2)
        grad = dot(middle_low, d_inner, TN).astype(bf16)
        grad = lax.psum_scatter(grad, "wide", scatter_dimension=1, tiled=True)
        grad = lax.psum_scatter(grad, "narrow", scatter_dimension=0, tiled=True)
        exp_grad = grad.astype(f32)
        activated = jnp.swapaxes(activated, 0, 1).reshape(ROWS, FF)
        grad = dot(d_ffn, activated, TN).astype(bf16)
        grad = lax.psum_scatter(grad, "wide", scatter_dimension=0, tiled=True)
        grad = lax.psum_scatter(grad, "narrow", scatter_dimension=1, tiled=True)
        red_grad = grad.astype(f32)

    att_first, att_second, att_update = adapt(
        attention_weight, att_grad, moment_attention, square_attention, matrix_decay
    )
    exp_first, exp_second, exp_update = adapt(
        expand_weight, exp_grad, moment_expand, square_expand, matrix_decay
    )
    red_first, red_second, red_update = adapt(
        reduce_weight.T, red_grad, moment_reduce.T, square_reduce.T, matrix_decay
    )
    update_local = jnp.concatenate(
        [
            jnp.sum(att_update * att_update, axis=(1, 2)),
            jnp.sum(exp_update * exp_update)[None],
            jnp.sum(red_update * red_update)[None],
        ]
    )
    update_total = sum_all(update_local)
    nrm_first, nrm_second, nrm_update = adapt(
        norm_params, norm_grads, moment_norms, square_norms, 0.0
    )
    weight_norm = jnp.sqrt(
        jnp.concatenate([weight_total, jnp.sum(norm_params * norm_params, axis=1)])
    )
    update_norm = jnp.sqrt(
        jnp.concatenate([update_total, jnp.sum(nrm_update * nrm_update, axis=1)])
    )
    trust = weight_norm / update_norm
    new_attention = attention_weight - learn_rate * trust[0:7, None, None] * att_update
    new_expand = expand_weight - learn_rate * trust[7] * exp_update
    new_reduce = reduce_weight - learn_rate * trust[8] * red_update.T
    new_norms = norm_params - learn_rate * trust[9:13, None] * nrm_update
    trust_stats = jnp.stack([jnp.log(weight_norm), jnp.log(update_norm), jnp.log(trust)], 1)
    return (
        word_out[None],
        ent_out[None],
        word_grad[None],
        ent_grad[None],
        new_attention,
        new_expand,
        new_reduce,
        new_norms,
        att_first,
        exp_first,
        red_first.T,
        nrm_first,
        att_second,
        exp_second,
        red_second.T,
        nrm_second,
        trust_stats,
    )


def solution(mesh):
    fast = mesh.shape["wide"] == 8 and mesh.shape["narrow"] == 4
    rows = P(("wide", "narrow"), None, None)
    matrix = P("narrow", "wide")
    stack = P(None, "narrow", "wide")
    weights = (stack, matrix, matrix, P())
    return jax.shard_map(
        functools.partial(shards, fast),
        mesh=mesh,
        in_specs=(rows, rows, P(("wide", "narrow"), None)) + weights * 3 + (rows, rows),
        out_specs=(rows,) * 4 + weights * 3 + (P(),),
        check_vma=False,
    )
```

```python
import functools

import jax
import jax.numpy as jnp
from jax import lax
from jax.experimental import pallas as pl
from jax.experimental.layout import Layout, with_layout_constraint
from jax.experimental.pallas import tpu as pltpu
from jax.sharding import PartitionSpec as P

D = 768
FF = 3072
HEADS = 12
HEAD = 64
WORDS = 512
ENTS = 128
ROWS = WORDS + ENTS
STEP = 7

eps_norm = 1e-05
adam_eps = 1e-06
matrix_decay = 0.01
learn_rate = 0.5
masked_score = -1e30

f32 = jnp.float32
bf16 = jnp.bfloat16
NN = (((1,), (0,)), ((), ()))
NT = (((1,), (1,)), ((), ()))
TN = (((0,), (0,)), ((), ()))
VMEM = pl.BlockSpec(memory_space=pltpu.VMEM)
SMEM = pl.BlockSpec(memory_space=pltpu.SMEM)
ANY = pl.BlockSpec(memory_space=pl.ANY)
HBM = pl.BlockSpec(memory_space=pltpu.HBM)
COST_RATE = 4e9
PARAMS = pltpu.CompilerParams(vmem_limit_bytes=12 * 2**20)
WIDE = pltpu.CompilerParams(vmem_limit_bytes=28 * 2**20)


def dot(left, right, dims):
    return lax.dot_general(left, right, dims, preferred_element_type=f32)


def shape(dims, dtype):
    return jax.ShapeDtypeStruct(dims, dtype)


def kept(dims, dtype):
    return pltpu.VMEM(dims, dtype)


def stored(dims, dtype):
    return pltpu.HBM(dims, dtype)


def tokens(values):
    return [v for v in values if v is not None]


def cost(us, rate=COST_RATE):
    return pl.CostEstimate(flops=int(us * rate), bytes_accessed=0, transcendentals=0)


def away_blocks():
    for core in range(2):
        for outer in range(2):
            for lead in range(2):
                for low in range(2):
                    for high in range(2):
                        yield core, outer, lead, low, high


def places(wide, narrow, second, block):
    core, outer, lead, low, high = block
    x_away, y_away = (outer, lead) if second else (lead, outer)
    w = wide ^ (high * 4 + low * 2 + y_away)
    n = narrow ^ (x_away * 2 + core)
    return w, n


def piece_of(bufs, block):
    core, outer, lead, low, high = block
    return bufs[core].at[outer, lead, low, high]


def coords():
    return lax.axis_index("wide"), lax.axis_index("narrow")


def start_attention(bufs, second, target, slots, sem):
    wide, narrow = coords()
    for block in away_blocks():
        w, n = places(wide, narrow, second, block)
        row = pl.multiple_of(w * 96 + (n % 2) * 48, 16)
        lane = pl.multiple_of((n // 2) * 384, 128)
        src = piece_of(bufs, block)
        pltpu.make_async_copy(src, target.at[slots, pl.ds(row, 48), pl.ds(lane, 384)], sem).start()


def drain(ref, sem):
    pltpu.make_async_copy(ref, ref, sem).wait()


def prep_kernel(att, exp, red, keep, send, exp_low, red_low, sums):
    narrow = lax.axis_index("narrow")
    core = narrow % 2
    total = []
    for i in range(7):
        value = att[i]
        total.append(jnp.sum(value * value))
        turned = value.T.astype(bf16)
        halves = turned.reshape(2, 48, 192)

        @pl.when(core == 0)
        def _():
            keep[i] = halves[0]
            send[i] = halves[1]

        @pl.when(core == 1)
        def _():
            keep[i] = halves[1]
            send[i] = halves[0]

    value = exp[...]
    total.append(jnp.sum(value * value))
    exp_low[...] = value.astype(bf16)
    value = red[...]
    total.append(jnp.sum(value * value))
    red_low[...] = value.astype(bf16)
    for i in range(9):
        sums[i] = total[i]


def prep(att, exp, red):
    return pl.pallas_call(
        prep_kernel,
        in_specs=[VMEM] * 3,
        out_specs=[VMEM] * 4 + [SMEM],
        out_shape=[
            shape((7, 48, 192), bf16),
            shape((7, 48, 192), bf16),
            shape((192, 384), bf16),
            shape((96, D), bf16),
            shape((9,), f32),
        ],
        compiler_params=pltpu.CompilerParams(vmem_limit_bytes=60 * 2**20),
        name="prep",
    )(att, exp, red)


def pick_rows(source, mine, other):
    core = lax.axis_index("narrow") % 2
    for c in range(2):

        @pl.when(core == c)
        def _():
            for target, at in ((mine, c * 192), (other, 192 - c * 192)):
                target[:, :192] = source[:, at : at + 192]
                target[:, 192:] = source[:, at + 384 : at + 576]


def pick_tiles(source, mine, other):
    core = lax.axis_index("narrow") % 2
    for c in range(2):

        @pl.when(core == c)
        def _():
            for target, at in ((mine, c * 192), (other, 192 - c * 192)):
                target[:, :128] = source[:, at : at + 128]
                target[:, 128:256] = source[:, at + 384 : at + 512]
                target[:, 256:320] = source[:, at + 128 : at + 192]
                target[:, 320:] = source[:, at + 512 : at + 576]


def project_kv_kernel(fast, n_after, word, ent, *refs):
    if fast:
        first, second, refs = refs[:2], refs[2:4], refs[4:]
    else:
        whole, refs = refs[0], refs[1:]
    low, keys, values, mine, other, saved, target, sem, sem_save = refs[n_after:]
    if fast:
        start_attention(first, False, target, pl.ds(0, 1), sem)
        start_attention(second, True, target, pl.ds(1, 1), sem)
    else:
        pltpu.make_async_copy(whole.at[pl.ds(4, 2)], target, sem).start()
    low[:WORDS] = word[...].astype(bf16)
    low[WORDS:] = ent[...].astype(bf16)
    pick_tiles(low, mine, other)
    drain(target, sem)
    save = pltpu.make_async_copy(target, saved, sem_save)
    save.start()
    keys[...] = dot(low[...], target[0], NT).astype(bf16)
    values[...] = dot(low[...], target[1], NT).astype(bf16)
    save.wait()


def project_kv(fast, word, ent, pieces, after=()):
    after = tokens(after)
    return pl.pallas_call(
        functools.partial(project_kv_kernel, fast, len(after)),
        in_specs=[VMEM, VMEM] + [ANY] * (len(pieces) + len(after)),
        out_specs=[VMEM] * 5 + [HBM],
        out_shape=[kept((ROWS, D), bf16)] * 3
        + [stored((ROWS, D // 2), bf16)] * 2
        + [stored((2, D, D), bf16)],
        scratch_shapes=[
            pltpu.VMEM((2, D, D), bf16),
            pltpu.SemaphoreType.DMA,
            pltpu.SemaphoreType.DMA,
        ],
        compiler_params=PARAMS,
        cost_estimate=cost(6, 4e8),
        name="project_kv",
    )(word, ent, *pieces, *after)


def project_q_kernel(fast, n_after, low, *refs):
    if fast:
        first, second, refs = refs[:2], refs[2:4], refs[4:]
    else:
        whole, refs = refs[0], refs[1:]
    to_words, to_ents, saved, target, sem, sem_save = refs[n_after:]
    if fast:
        start_attention(first, False, target, pl.ds(0, 2), sem)
        start_attention(second, True, target, pl.ds(2, 2), sem)
    else:
        for slot, k in enumerate((0, 2, 1, 3)):
            pltpu.make_async_copy(whole.at[k], target.at[slot], sem).start()
    drain(target, sem)
    save = pltpu.make_async_copy(target, saved, sem_save)
    save.start()
    scale = HEAD ** (-0.5)
    word = low[:WORDS]
    ent = low[WORDS:]
    to_words[:WORDS] = (dot(word, target[0], NT) * scale).astype(bf16)
    to_words[WORDS:] = (dot(ent, target[1], NT) * scale).astype(bf16)
    to_ents[:WORDS] = (dot(word, target[2], NT) * scale).astype(bf16)
    to_ents[WORDS:] = (dot(ent, target[3], NT) * scale).astype(bf16)
    save.wait()


def project_q(fast, low, pieces, after=()):
    after = tokens(after)
    return pl.pallas_call(
        functools.partial(project_q_kernel, fast, len(after)),
        in_specs=[VMEM] + [ANY] * (len(pieces) + len(after)),
        out_specs=[VMEM] * 2 + [HBM],
        out_shape=[kept((ROWS, D), bf16)] * 2 + [stored((4, D, D), bf16)],
        scratch_shapes=[
            pltpu.VMEM((4, D, D), bf16),
            pltpu.SemaphoreType.DMA,
            pltpu.SemaphoreType.DMA,
        ],
        compiler_params=PARAMS,
        cost_estimate=cost(7, 4e8),
        name="project_q",
    )(low, *pieces, *after)


def head_masks(counts):
    lane = lax.broadcasted_iota(jnp.int32, (ROWS, 128), 1)
    row = lax.broadcasted_iota(jnp.int32, (ROWS, 128), 0)
    edge = jnp.where(row < WORDS, counts[0], counts[1] + WORDS)
    bias = jnp.where(row < edge, 0.0, masked_score)
    out = []
    for h in range(2):
        own = jnp.where((lane < HEAD) if h == 0 else (lane >= HEAD), 1.0, 0.0).astype(bf16)
        mark = jnp.where(lane == (HEAD if h == 0 else 0), 1.0, 0.0)
        rest = (1.0 - mark).astype(bf16)
        tag = (bias * mark).astype(bf16)
        out.append((own, mark.astype(bf16), rest, tag))
    return out


def scores_of(masks, keys, to_words, to_ents):
    own, mark, rest, tag = masks
    tagged = keys * own + tag
    upper = dot(tagged[:WORDS], to_words * rest + mark, NT)
    lower = dot(tagged[WORDS:], to_ents * rest + mark, NT)
    return jnp.concatenate([upper, lower], 0)


def attend_kernel(n_after, counts, to_words, to_ents, keys, values, *refs):
    context, exact, lse = refs[n_after:]
    masks = head_masks(counts)
    pair = pl.program_id(0)
    lanes = pl.ds(pl.multiple_of(pair * 128, 128), 128)
    key, value = keys[:, lanes], values[:, lanes]
    outs = []
    for h in range(2):
        scores = scores_of(masks[h], key, to_words[:, lanes], to_ents[:, lanes])
        top = jnp.max(scores, axis=0, keepdims=True)
        expd = jnp.exp(scores - top)
        total = jnp.sum(expd, axis=0, keepdims=True)
        lse[pair, h : h + 1, :] = top + jnp.log(total)
        mixed = dot(value[:, h * HEAD : (h + 1) * HEAD], expd.astype(bf16), TN)
        outs.append(mixed * (1.0 / total))
    joined = jnp.concatenate(outs, 0).T
    exact[...] = joined
    context[:, lanes] = joined.astype(bf16)


def attend(counts, to_words, to_ents, keys, values, after=()):
    after = tokens(after)
    return pl.pallas_call(
        functools.partial(attend_kernel, len(after)),
        grid=(HEADS // 2,),
        in_specs=[SMEM] + [VMEM] * 4 + [ANY] * len(after),
        out_specs=[VMEM, pl.BlockSpec((ROWS, 128), lambda i: (0, i)), VMEM],
        out_shape=[
            kept((ROWS, D), bf16),
            stored((ROWS, D), f32),
            kept((HEADS // 2, 2, ROWS), f32),
        ],
        compiler_params=PARAMS,
        cost_estimate=cost(12, 4e8),
        name="attend",
    )(counts, to_words, to_ents, keys, values, *after)


def normed(value):
    center = value - jnp.mean(value, axis=-1, keepdims=True)
    spread = jnp.mean(center * center, axis=-1, keepdims=True)
    inverse = lax.rsqrt(spread + eps_norm)
    return center * inverse, inverse


def normed_back(unit, inverse, cotangent):
    mean = jnp.mean(cotangent, axis=-1, keepdims=True)
    inner = jnp.mean(cotangent * unit, axis=-1, keepdims=True)
    return inverse * (cotangent - mean - unit * inner)


def column_sum(value):
    return jnp.sum(value, axis=0, keepdims=True)


def feed_in_kernel(fast, n_after, word, ent, context, norms, *refs):
    if fast:
        bufs, refs = (refs[0:2], refs[2:4]), refs[4:]
    else:
        bufs, refs = refs[0:2], refs[2:]
    (
        middle_saved,
        middle_low,
        act_saved,
        slope_saved,
        unit_saved,
        picks_saved,
        out_saved,
        exp_saved,
        middle,
        activated,
        slope,
        unit_here,
        picks,
        out_all,
        exp_all,
        sem_out,
        sem_exp,
        sem_save,
    ) = refs[n_after:]
    step = pl.program_id(0)
    pairs = (
        (unit_here, unit_saved),
        (picks, picks_saved),
        (out_all, out_saved),
        (middle, middle_saved),
    )
    saves = [pltpu.make_async_copy(*pair, sem_save.at[i]) for i, pair in enumerate(pairs)]

    @pl.when(step == 0)
    def _():
        if fast:
            start_feed_in(bufs, out_all, exp_all, sem_out, sem_exp)
        else:
            pltpu.make_async_copy(bufs[0].at[6], out_all, sem_out).start()
            for j in range(4):
                cols = pl.ds(j * D, D)
                pltpu.make_async_copy(bufs[1].at[:, cols], exp_all.at[j], sem_exp.at[j]).start()
        drain(out_all, sem_out)
        saves[2].start()
        hidden = jnp.concatenate([word[...], ent[...]], 0)
        unit, inverse = normed(hidden + dot(context[...], out_all[...], NT))
        value = unit * norms[0:1, :] + norms[1:2, :]
        unit_here[:, :D] = unit
        unit_here[:, D:] = jnp.broadcast_to(inverse, (ROWS, 128))
        saves[0].start()
        middle_low[...] = value.astype(bf16)
        middle[...] = value
        saves[3].start()
        pick_rows(middle_low, picks.at[0], picks.at[1])
        pick_tiles(context, picks.at[2], picks.at[3])
        saves[1].start()

    drain(exp_all.at[step], sem_exp.at[step])
    pltpu.make_async_copy(exp_all.at[step], exp_saved.at[step], sem_save.at[4 + step]).start()
    inner = dot(middle_low[...], exp_all[step], NN)
    share = 0.5 + 0.5 * lax.erf(inner * 0.7071067811865476)
    bell = jnp.exp(-0.5 * inner * inner) * 0.3989422804014327
    slope[step] = (share + inner * bell).astype(bf16)
    activated[step] = (inner * share).astype(bf16)
    pltpu.make_async_copy(slope.at[step], slope_saved.at[step], sem_save.at[8 + step]).start()
    pltpu.make_async_copy(activated.at[step], act_saved.at[step], sem_save.at[12 + step]).start()

    @pl.when(step == 3)
    def _():
        for save in saves:
            save.wait()
        for j in range(4):
            pltpu.make_async_copy(exp_all.at[j], exp_saved.at[j], sem_save.at[4 + j]).wait()
            pltpu.make_async_copy(slope.at[j], slope_saved.at[j], sem_save.at[8 + j]).wait()
            pltpu.make_async_copy(activated.at[j], act_saved.at[j], sem_save.at[12 + j]).wait()


def start_feed_in(bufs, out_all, exp_all, sem_out, sem_exp):
    wide, narrow = coords()
    for half in range(2):
        skip, count = ((0, 32), (32, 16))[half]
        for block in away_blocks():
            w, n = places(wide, narrow, half == 1, block)
            row = pl.multiple_of(w * 96 + (n % 2) * 48 + skip, 16)
            lane = pl.multiple_of((n // 2) * 384, 128)
            src = piece_of(bufs[half], block).at[pl.ds(96, count)]
            dst = out_all.at[pl.ds(row, count), pl.ds(lane, 384)]
            pltpu.make_async_copy(src, dst, sem_out).start()
    for half in range(2):
        for block in away_blocks():
            w, n = places(wide, narrow, half == 1, block)
            src = piece_of(bufs[half], block).at[pl.ds(0, 96)]
            row = pl.multiple_of(n * 192 + half * 96, 16)
            lane = pl.multiple_of((w % 2) * 384, 128)
            dst = exp_all.at[w // 2, pl.ds(row, 96), pl.ds(lane, 384)]
            pltpu.make_async_copy(src, dst, sem_exp.at[w // 2]).start()


def feed_in(fast, word, ent, context, norms, pieces, after=()):
    after = tokens(after)
    return pl.pallas_call(
        functools.partial(feed_in_kernel, fast, len(after)),
        grid=(4,),
        in_specs=[VMEM] * 4 + [ANY] * (len(pieces) + len(after)),
        out_specs=[HBM, VMEM] + [HBM] * 6,
        out_shape=[
            stored((ROWS, D), f32),
            kept((ROWS, D), bf16),
            stored((4, ROWS, D), bf16),
            stored((4, ROWS, D), bf16),
            stored((ROWS, D + 128), f32),
            stored((4, ROWS, D // 2), bf16),
            stored((D, D), bf16),
            stored((4, D, D), bf16),
        ],
        scratch_shapes=[
            pltpu.VMEM((ROWS, D), f32),
            pltpu.VMEM((4, ROWS, D), bf16),
            pltpu.VMEM((4, ROWS, D), bf16),
            pltpu.VMEM((ROWS, D + 128), f32),
            pltpu.VMEM((4, ROWS, D // 2), bf16),
            pltpu.VMEM((D, D), bf16),
            pltpu.VMEM((4, D, D), bf16),
            pltpu.SemaphoreType.DMA,
            pltpu.SemaphoreType.DMA((4,)),
            pltpu.SemaphoreType.DMA((16,)),
        ],
        compiler_params=pltpu.CompilerParams(vmem_limit_bytes=28 * 2**20),
        cost_estimate=cost(0),
        name="feed_in",
    )(word, ent, context, norms, *pieces, *after)


def feed_out_kernel(fast, n_after, norms, activated, middle, word_cot, ent_cot, *refs):
    if fast:
        bufs, refs = (refs[0:2], refs[2:4], refs[4:6], refs[6:8]), refs[8:]
    else:
        bufs, refs = refs[0:1], refs[1:]
    (
        word_out,
        ent_out,
        second_saved,
        d_ffn,
        grads_two,
        red_saved,
        total,
        cot_here,
        middle_here,
        d_second,
        act_here,
        red_all,
        sem_red,
        sem_act,
        sem_save,
        sem_late,
    ) = refs[n_after:]
    step = pl.program_id(0)
    upper, lower = pl.ds(0, WORDS), pl.ds(WORDS, ENTS)
    late = (
        pltpu.make_async_copy(word_cot, cot_here.at[upper], sem_late.at[0]),
        pltpu.make_async_copy(ent_cot, cot_here.at[lower], sem_late.at[1]),
        pltpu.make_async_copy(middle, middle_here, sem_late.at[2]),
    )
    saves = (
        pltpu.make_async_copy(total.at[upper], word_out, sem_save.at[0]),
        pltpu.make_async_copy(total.at[lower], ent_out, sem_save.at[1]),
        pltpu.make_async_copy(d_second, second_saved, sem_save.at[2]),
    )

    @pl.when(step == 0)
    def _():
        for j in range(4):
            pltpu.make_async_copy(activated.at[j], act_here.at[j], sem_act.at[j]).start()
        if fast:
            start_feed_out(bufs, red_all, sem_red)
        else:
            for j in range(4):
                cols = pl.ds(j * D, D)
                pltpu.make_async_copy(bufs[0].at[:, cols], red_all.at[j], sem_red.at[j]).start()
        for copy in late:
            copy.start()

    drain(act_here.at[step], sem_act.at[step])
    drain(red_all.at[step], sem_red.at[step])
    pltpu.make_async_copy(red_all.at[step], red_saved.at[step], sem_save.at[3 + step]).start()
    part = dot(act_here[step], red_all[step], NT)

    @pl.when(step == 0)
    def _():
        total[...] = part

    @pl.when(step > 0)
    def _():
        total[...] += part

    @pl.when(step == 3)
    def _():
        for copy in late:
            copy.wait()
        unit, inverse = normed(total[...] + middle_here[...])
        total[...] = unit * norms[2:3, :] + norms[3:4, :]
        saves[0].start()
        saves[1].start()
        cot = cot_here[...]
        back = normed_back(unit, inverse, cot * norms[2:3, :])
        d_second[...] = back
        saves[2].start()
        d_ffn[...] = back.astype(bf16)
        grads_two[0:1, :] = column_sum(cot * unit)
        grads_two[1:2, :] = column_sum(cot)
        for save in saves:
            save.wait()
        for j in range(4):
            pltpu.make_async_copy(red_all.at[j], red_saved.at[j], sem_save.at[3 + j]).wait()


def start_feed_out(bufs, red_all, sem_red):
    wide, narrow = coords()
    for half in range(2):
        for block in away_blocks():
            w, n = places(wide, narrow, half == 1, block)
            core, outer, lead, low, high = block
            src = bufs[half + 2 * outer][core].at[lead, low, high]
            row = pl.multiple_of(w * 96 + half * 48, 16)
            pltpu.make_async_copy(src, red_all.at[n, pl.ds(row, 48)], sem_red.at[n]).start()


def feed_out(fast, activated, middle, norms, word_cot, ent_cot, pieces, after=()):
    after = tokens(after)
    return pl.pallas_call(
        functools.partial(feed_out_kernel, fast, len(after)),
        grid=(4,),
        in_specs=[VMEM] + [HBM] * 4 + [ANY] * (len(pieces) + len(after)),
        out_specs=[HBM] * 3 + [VMEM] * 2 + [HBM],
        out_shape=[
            stored((WORDS, D), f32),
            stored((ENTS, D), f32),
            stored((ROWS, D), f32),
            kept((ROWS, D), bf16),
            kept((2, D), f32),
            stored((4, D, D), bf16),
        ],
        scratch_shapes=[
            pltpu.VMEM((ROWS, D), f32),
            pltpu.VMEM((ROWS, D), f32),
            pltpu.VMEM((ROWS, D), f32),
            pltpu.VMEM((ROWS, D), f32),
            pltpu.VMEM((4, ROWS, D), bf16),
            pltpu.VMEM((4, D, D), bf16),
            pltpu.SemaphoreType.DMA((4,)),
            pltpu.SemaphoreType.DMA((4,)),
            pltpu.SemaphoreType.DMA((7,)),
            pltpu.SemaphoreType.DMA((3,)),
        ],
        compiler_params=pltpu.CompilerParams(vmem_limit_bytes=56 * 2**20),
        cost_estimate=cost(12),
        name="feed_out",
    )(norms, activated, middle, word_cot, ent_cot, *pieces, *after)


def feed_back_kernel(
    n_after, d_ffn, norms, red_all, exp_all, slope, d_second, unit_one, out_all, exact, *refs
):
    (
        d_inner,
        d_first,
        d_out,
        d_context,
        row_inner,
        grads_one,
        total,
        red_here,
        exp_here,
        slope_here,
        second_here,
        unit_here,
        out_here,
        exact_here,
        sem_step,
        sem_late,
        sem_save,
    ) = refs[n_after:]
    step = pl.program_id(0)
    pairs = (
        (d_second, second_here),
        (unit_one, unit_here),
        (out_all, out_here),
        (exact, exact_here),
    )
    late = [pltpu.make_async_copy(*pair, sem_late.at[i]) for i, pair in enumerate(pairs)]
    save = pltpu.make_async_copy(total, d_first, sem_save)
    parts = ((red_all, red_here), (slope, slope_here), (exp_all, exp_here))

    @pl.when(step == 0)
    def _():
        for j in range(4):
            for k, (there, here) in enumerate(parts):
                pltpu.make_async_copy(there.at[j], here.at[j], sem_step.at[k, j]).start()
        for copy in late:
            copy.start()

    drain(red_here.at[step], sem_step.at[0, step])
    drain(slope_here.at[step], sem_step.at[1, step])
    drain(exp_here.at[step], sem_step.at[2, step])
    lanes = pl.ds(pl.multiple_of(step * D, D), D)
    back = (dot(d_ffn[...], red_here[step], NN) * slope_here[step].astype(f32)).astype(bf16)
    d_inner[:, lanes] = back
    part = dot(back, exp_here[step], NT)

    @pl.when(step == 0)
    def _():
        total[...] = part

    @pl.when(step > 0)
    def _():
        total[...] += part

    @pl.when(step == 3)
    def _():
        for copy in late:
            copy.wait()
        d_middle = total[...] + second_here[...]
        unit = unit_here[:, :D]
        grads_one[0:1, :] = column_sum(d_middle * unit)
        grads_one[1:2, :] = column_sum(d_middle)
        first = normed_back(unit, unit_here[:, D : D + 1], d_middle * norms[0:1, :])
        total[...] = first
        save.start()
        low_first = first.astype(bf16)
        d_out[...] = low_first
        context = dot(low_first, out_here[...], NN).astype(bf16)
        d_context[...] = context
        product = context.astype(f32) * exact_here[...]
        head = lax.broadcasted_iota(jnp.int32, (16, D), 1) // HEAD
        pick = jnp.where(head == lax.broadcasted_iota(jnp.int32, (16, D), 0), 1.0, 0.0).astype(bf16)
        high = product.astype(bf16)
        low = (product - high.astype(f32)).astype(bf16)
        sums = dot(pick, high, NT) + dot(pick, low, NT)
        for i in range(HEADS // 2):
            row_inner[i] = sums[2 * i : 2 * i + 2]
        save.wait()


def feed_back(d_ffn, red_all, exp_all, slope, norms, d_second, unit_one, out_all, exact, after=()):
    after = tokens(after)
    return pl.pallas_call(
        functools.partial(feed_back_kernel, len(after)),
        grid=(4,),
        in_specs=[VMEM, VMEM] + [HBM] * 7 + [ANY] * len(after),
        out_specs=[VMEM, HBM] + [VMEM] * 4,
        out_shape=[
            kept((ROWS, FF), bf16),
            stored((ROWS, D), f32),
            kept((ROWS, D), bf16),
            kept((ROWS, D), bf16),
            kept((HEADS // 2, 2, ROWS), f32),
            kept((2, D), f32),
        ],
        scratch_shapes=[
            pltpu.VMEM((ROWS, D), f32),
            pltpu.VMEM((4, D, D), bf16),
            pltpu.VMEM((4, D, D), bf16),
            pltpu.VMEM((4, ROWS, D), bf16),
            pltpu.VMEM((ROWS, D), f32),
            pltpu.VMEM((ROWS, D + 128), f32),
            pltpu.VMEM((D, D), bf16),
            pltpu.VMEM((ROWS, D), f32),
            pltpu.SemaphoreType.DMA((3, 4)),
            pltpu.SemaphoreType.DMA((4,)),
            pltpu.SemaphoreType.DMA,
        ],
        compiler_params=pltpu.CompilerParams(vmem_limit_bytes=36 * 2**20),
        cost_estimate=cost(14),
        name="feed_back",
    )(d_ffn, norms, red_all, exp_all, slope, d_second, unit_one, out_all, exact, *after)


def attend_back_kernel(
    first, n_after, counts, to_words, to_ents, keys, values, d_context, lse, row_inner, *refs
):
    d_to_words, d_to_ents, d_keys, d_values = refs[n_after:]
    masks = head_masks(counts)
    scale = HEAD ** (-0.5)
    step = pl.program_id(0)
    pair = step + first
    lanes = pl.ds(pl.multiple_of(pair * 128, 128), 128)
    here = pl.ds(pl.multiple_of(step * 128, 128), 128)
    word_query, ent_query = to_words[...], to_ents[...]
    key, value, d_mixed = keys[...], values[...], d_context[:, lanes]
    one, two, three, four = [], [], [], []
    for h in range(2):
        cols = slice(h * HEAD, (h + 1) * HEAD)
        scores = scores_of(masks[h], key, word_query, ent_query)
        probs = jnp.exp(scores - lse[pair, h : h + 1, :])
        d_probs = dot(value * masks[h][0], d_mixed, NT)
        d_scores = (probs * (d_probs - row_inner[pair, h : h + 1, :])).astype(bf16)
        one.append(dot(key[:WORDS, cols], d_scores[:WORDS], TN))
        two.append(dot(key[WORDS:, cols], d_scores[WORDS:], TN))
        three.append(
            jnp.concatenate(
                [
                    dot(d_scores[:WORDS], word_query[:, cols], NN),
                    dot(d_scores[WORDS:], ent_query[:, cols], NN),
                ],
                0,
            )
        )
        four.append(dot(probs.astype(bf16), d_mixed[:, cols], NN))
    d_to_words[:, here] = (jnp.concatenate(one, 0).T * scale).astype(bf16)
    d_to_ents[:, here] = (jnp.concatenate(two, 0).T * scale).astype(bf16)
    d_keys[:, here] = jnp.concatenate(three, 1).astype(bf16)
    d_values[:, here] = jnp.concatenate(four, 1).astype(bf16)


def attend_back(first, counts, to_words, to_ents, keys, values, d_context, lse, row_inner, after=()):
    after = tokens(after)
    pair = pl.BlockSpec((ROWS, 128), lambda i: (0, i + first))
    return pl.pallas_call(
        functools.partial(attend_back_kernel, first, len(after)),
        grid=(HEADS // 4,),
        in_specs=[SMEM] + [pair] * 4 + [VMEM] * 3 + [ANY] * len(after),
        out_specs=[VMEM] * 4,
        out_shape=[kept((ROWS, D // 2), bf16)] * 4,
        compiler_params=PARAMS,
        cost_estimate=cost(10),
        name="attend_back",
    )(counts, to_words, to_ents, keys, values, d_context, lse, row_inner, *after)


def relative():
    for x in range(2):
        for y in range(2):
            for low in range(2):
                for high in range(2):
                    yield x, y, low, high


def emit(mine, got, outs, half, first, rest, rows, value):
    if not mine:
        outs[0][(half, first) + rest + (rows,)] = value.astype(bf16)
        return
    value = (value + got[(half, first) + rest + (rows,)].astype(f32)).astype(bf16)
    if first:
        outs[half][rest + (rows,)] = value
    else:
        outs[2][(half,) + rest + (rows,)] = value


def grad_call(kernel, name, mine, operands, got, steps, dims, extra, after, specs=(), limit=12):
    after = tokens(after)
    if mine:
        outs = [kept((2,) + dims, bf16)] * 2 + [kept((2, 2) + dims, bf16)]
        operands = list(operands) + [got]
    else:
        outs = [kept((2, 2, 2) + dims, bf16)]
    return pl.pallas_call(
        functools.partial(kernel, mine, len(after), len(outs)),
        grid=(steps,),
        in_specs=list(specs)
        + [VMEM] * (len(operands) - len(specs))
        + [ANY] * len(after),
        out_specs=[VMEM] * len(outs),
        out_shape=outs,
        scratch_shapes=extra,
        compiler_params=pltpu.CompilerParams(vmem_limit_bytes=limit * 2**20),
        cost_estimate=cost(7),
        name=name,
    )(*operands, *after)


def split_refs(mine, n_after, n_outs, refs):
    got, refs = (refs[0], refs[1:]) if mine else (None, refs)
    refs = refs[n_after:]
    return got, refs[:n_outs], refs[n_outs:]


def grad_red_kernel(mine, n_after, n_outs, d_ffn, activated, *refs):
    got, outs, (whole, act, sem) = split_refs(mine, n_after, n_outs, refs)
    wide, narrow = coords()
    for x in range(2):
        n = narrow ^ (x * 2 + (0 if mine else 1))
        pltpu.make_async_copy(activated.at[n], act.at[x], sem.at[x]).start()
    for x in range(2):
        drain(act.at[x], sem.at[x])
        whole[...] = dot(d_ffn[...], act[x], TN)
        for y in range(2):
            for low in range(2):
                for high in range(2):
                    w = wide ^ (high * 4 + low * 2 + y)
                    for half in range(2):
                        rows = pl.ds(pl.multiple_of(w * 96 + half * 48, 16), 48)
                        first, second = (x, y) if half == 0 else (y, x)
                        rest = (second, low, high)
                        emit(mine, got, outs, half, first, rest, slice(0, 48), whole[rows, :])


def grad_red(mine, d_ffn, activated, got=None, after=()):
    scratch = [
        pltpu.VMEM((D, D), f32),
        pltpu.VMEM((2, ROWS, D), bf16),
        pltpu.SemaphoreType.DMA((2,)),
    ]
    operands, specs = (d_ffn, activated), [VMEM, HBM]
    return grad_call(
        grad_red_kernel, "grad_red", mine, operands, got, 1, (2, 2, 48, D), scratch, after, specs, 24
    )


def grad_exp_kernel(
    mine, n_after, n_outs, picks, d_inner, d_out, norms_one, norms_two, *refs
):
    got, outs, (whole, turned, norms, middle, context, sem) = split_refs(
        mine, n_after, n_outs, refs
    )
    wide, narrow = coords()
    step = pl.program_id(0)

    @pl.when(step == 0)
    def _():
        at = 0 if mine else 1
        pltpu.make_async_copy(picks.at[at], middle, sem.at[0]).start()
        pltpu.make_async_copy(picks.at[at + 2], context, sem.at[1]).start()
        drain(middle, sem.at[0])
        drain(context, sem.at[1])
        norms[0:2] = norms_one[...]
        norms[2:4] = norms_two[...]
        turned[...] = dot(d_out[...], context[...], TN)

    z = (wide // 2) ^ step
    whole[...] = dot(middle[...], d_inner[:, pl.ds(pl.multiple_of(z * D, D), D)], TN)
    low, high = step % 2, step // 2
    for y in range(2):
        w = wide ^ (step * 2 + y)
        lanes = pl.ds(pl.multiple_of((w % 2) * 384, 128), 384)
        blocks = packed(turned, w * 96, narrow)
        norm_lanes = pl.ds(pl.multiple_of(jnp.minimum(w, 5) * 128, 128), 128)
        for x in range(2):
            n = narrow ^ (x * 2 + (0 if mine else 1))
            for half in range(2):
                rows = pl.ds(pl.multiple_of((n // 2) * 192 + half * 96, 16), 96)
                first, second = (x, y) if half == 0 else (y, x)
                rest = (second, low, high)
                emit(mine, got, outs, half, first, rest, slice(0, 96), whole[rows, lanes])
            here = lax.broadcasted_iota(jnp.int32, (8, 128), 0) == n
            norm = jnp.sum(jnp.where(here, norms[:, norm_lanes], 0.0), axis=0, keepdims=True)
            norm = jnp.broadcast_to(norm, (16, 128))
            norm = jnp.concatenate([norm] * 3, 1)
            lower = jnp.concatenate([norm, blocks[x][32:]], 0)
            emit(mine, got, outs, 0, x, (y, low, high), slice(96, 128), blocks[x][:32])
            emit(mine, got, outs, 1, y, (x, low, high), slice(96, 128), lower)


def packed(turned, start, narrow):
    upper = pl.ds(pl.multiple_of(start, 16), 48)
    lower = pl.ds(pl.multiple_of(start + 48, 16), 48)
    tail_upper = turned[upper, 256:]
    tail_lower = turned[lower, 256:]
    tails = (
        jnp.concatenate([tail_upper[:, :64], tail_lower[:, :64]], 1),
        jnp.concatenate([tail_upper[:, 64:], tail_lower[:, 64:]], 1),
    )
    x_own = narrow // 2
    out = []
    for x in range(2):
        lanes = pl.ds(pl.multiple_of((x_own ^ x) * 128, 128), 128)
        tail = jnp.where(x_own == x, tails[0], tails[1])
        out.append(jnp.concatenate([turned[upper, lanes], turned[lower, lanes], tail], 1))
    return out


def unpacked(block):
    upper = jnp.concatenate([block[..., :128], block[..., 256:320]], -1)
    lower = jnp.concatenate([block[..., 128:256], block[..., 320:]], -1)
    return jnp.concatenate([upper, lower], -2)


def grad_exp(mine, picks, d_inner, d_out, norms, got=None, after=()):
    operands, specs = (picks, d_inner, d_out) + norms, [HBM]
    scratch = [
        pltpu.VMEM((384, D), f32),
        pltpu.VMEM((D, 384), f32),
        pltpu.VMEM((8, D), f32),
        pltpu.VMEM((ROWS, D // 2), bf16),
        pltpu.VMEM((ROWS, D // 2), bf16),
        pltpu.SemaphoreType.DMA((2,)),
    ]
    return grad_call(
        grad_exp_kernel, "grad_exp", mine, operands, got, 4, (2, 2, 128, 384), scratch, after, specs
    )


def grad_att_kernel(
    part, mine, n_after, n_outs, picked, d_to_words, d_to_ents, d_keys, d_values, *refs
):
    got, outs, (turned,) = split_refs(mine, n_after, n_outs, refs)
    wide, narrow = coords()
    work = (
        (d_keys, slice(0, ROWS), 0, 0),
        (d_to_words, slice(0, WORDS), 0, 1),
        (d_to_words, slice(WORDS, ROWS), 0, 2),
        (d_values, slice(0, ROWS), 1, 0),
        (d_to_ents, slice(0, WORDS), 1, 1),
        (d_to_ents, slice(WORDS, ROWS), 1, 2),
    )
    for ref, rows, half, at in work:
        turned[...] = dot(ref[rows, :], picked[rows, :], TN)
        for y in range(2):
            for low in range(2):
                w = (wide % 4) ^ (low * 2 + y)
                blocks = packed(turned, w * 96, narrow)
                for x in range(2):
                    first, second = (x, y) if half == 0 else (y, x)
                    where = slice(at * 48, at * 48 + 48)
                    emit(mine, got, outs, half, first, (second, low), where, blocks[x])


def grad_att(part, mine, picked, grads, got=None, after=()):
    kernel = functools.partial(grad_att_kernel, part)
    operands = (picked,) + tuple(grads)
    scratch = [pltpu.VMEM((D // 2, 384), f32)]
    return grad_call(
        kernel, "grad_att", mine, operands, got, 1, (2, 144, 384), scratch, after
    )


def grad_hidden_kernel(n_after, kv, q, *refs):
    grads, d_first = refs[:8], refs[8]
    word, ent, joined, first_here, sem = refs[9 + n_after :]
    step = pl.program_id(0)
    upper, lower = slice(0, WORDS), slice(WORDS, ROWS)
    late = pltpu.make_async_copy(d_first, first_here, sem)

    def both(kind):
        joined[:, : D // 2] = grads[kind][...]
        joined[:, D // 2 :] = grads[4 + kind][...]

    @pl.when(step == 0)
    def _():
        late.start()
        both(2)
        word[...] = dot(joined[upper], kv[...], NN)
        ent[...] = dot(joined[lower], kv[...], NN)

    @pl.when(step == 1)
    def _():
        both(3)
        word[...] += dot(joined[upper], kv[...], NN)
        ent[...] += dot(joined[lower], kv[...], NN)

    @pl.when(step == 2)
    def _():
        both(0)
        word[...] += dot(joined[upper], q[...], NN)

    @pl.when(step == 3)
    def _():
        ent[...] += dot(joined[lower], q[...], NN)

    @pl.when(step == 4)
    def _():
        both(1)
        late.wait()
        word[...] += first_here[upper] + dot(joined[upper], q[...], NN)

    @pl.when(step == 5)
    def _():
        ent[...] += first_here[lower] + dot(joined[lower], q[...], NN)


def grad_hidden(d_first, grads, kv, q, after=()):
    after = tokens(after)
    return pl.pallas_call(
        functools.partial(grad_hidden_kernel, len(after)),
        grid=(6,),
        in_specs=[
            pl.BlockSpec((None, D, D), lambda i: (jnp.minimum(i, 1), 0, 0)),
            pl.BlockSpec((None, D, D), lambda i: (jnp.maximum(i - 2, 0), 0, 0)),
        ]
        + [VMEM] * 8
        + [HBM]
        + [ANY] * len(after),
        out_specs=[VMEM] * 2,
        out_shape=[stored((WORDS, D), f32), stored((ENTS, D), f32)],
        scratch_shapes=[
            pltpu.VMEM((ROWS, D), bf16),
            pltpu.VMEM((ROWS, D), f32),
            pltpu.SemaphoreType.DMA,
        ],
        compiler_params=PARAMS,
        cost_estimate=cost(9),
        name="grad_hidden",
    )(kv, q, *grads, d_first, *after)


def flip(axis, bit, value):
    size = lax.axis_size(axis)
    return lax.ppermute(value, axis, [(i, i ^ bit) for i in range(size)])


def over(name, value):
    axis, bit = {
        "core": ("narrow", 1),
        "x": ("narrow", 2),
        "y": ("wide", 1),
        "low": ("wide", 2),
        "high": ("wide", 4),
    }[name]
    return flip(axis, bit, value)


class Links:
    def __init__(self):
        self.past = {}

    def send(self, name, value):
        kind = "z" if name in ("low", "high") else name
        past = self.past.setdefault(kind, [])
        if len(past) > 1:
            value, unused = lax.optimization_barrier((value, past[-2]))
        got = over(name, value)
        past.append(got)
        return got


def later(values, token):
    return lax.optimization_barrier((values, token))[0]


def gather_high(links, first, second):
    both = jnp.concatenate([first, second], 0)
    return both, links.send("high", both)


def gather_low(links, cut, both):
    both = jnp.stack(both, 0)
    got = links.send("low", both)
    left = jnp.stack([both[:, :cut], got[:, :cut]], 0)
    right = jnp.stack([both[:, cut:], got[:, cut:]], 0)
    return left, right


def gather_near(links, left, right, token=None):
    got_left = links.send("x", left)
    got_right = links.send("y", right)
    if token is not None:
        got_left, got_right = later((got_left, got_right), token)
    left = jnp.stack([left, got_left], 0)
    right = jnp.stack([right, got_right], 0)
    return left, right


def gather_far(links, left, right):
    return gather_core(left, right, links.send("y", left), links.send("x", right))


def gather_core(left, right, left_far, right_far):
    left = jnp.stack([left, left_far], 0)
    right = jnp.stack([right, right_far], 0)
    return left, over("core", left), right, over("core", right)


def plus(kept, got):
    return (kept.astype(f32) + got.astype(f32)).astype(bf16)


class Sum:
    def __init__(self, send_left, send_right, keep):
        self.keep = keep
        self.got = over("x", send_left), over("y", send_right)

    def wait(self, token):
        self.got = later(self.got, token) if isinstance(self.got, tuple) else later((self.got,), token)[0]
        return self

    def parts(self):
        left, right = self.got
        keep = self.keep
        return (
            plus(keep[0, 1], left[1]),
            plus(keep[1, 1], right[1]),
            (plus(keep[0, 0], left[0]), plus(keep[1, 0], right[0])),
        )

    def second(self):
        left, right, self.keep = self.parts()
        self.got = over("y", left), over("x", right)

    def near(self):
        left, right = self.got
        return plus(self.keep[0], left), plus(self.keep[1], right)


def flat(blocks, leading):
    return jnp.concatenate([v.reshape(v.shape[:leading] + (-1, 384)) for v in blocks], leading)


def gather_all(value):
    size = lax.axis_size("wide") * lax.axis_size("narrow")
    spread = jnp.broadcast_to(value[None], (size,) + value.shape)
    return lax.all_to_all(spread, ("wide", "narrow"), 0, 0, tiled=False)


def sum_all(value):
    return jnp.sum(gather_all(value), axis=0)


def adapt(weight, grad, first, second, decay):
    first = 0.5 * first + 0.5 * grad
    second = 0.5 * second + 0.5 * grad * grad
    fix_first = 1.0 - 0.5**STEP
    fix_second = 1.0 - 0.5**STEP
    update = first / fix_first / (jnp.sqrt(second / fix_second) + adam_eps) + decay * weight
    return (first, second, update)


def apply_kernel(rates, att, exp, red, att_update, exp_update, red_update, *new):
    for k in range(7):
        new[0][k] = att[k] - rates[k] * att_update[k]
    new[1][...] = exp[...] - rates[7] * exp_update[...]
    new[2][...] = red[...] - rates[8] * red_update[...]


def apply_updates(rates, weights, updates):
    return pl.pallas_call(
        apply_kernel,
        in_specs=[SMEM] + [VMEM] * 6,
        out_specs=[VMEM] * 3,
        out_shape=[stored(w.shape, f32) for w in weights],
        compiler_params=PARAMS,
        name="apply_updates",
    )(rates, *weights, *updates)


def shards(
    fast,
    word_states,
    entity_states,
    seq_counts,
    attention_weight,
    expand_weight,
    reduce_weight,
    norm_params,
    moment_attention,
    moment_expand,
    moment_reduce,
    moment_norms,
    square_attention,
    square_expand,
    square_reduce,
    square_norms,
    word_cotangent,
    entity_cotangent,
):
    word, ent, counts = word_states[0], entity_states[0], seq_counts[0]
    core = lax.axis_index("narrow") % 2
    high = lax.axis_index("wide") // 4
    if fast:
        keep, send, exp_low, red_low, weight_local = prep(
            attention_weight, expand_weight, reduce_weight.T
        )
        got = over("core", send)
        rows = jnp.where(
            core == 0, jnp.concatenate([keep, got], 2), jnp.concatenate([got, keep], 2)
        )
        links = Links()
        kv = gather_high(links, rows[4], rows[5])
        query = gather_high(
            links,
            jnp.concatenate([rows[0], rows[2]], 0),
            jnp.concatenate([rows[1], rows[3]], 0),
        )
        kv = gather_low(links, 48, kv)
        query = gather_low(links, 96, query)
        kv = gather_near(links, *kv)
        kv_pieces = gather_far(links, *kv)
        query = gather_near(links, *query)
        query_far = links.send("y", query[0]), links.send("x", query[1])
        one = gather_high(
            links,
            jnp.concatenate([exp_low[:96], rows[6, :32]], 0),
            jnp.concatenate([exp_low[96:], rows[6, 32:]], 0),
        )
        one = gather_low(links, 128, one)
        kv_pieces = [v.reshape(v.shape[:4] + (1, 48, 384)) for v in kv_pieces]
    else:
        weight_local = jnp.concatenate(
            [
                jnp.sum(attention_weight * attention_weight, axis=(1, 2)),
                jnp.sum(expand_weight * expand_weight)[None],
                jnp.sum(reduce_weight * reduce_weight)[None],
            ]
        )
        turned = jnp.swapaxes(attention_weight.astype(bf16), 1, 2)
        turned = lax.all_gather(turned, "wide", axis=1, tiled=True)
        turned = lax.all_gather(turned, "narrow", axis=2, tiled=True)
        exp_all = lax.all_gather(expand_weight.astype(bf16), "wide", axis=1, tiled=True)
        exp_all = lax.all_gather(exp_all, "narrow", axis=0, tiled=True)
        red_all = lax.all_gather(reduce_weight.astype(bf16).T, "wide", axis=0, tiled=True)
        red_all = lax.all_gather(red_all, "narrow", axis=1, tiled=True)
        kv_pieces = query_pieces = [turned]
        one_pieces = [turned, exp_all]
        two_pieces = [red_all]
        one = two = (None, None)

    low, keys, values, low_mine, low_other, kv_all = project_kv(fast, word, ent, kv_pieces)
    if fast:
        query_pieces = gather_core(*query, *later(query_far, keys))
        query_pieces = [v.reshape(v.shape[:4] + (2, 48, 384)) for v in query_pieces]
        two = gather_high(links, *later((red_low[:48], red_low[48:]), keys))
        one = gather_near(links, *later(one, keys))
        one_far = links.send("y", one[0]), links.send("x", one[1])
    to_words, to_ents, q_all = project_q(fast, low, query_pieces, after=two)
    if fast:
        two = gather_low(links, 48, two)
    context, exact, lse = attend(counts, to_words, to_ents, keys, values, after=one + two)
    if fast:
        two = gather_near(links, *two, token=context)
        one_pieces = gather_core(*one, *later(one_far, two))
        two_far = links.send("y", two[0]), links.send("x", two[1])
        two_core = over("core", two[0]), over("core", two[1])
    (
        middle,
        middle_low,
        activated,
        slope,
        unit_one,
        picks,
        out_all,
        exp_all,
    ) = feed_in(fast, word, ent, context, norm_params, one_pieces, after=two)
    if fast:
        two_far = later(two_far, activated)
        two_pieces = (two[0], two_core[0], two[1], two_core[1])
        two_pieces += (two_far[0], over("core", two_far[0]), two_far[1], over("core", two_far[1]))
    word_out, ent_out, d_second, d_ffn, grads_two, red_all = feed_out(
        fast, activated, middle, norm_params, word_cotangent[0], entity_cotangent[0], two_pieces
    )
    got = red = exp = att_one = att_two = None
    if fast:
        got = over("core", grad_red(False, d_ffn, activated)[0])
    d_inner, d_first, d_out, d_context, row_inner, grads_one = feed_back(
        d_ffn, red_all, exp_all, slope, norm_params, d_second, unit_one, out_all, exact
    )
    if fast:
        red = Sum(*grad_red(True, d_ffn, activated, got, after=(d_first,)))
    exp_args = (d_inner, d_out)
    norm_args = (grads_one, grads_two)
    att_args = (counts, to_words, to_ents, keys, values, d_context, lse, row_inner)
    if fast:
        sent = grad_exp(False, picks, *exp_args, norm_args, after=(red.keep,))[0]
        got = over("core", sent)
    grads = attend_back(0, *att_args, after=(sent,) if fast else ())
    if fast:
        red.wait(grads[0]).second()
        exp = Sum(
            *grad_exp(True, picks, *exp_args, norm_args, got, after=red.keep)
        )
        sent = grad_att(0, False, low_other, grads, after=(exp.keep,))[0]
        got = over("core", sent)
    more = attend_back(3, *att_args, after=(sent,) if fast else ())
    if fast:
        red_near = red.wait(more[0]).near()
        exp.wait(more[0]).second()
        sent = grad_att(1, False, low_other, more, after=exp.keep + red_near)[0]
        got_two = over("core", sent)
        att_one = Sum(*grad_att(0, True, low_mine, grads, got, after=(sent,)))
        att_two = Sum(*grad_att(1, True, low_mine, more, got_two, after=(att_one.keep,)))
        exp_near = exp.wait(att_two.keep).near()
        near = flat(red_near + exp_near, 2)
        low_got = over("low", near[1])
    word_grad, ent_grad = grad_hidden(
        d_first, grads + more, kv_all, q_all, after=(att_two.keep,) if fast else ()
    )

    if fast:
        att_one.got, att_two.got = later((att_one.got, att_two.got), word_grad)
        one_left, one_right, one_keep = att_one.parts()
        two_left, two_right, two_keep = att_two.parts()
        left_got = over("y", jnp.concatenate([one_left, two_left], 1))
        right_got = over("x", jnp.concatenate([one_right, two_right], 1))
        near = plus(near[0], later(low_got, (two_left, two_right)))
        high_got = over("high", near[1])
        left = plus(jnp.concatenate([one_keep[0], two_keep[0]], 1), left_got)
        right = plus(jnp.concatenate([one_keep[1], two_keep[1]], 1), right_got)
        got = over("low", jnp.concatenate([left[1], right[1]], 0))
        att_low = plus(jnp.concatenate([left[0], right[0]], 0), got).reshape(2, 2, 144, 384)
        att_low = jnp.swapaxes(att_low, 0, 1).reshape(2, 288, 384)
        high_got = later(high_got, att_low)
        near = near[0].astype(f32) + high_got.astype(f32)
        red_sum = near[:192].reshape(2, 48, D)
        exp_sum = near[192:].reshape(2, 128, 384)
        norm_row = jnp.concatenate([exp_sum[1, 96, :128], jnp.pad(weight_local, (0, 119))])
        norm_rows = gather_all(norm_row)
        weight_total = jnp.sum(norm_rows[:, 128:137], axis=0)
        norm_grads = norm_rows[:, :128].reshape(8, 4, 128)[:6]
        norm_grads = jnp.swapaxes(norm_grads, 0, 1).reshape(4, D)
        first, second = att_low[0], att_low[1]
        got = over("high", jnp.where(high == 0, second, first))
        att_sum = jnp.where(high == 0, first, second).astype(f32) + got.astype(f32)
        att_sum = att_sum.reshape(2, 144, 384)
        out_rows = jnp.concatenate([exp_sum[0, 96:], exp_sum[1, 112:]], 0)
        turned = jnp.stack(
            [
                att_sum[0, 48:96],
                att_sum[1, 48:96],
                att_sum[0, 96:],
                att_sum[1, 96:],
                att_sum[0, :48],
                att_sum[1, :48],
                out_rows,
            ]
        )
        att_grad = with_layout_constraint(
            jnp.swapaxes(unpacked(turned), 1, 2), Layout((0, 1, 2))
        )
        exp_grad = jnp.concatenate([exp_sum[0, :96], exp_sum[1, :96]], 0)
        red_grad = jnp.concatenate([red_sum[0], red_sum[1]], 0)
    else:
        d_to_words, d_to_ents, d_keys, d_values = [
            jnp.concatenate([a, b], 1) for a, b in zip(grads, more)
        ]
        norm_grads = sum_all(jnp.concatenate([grads_one, grads_two], 0))
        weight_total = sum_all(weight_local)
        words, ents = low[:WORDS], low[WORDS:]
        turned = jnp.stack(
            [
                dot(d_to_words[:WORDS], words, TN),
                dot(d_to_ents[:WORDS], words, TN),
                dot(d_to_words[WORDS:], ents, TN),
                dot(d_to_ents[WORDS:], ents, TN),
                dot(d_keys, low, TN),
                dot(d_values, low, TN),
                dot(d_out, context, TN),
            ]
        ).astype(bf16)
        turned = lax.psum_scatter(turned, "wide", scatter_dimension=1, tiled=True)
        turned = lax.psum_scatter(turned, "narrow", scatter_dimension=2, tiled=True)
        att_grad = jnp.swapaxes(turned.astype(f32), 1, 2)
        grad = dot(middle_low, d_inner, TN).astype(bf16)
        grad = lax.psum_scatter(grad, "wide", scatter_dimension=1, tiled=True)
        grad = lax.psum_scatter(grad, "narrow", scatter_dimension=0, tiled=True)
        exp_grad = grad.astype(f32)
        activated = jnp.swapaxes(activated, 0, 1).reshape(ROWS, FF)
        grad = dot(d_ffn, activated, TN).astype(bf16)
        grad = lax.psum_scatter(grad, "wide", scatter_dimension=0, tiled=True)
        grad = lax.psum_scatter(grad, "narrow", scatter_dimension=1, tiled=True)
        red_grad = grad.astype(f32)

    att_first, att_second, att_update = adapt(
        attention_weight, att_grad, moment_attention, square_attention, matrix_decay
    )
    exp_first, exp_second, exp_update = adapt(
        expand_weight, exp_grad, moment_expand, square_expand, matrix_decay
    )
    red_first, red_second, red_update = adapt(
        reduce_weight.T, red_grad, moment_reduce.T, square_reduce.T, matrix_decay
    )
    update_local = jnp.concatenate(
        [
            jnp.sum(att_update * att_update, axis=(1, 2)),
            jnp.sum(exp_update * exp_update)[None],
            jnp.sum(red_update * red_update)[None],
        ]
    )
    update_total = sum_all(update_local)
    nrm_first, nrm_second, nrm_update = adapt(
        norm_params, norm_grads, moment_norms, square_norms, 0.0
    )
    weight_norm = jnp.sqrt(
        jnp.concatenate([weight_total, jnp.sum(norm_params * norm_params, axis=1)])
    )
    update_norm = jnp.sqrt(
        jnp.concatenate([update_total, jnp.sum(nrm_update * nrm_update, axis=1)])
    )
    trust = weight_norm / update_norm
    new_attention, new_expand, new_reduce = apply_updates(
        learn_rate * trust[:9],
        (attention_weight, expand_weight, reduce_weight.T),
        (att_update, exp_update, red_update),
    )
    new_reduce = new_reduce.T
    new_norms = norm_params - learn_rate * trust[9:13, None] * nrm_update
    trust_stats = jnp.stack([jnp.log(weight_norm), jnp.log(update_norm), jnp.log(trust)], 1)
    return (
        word_out[None],
        ent_out[None],
        word_grad[None],
        ent_grad[None],
        new_attention,
        new_expand,
        new_reduce,
        new_norms,
        att_first,
        exp_first,
        red_first.T,
        nrm_first,
        att_second,
        exp_second,
        red_second.T,
        nrm_second,
        trust_stats,
    )


def solution(mesh):
    fast = mesh.shape["wide"] == 8 and mesh.shape["narrow"] == 4
    rows = P(("wide", "narrow"), None, None)
    matrix = P("narrow", "wide")
    stack = P(None, "narrow", "wide")
    weights = (stack, matrix, matrix, P())
    return jax.shard_map(
        functools.partial(shards, fast),
        mesh=mesh,
        in_specs=(rows, rows, P(("wide", "narrow"), None)) + weights * 3 + (rows, rows),
        out_specs=(rows,) * 4 + weights * 3 + (P(),),
        check_vma=False,
    )
```

```python
import functools

import jax
import jax.numpy as jnp
from jax import lax
from jax.experimental import pallas as pl
from jax.experimental.pallas import tpu as pltpu
from jax.sharding import PartitionSpec as P

D = 768
FF = 3072
HEADS = 12
HEAD = 64
WORDS = 512
ENTS = 128
ROWS = WORDS + ENTS
STEP = 7

eps_norm = 1e-05
adam_eps = 1e-06
matrix_decay = 0.01
learn_rate = 0.5
masked_score = -1e30

f32 = jnp.float32
bf16 = jnp.bfloat16
NN = (((1,), (0,)), ((), ()))
NT = (((1,), (1,)), ((), ()))
TN = (((0,), (0,)), ((), ()))
VMEM = pl.BlockSpec(memory_space=pltpu.VMEM)
SMEM = pl.BlockSpec(memory_space=pltpu.SMEM)
ANY = pl.BlockSpec(memory_space=pl.ANY)
HBM = pl.BlockSpec(memory_space=pltpu.HBM)
COST_RATE = 4e9
PARAMS = pltpu.CompilerParams(vmem_limit_bytes=12 * 2**20)
WIDE = pltpu.CompilerParams(vmem_limit_bytes=28 * 2**20)


def dot(left, right, dims):
    return lax.dot_general(left, right, dims, preferred_element_type=f32)


def shape(dims, dtype):
    return jax.ShapeDtypeStruct(dims, dtype)


def kept(dims, dtype):
    return pltpu.VMEM(dims, dtype)


def stored(dims, dtype):
    return pltpu.HBM(dims, dtype)


def tokens(values):
    return [v for v in values if v is not None]


def cost(us, rate=COST_RATE):
    return pl.CostEstimate(flops=int(us * rate), bytes_accessed=0, transcendentals=0)


def away_blocks():
    for core in range(2):
        for outer in range(2):
            for lead in range(2):
                for low in range(2):
                    for high in range(2):
                        yield core, outer, lead, low, high


def places(wide, narrow, second, block):
    core, outer, lead, low, high = block
    x_away, y_away = (outer, lead) if second else (lead, outer)
    w = wide ^ (high * 4 + low * 2 + y_away)
    n = narrow ^ (x_away * 2 + core)
    return w, n


def piece_of(bufs, block):
    core, outer, lead, low, high = block
    return bufs[core].at[outer, lead, low, high]


def coords():
    return lax.axis_index("wide"), lax.axis_index("narrow")


def start_attention(bufs, second, target, slots, sem):
    wide, narrow = coords()
    for block in away_blocks():
        w, n = places(wide, narrow, second, block)
        row = pl.multiple_of(w * 96 + (n % 2) * 48, 16)
        lane = pl.multiple_of((n // 2) * 384, 128)
        src = piece_of(bufs, block)
        pltpu.make_async_copy(src, target.at[slots, pl.ds(row, 48), pl.ds(lane, 384)], sem).start()


def drain(ref, sem):
    pltpu.make_async_copy(ref, ref, sem).wait()


def prep_kernel(att, exp, red, keep, send, exp_low, red_low, sums):
    narrow = lax.axis_index("narrow")
    core = narrow % 2
    total = []
    for i in range(7):
        value = att[i]
        total.append(jnp.sum(value * value))
        turned = value.T.astype(bf16)
        halves = turned.reshape(2, 48, 192)

        @pl.when(core == 0)
        def _():
            keep[i] = halves[0]
            send[i] = halves[1]

        @pl.when(core == 1)
        def _():
            keep[i] = halves[1]
            send[i] = halves[0]

    value = exp[...]
    total.append(jnp.sum(value * value))
    exp_low[...] = value.astype(bf16)
    value = red[...]
    total.append(jnp.sum(value * value))
    red_low[...] = value.astype(bf16)
    for i in range(9):
        sums[i] = total[i]


def prep(att, exp, red):
    return pl.pallas_call(
        prep_kernel,
        in_specs=[VMEM] * 3,
        out_specs=[VMEM] * 4 + [SMEM],
        out_shape=[
            shape((7, 48, 192), bf16),
            shape((7, 48, 192), bf16),
            shape((192, 384), bf16),
            shape((96, D), bf16),
            shape((9,), f32),
        ],
        compiler_params=pltpu.CompilerParams(vmem_limit_bytes=60 * 2**20),
        name="prep",
    )(att, exp, red)


def pick_rows(source, mine, other):
    core = lax.axis_index("narrow") % 2
    for c in range(2):

        @pl.when(core == c)
        def _():
            for target, at in ((mine, c * 192), (other, 192 - c * 192)):
                target[:, :192] = source[:, at : at + 192]
                target[:, 192:] = source[:, at + 384 : at + 576]


def pick_tiles(source, mine, other):
    core = lax.axis_index("narrow") % 2
    for c in range(2):

        @pl.when(core == c)
        def _():
            for target, at in ((mine, c * 192), (other, 192 - c * 192)):
                target[:, :128] = source[:, at : at + 128]
                target[:, 128:256] = source[:, at + 384 : at + 512]
                target[:, 256:320] = source[:, at + 128 : at + 192]
                target[:, 320:] = source[:, at + 512 : at + 576]


def project_kv_kernel(fast, n_after, word, ent, *refs):
    if fast:
        first, second, refs = refs[:2], refs[2:4], refs[4:]
    else:
        whole, refs = refs[0], refs[1:]
    low, keys, values, mine, other, saved, target, sem, sem_save = refs[n_after:]
    if fast:
        start_attention(first, False, target, pl.ds(0, 1), sem)
        start_attention(second, True, target, pl.ds(1, 1), sem)
    else:
        pltpu.make_async_copy(whole.at[pl.ds(4, 2)], target, sem).start()
    low[:WORDS] = word[...].astype(bf16)
    low[WORDS:] = ent[...].astype(bf16)
    pick_tiles(low, mine, other)
    drain(target, sem)
    save = pltpu.make_async_copy(target, saved, sem_save)
    save.start()
    keys[...] = dot(low[...], target[0], NT).astype(bf16)
    values[...] = dot(low[...], target[1], NT).astype(bf16)
    save.wait()


def project_kv(fast, word, ent, pieces, after=()):
    after = tokens(after)
    return pl.pallas_call(
        functools.partial(project_kv_kernel, fast, len(after)),
        in_specs=[VMEM, VMEM] + [ANY] * (len(pieces) + len(after)),
        out_specs=[VMEM] * 5 + [HBM],
        out_shape=[kept((ROWS, D), bf16)] * 3
        + [stored((ROWS, D // 2), bf16)] * 2
        + [stored((2, D, D), bf16)],
        scratch_shapes=[
            pltpu.VMEM((2, D, D), bf16),
            pltpu.SemaphoreType.DMA,
            pltpu.SemaphoreType.DMA,
        ],
        compiler_params=PARAMS,
        cost_estimate=cost(6, 4e8),
        name="project_kv",
    )(word, ent, *pieces, *after)


def project_q_kernel(fast, n_after, low, *refs):
    if fast:
        first, second, refs = refs[:2], refs[2:4], refs[4:]
    else:
        whole, refs = refs[0], refs[1:]
    to_words, to_ents, saved, target, sem, sem_save = refs[n_after:]
    if fast:
        start_attention(first, False, target, pl.ds(0, 2), sem)
        start_attention(second, True, target, pl.ds(2, 2), sem)
    else:
        for slot, k in enumerate((0, 2, 1, 3)):
            pltpu.make_async_copy(whole.at[k], target.at[slot], sem).start()
    drain(target, sem)
    save = pltpu.make_async_copy(target, saved, sem_save)
    save.start()
    scale = HEAD ** (-0.5)
    word = low[:WORDS]
    ent = low[WORDS:]
    to_words[:WORDS] = (dot(word, target[0], NT) * scale).astype(bf16)
    to_words[WORDS:] = (dot(ent, target[1], NT) * scale).astype(bf16)
    to_ents[:WORDS] = (dot(word, target[2], NT) * scale).astype(bf16)
    to_ents[WORDS:] = (dot(ent, target[3], NT) * scale).astype(bf16)
    save.wait()


def project_q(fast, low, pieces, after=()):
    after = tokens(after)
    return pl.pallas_call(
        functools.partial(project_q_kernel, fast, len(after)),
        in_specs=[VMEM] + [ANY] * (len(pieces) + len(after)),
        out_specs=[VMEM] * 2 + [HBM],
        out_shape=[kept((ROWS, D), bf16)] * 2 + [stored((4, D, D), bf16)],
        scratch_shapes=[
            pltpu.VMEM((4, D, D), bf16),
            pltpu.SemaphoreType.DMA,
            pltpu.SemaphoreType.DMA,
        ],
        compiler_params=PARAMS,
        cost_estimate=cost(7, 4e8),
        name="project_q",
    )(low, *pieces, *after)


def head_masks(counts):
    lane = lax.broadcasted_iota(jnp.int32, (ROWS, 128), 1)
    row = lax.broadcasted_iota(jnp.int32, (ROWS, 128), 0)
    edge = jnp.where(row < WORDS, counts[0], counts[1] + WORDS)
    bias = jnp.where(row < edge, 0.0, masked_score)
    out = []
    for h in range(2):
        own = jnp.where((lane < HEAD) if h == 0 else (lane >= HEAD), 1.0, 0.0).astype(bf16)
        mark = jnp.where(lane == (HEAD if h == 0 else 0), 1.0, 0.0)
        rest = (1.0 - mark).astype(bf16)
        tag = (bias * mark).astype(bf16)
        out.append((own, mark.astype(bf16), rest, tag))
    return out


def scores_of(masks, keys, to_words, to_ents):
    own, mark, rest, tag = masks
    tagged = keys * own + tag
    upper = dot(tagged[:WORDS], to_words * rest + mark, NT)
    lower = dot(tagged[WORDS:], to_ents * rest + mark, NT)
    return jnp.concatenate([upper, lower], 0)


def attend_kernel(n_after, counts, to_words, to_ents, keys, values, *refs):
    context, exact, lse = refs[n_after:]
    masks = head_masks(counts)
    pair = pl.program_id(0)
    lanes = pl.ds(pl.multiple_of(pair * 128, 128), 128)
    key, value = keys[:, lanes], values[:, lanes]
    outs = []
    for h in range(2):
        scores = scores_of(masks[h], key, to_words[:, lanes], to_ents[:, lanes])
        top = jnp.max(scores, axis=0, keepdims=True)
        expd = jnp.exp(scores - top)
        total = jnp.sum(expd, axis=0, keepdims=True)
        lse[pair, h : h + 1, :] = top + jnp.log(total)
        mixed = dot(value[:, h * HEAD : (h + 1) * HEAD], expd.astype(bf16), TN)
        outs.append(mixed * (1.0 / total))
    joined = jnp.concatenate(outs, 0).T
    exact[...] = joined
    context[:, lanes] = joined.astype(bf16)


def attend(counts, to_words, to_ents, keys, values, after=()):
    after = tokens(after)
    return pl.pallas_call(
        functools.partial(attend_kernel, len(after)),
        grid=(HEADS // 2,),
        in_specs=[SMEM] + [VMEM] * 4 + [ANY] * len(after),
        out_specs=[VMEM, pl.BlockSpec((ROWS, 128), lambda i: (0, i)), VMEM],
        out_shape=[
            kept((ROWS, D), bf16),
            stored((ROWS, D), f32),
            kept((HEADS // 2, 2, ROWS), f32),
        ],
        compiler_params=PARAMS,
        cost_estimate=cost(12, 4e8),
        name="attend",
    )(counts, to_words, to_ents, keys, values, *after)


def normed(value):
    center = value - jnp.mean(value, axis=-1, keepdims=True)
    spread = jnp.mean(center * center, axis=-1, keepdims=True)
    inverse = lax.rsqrt(spread + eps_norm)
    return center * inverse, inverse


def normed_back(unit, inverse, cotangent):
    mean = jnp.mean(cotangent, axis=-1, keepdims=True)
    inner = jnp.mean(cotangent * unit, axis=-1, keepdims=True)
    return inverse * (cotangent - mean - unit * inner)


def column_sum(value):
    return jnp.sum(value, axis=0, keepdims=True)


def feed_in_kernel(fast, n_after, word, ent, context, norms, *refs):
    if fast:
        bufs, refs = (refs[0:2], refs[2:4]), refs[4:]
    else:
        bufs, refs = refs[0:2], refs[2:]
    (
        middle_saved,
        middle_low,
        act_saved,
        slope_saved,
        unit_saved,
        picks_saved,
        out_saved,
        exp_saved,
        middle,
        activated,
        slope,
        unit_here,
        picks,
        out_all,
        exp_all,
        sem_out,
        sem_exp,
        sem_save,
    ) = refs[n_after:]
    step = pl.program_id(0)
    pairs = (
        (unit_here, unit_saved),
        (picks, picks_saved),
        (out_all, out_saved),
        (middle, middle_saved),
    )
    saves = [pltpu.make_async_copy(*pair, sem_save.at[i]) for i, pair in enumerate(pairs)]

    @pl.when(step == 0)
    def _():
        if fast:
            start_feed_in(bufs, out_all, exp_all, sem_out, sem_exp)
        else:
            pltpu.make_async_copy(bufs[0].at[6], out_all, sem_out).start()
            for j in range(4):
                cols = pl.ds(j * D, D)
                pltpu.make_async_copy(bufs[1].at[:, cols], exp_all.at[j], sem_exp.at[j]).start()
        drain(out_all, sem_out)
        saves[2].start()
        hidden = jnp.concatenate([word[...], ent[...]], 0)
        unit, inverse = normed(hidden + dot(context[...], out_all[...], NT))
        value = unit * norms[0:1, :] + norms[1:2, :]
        unit_here[:, :D] = unit
        unit_here[:, D:] = jnp.broadcast_to(inverse, (ROWS, 128))
        saves[0].start()
        middle_low[...] = value.astype(bf16)
        middle[...] = value
        saves[3].start()
        pick_rows(middle_low, picks.at[0], picks.at[1])
        pick_tiles(context, picks.at[2], picks.at[3])
        saves[1].start()

    drain(exp_all.at[step], sem_exp.at[step])
    pltpu.make_async_copy(exp_all.at[step], exp_saved.at[step], sem_save.at[4 + step]).start()
    inner = dot(middle_low[...], exp_all[step], NN)
    share = 0.5 + 0.5 * lax.erf(inner * 0.7071067811865476)
    bell = jnp.exp(-0.5 * inner * inner) * 0.3989422804014327
    slope[step] = (share + inner * bell).astype(bf16)
    activated[step] = (inner * share).astype(bf16)
    pltpu.make_async_copy(slope.at[step], slope_saved.at[step], sem_save.at[8 + step]).start()
    pltpu.make_async_copy(activated.at[step], act_saved.at[step], sem_save.at[12 + step]).start()

    @pl.when(step == 3)
    def _():
        for save in saves:
            save.wait()
        for j in range(4):
            pltpu.make_async_copy(exp_all.at[j], exp_saved.at[j], sem_save.at[4 + j]).wait()
            pltpu.make_async_copy(slope.at[j], slope_saved.at[j], sem_save.at[8 + j]).wait()
            pltpu.make_async_copy(activated.at[j], act_saved.at[j], sem_save.at[12 + j]).wait()


def start_feed_in(bufs, out_all, exp_all, sem_out, sem_exp):
    wide, narrow = coords()
    for half in range(2):
        skip, count = ((0, 32), (32, 16))[half]
        for block in away_blocks():
            w, n = places(wide, narrow, half == 1, block)
            row = pl.multiple_of(w * 96 + (n % 2) * 48 + skip, 16)
            lane = pl.multiple_of((n // 2) * 384, 128)
            src = piece_of(bufs[half], block).at[pl.ds(96, count)]
            dst = out_all.at[pl.ds(row, count), pl.ds(lane, 384)]
            pltpu.make_async_copy(src, dst, sem_out).start()
    for half in range(2):
        for block in away_blocks():
            w, n = places(wide, narrow, half == 1, block)
            src = piece_of(bufs[half], block).at[pl.ds(0, 96)]
            row = pl.multiple_of(n * 192 + half * 96, 16)
            lane = pl.multiple_of((w % 2) * 384, 128)
            dst = exp_all.at[w // 2, pl.ds(row, 96), pl.ds(lane, 384)]
            pltpu.make_async_copy(src, dst, sem_exp.at[w // 2]).start()


def feed_in(fast, word, ent, context, norms, pieces, after=()):
    after = tokens(after)
    return pl.pallas_call(
        functools.partial(feed_in_kernel, fast, len(after)),
        grid=(4,),
        in_specs=[VMEM] * 4 + [ANY] * (len(pieces) + len(after)),
        out_specs=[HBM, VMEM] + [HBM] * 6,
        out_shape=[
            stored((ROWS, D), f32),
            kept((ROWS, D), bf16),
            stored((4, ROWS, D), bf16),
            stored((4, ROWS, D), bf16),
            stored((ROWS, D + 128), f32),
            stored((4, ROWS, D // 2), bf16),
            stored((D, D), bf16),
            stored((4, D, D), bf16),
        ],
        scratch_shapes=[
            pltpu.VMEM((ROWS, D), f32),
            pltpu.VMEM((4, ROWS, D), bf16),
            pltpu.VMEM((4, ROWS, D), bf16),
            pltpu.VMEM((ROWS, D + 128), f32),
            pltpu.VMEM((4, ROWS, D // 2), bf16),
            pltpu.VMEM((D, D), bf16),
            pltpu.VMEM((4, D, D), bf16),
            pltpu.SemaphoreType.DMA,
            pltpu.SemaphoreType.DMA((4,)),
            pltpu.SemaphoreType.DMA((16,)),
        ],
        compiler_params=pltpu.CompilerParams(vmem_limit_bytes=28 * 2**20),
        cost_estimate=cost(0),
        name="feed_in",
    )(word, ent, context, norms, *pieces, *after)


def feed_out_kernel(fast, n_after, norms, activated, middle, word_cot, ent_cot, *refs):
    if fast:
        bufs, refs = (refs[0:2], refs[2:4], refs[4:6], refs[6:8]), refs[8:]
    else:
        bufs, refs = refs[0:1], refs[1:]
    (
        word_out,
        ent_out,
        second_saved,
        d_ffn,
        grads_two,
        red_saved,
        total,
        cot_here,
        middle_here,
        d_second,
        act_here,
        red_all,
        sem_red,
        sem_act,
        sem_save,
        sem_late,
    ) = refs[n_after:]
    step = pl.program_id(0)
    upper, lower = pl.ds(0, WORDS), pl.ds(WORDS, ENTS)
    late = (
        pltpu.make_async_copy(word_cot, cot_here.at[upper], sem_late.at[0]),
        pltpu.make_async_copy(ent_cot, cot_here.at[lower], sem_late.at[1]),
        pltpu.make_async_copy(middle, middle_here, sem_late.at[2]),
    )
    saves = (
        pltpu.make_async_copy(total.at[upper], word_out, sem_save.at[0]),
        pltpu.make_async_copy(total.at[lower], ent_out, sem_save.at[1]),
        pltpu.make_async_copy(d_second, second_saved, sem_save.at[2]),
    )

    @pl.when(step == 0)
    def _():
        for j in range(4):
            pltpu.make_async_copy(activated.at[j], act_here.at[j], sem_act.at[j]).start()
        if fast:
            start_feed_out(bufs, red_all, sem_red)
        else:
            for j in range(4):
                cols = pl.ds(j * D, D)
                pltpu.make_async_copy(bufs[0].at[:, cols], red_all.at[j], sem_red.at[j]).start()
        for copy in late:
            copy.start()

    drain(act_here.at[step], sem_act.at[step])
    drain(red_all.at[step], sem_red.at[step])
    pltpu.make_async_copy(red_all.at[step], red_saved.at[step], sem_save.at[3 + step]).start()
    part = dot(act_here[step], red_all[step], NT)

    @pl.when(step == 0)
    def _():
        total[...] = part

    @pl.when(step > 0)
    def _():
        total[...] += part

    @pl.when(step == 3)
    def _():
        for copy in late:
            copy.wait()
        unit, inverse = normed(total[...] + middle_here[...])
        total[...] = unit * norms[2:3, :] + norms[3:4, :]
        saves[0].start()
        saves[1].start()
        cot = cot_here[...]
        back = normed_back(unit, inverse, cot * norms[2:3, :])
        d_second[...] = back
        saves[2].start()
        d_ffn[...] = back.astype(bf16)
        grads_two[0:1, :] = column_sum(cot * unit)
        grads_two[1:2, :] = column_sum(cot)
        for save in saves:
            save.wait()
        for j in range(4):
            pltpu.make_async_copy(red_all.at[j], red_saved.at[j], sem_save.at[3 + j]).wait()


def start_feed_out(bufs, red_all, sem_red):
    wide, narrow = coords()
    for half in range(2):
        for block in away_blocks():
            w, n = places(wide, narrow, half == 1, block)
            core, outer, lead, low, high = block
            src = bufs[half + 2 * outer][core].at[lead, low, high]
            row = pl.multiple_of(w * 96 + half * 48, 16)
            pltpu.make_async_copy(src, red_all.at[n, pl.ds(row, 48)], sem_red.at[n]).start()


def feed_out(fast, activated, middle, norms, word_cot, ent_cot, pieces, after=()):
    after = tokens(after)
    return pl.pallas_call(
        functools.partial(feed_out_kernel, fast, len(after)),
        grid=(4,),
        in_specs=[VMEM] + [HBM] * 4 + [ANY] * (len(pieces) + len(after)),
        out_specs=[HBM] * 3 + [VMEM] * 2 + [HBM],
        out_shape=[
            stored((WORDS, D), f32),
            stored((ENTS, D), f32),
            stored((ROWS, D), f32),
            kept((ROWS, D), bf16),
            kept((2, D), f32),
            stored((4, D, D), bf16),
        ],
        scratch_shapes=[
            pltpu.VMEM((ROWS, D), f32),
            pltpu.VMEM((ROWS, D), f32),
            pltpu.VMEM((ROWS, D), f32),
            pltpu.VMEM((ROWS, D), f32),
            pltpu.VMEM((4, ROWS, D), bf16),
            pltpu.VMEM((4, D, D), bf16),
            pltpu.SemaphoreType.DMA((4,)),
            pltpu.SemaphoreType.DMA((4,)),
            pltpu.SemaphoreType.DMA((7,)),
            pltpu.SemaphoreType.DMA((3,)),
        ],
        compiler_params=pltpu.CompilerParams(vmem_limit_bytes=56 * 2**20),
        cost_estimate=cost(12),
        name="feed_out",
    )(norms, activated, middle, word_cot, ent_cot, *pieces, *after)


def feed_back_kernel(
    n_after, d_ffn, norms, red_all, exp_all, slope, d_second, unit_one, out_all, exact, *refs
):
    (
        d_inner,
        d_first,
        d_out,
        d_context,
        row_inner,
        grads_one,
        total,
        red_here,
        exp_here,
        slope_here,
        second_here,
        unit_here,
        out_here,
        exact_here,
        sem_step,
        sem_late,
        sem_save,
    ) = refs[n_after:]
    step = pl.program_id(0)
    pairs = (
        (d_second, second_here),
        (unit_one, unit_here),
        (out_all, out_here),
        (exact, exact_here),
    )
    late = [pltpu.make_async_copy(*pair, sem_late.at[i]) for i, pair in enumerate(pairs)]
    save = pltpu.make_async_copy(total, d_first, sem_save)
    parts = ((red_all, red_here), (slope, slope_here), (exp_all, exp_here))

    @pl.when(step == 0)
    def _():
        for j in range(4):
            for k, (there, here) in enumerate(parts):
                pltpu.make_async_copy(there.at[j], here.at[j], sem_step.at[k, j]).start()
        for copy in late:
            copy.start()

    drain(red_here.at[step], sem_step.at[0, step])
    drain(slope_here.at[step], sem_step.at[1, step])
    drain(exp_here.at[step], sem_step.at[2, step])
    lanes = pl.ds(pl.multiple_of(step * D, D), D)
    back = (dot(d_ffn[...], red_here[step], NN) * slope_here[step].astype(f32)).astype(bf16)
    d_inner[:, lanes] = back
    part = dot(back, exp_here[step], NT)

    @pl.when(step == 0)
    def _():
        total[...] = part

    @pl.when(step > 0)
    def _():
        total[...] += part

    @pl.when(step == 3)
    def _():
        for copy in late:
            copy.wait()
        d_middle = total[...] + second_here[...]
        unit = unit_here[:, :D]
        grads_one[0:1, :] = column_sum(d_middle * unit)
        grads_one[1:2, :] = column_sum(d_middle)
        first = normed_back(unit, unit_here[:, D : D + 1], d_middle * norms[0:1, :])
        total[...] = first
        save.start()
        low_first = first.astype(bf16)
        d_out[...] = low_first
        context = dot(low_first, out_here[...], NN).astype(bf16)
        d_context[...] = context
        product = context.astype(f32) * exact_here[...]
        head = lax.broadcasted_iota(jnp.int32, (16, D), 1) // HEAD
        pick = jnp.where(head == lax.broadcasted_iota(jnp.int32, (16, D), 0), 1.0, 0.0).astype(bf16)
        high = product.astype(bf16)
        low = (product - high.astype(f32)).astype(bf16)
        sums = dot(pick, high, NT) + dot(pick, low, NT)
        for i in range(HEADS // 2):
            row_inner[i] = sums[2 * i : 2 * i + 2]
        save.wait()


def feed_back(d_ffn, red_all, exp_all, slope, norms, d_second, unit_one, out_all, exact, after=()):
    after = tokens(after)
    return pl.pallas_call(
        functools.partial(feed_back_kernel, len(after)),
        grid=(4,),
        in_specs=[VMEM, VMEM] + [HBM] * 7 + [ANY] * len(after),
        out_specs=[VMEM, HBM] + [VMEM] * 4,
        out_shape=[
            kept((ROWS, FF), bf16),
            stored((ROWS, D), f32),
            kept((ROWS, D), bf16),
            kept((ROWS, D), bf16),
            kept((HEADS // 2, 2, ROWS), f32),
            kept((2, D), f32),
        ],
        scratch_shapes=[
            pltpu.VMEM((ROWS, D), f32),
            pltpu.VMEM((4, D, D), bf16),
            pltpu.VMEM((4, D, D), bf16),
            pltpu.VMEM((4, ROWS, D), bf16),
            pltpu.VMEM((ROWS, D), f32),
            pltpu.VMEM((ROWS, D + 128), f32),
            pltpu.VMEM((D, D), bf16),
            pltpu.VMEM((ROWS, D), f32),
            pltpu.SemaphoreType.DMA((3, 4)),
            pltpu.SemaphoreType.DMA((4,)),
            pltpu.SemaphoreType.DMA,
        ],
        compiler_params=pltpu.CompilerParams(vmem_limit_bytes=36 * 2**20),
        cost_estimate=cost(14),
        name="feed_back",
    )(d_ffn, norms, red_all, exp_all, slope, d_second, unit_one, out_all, exact, *after)


def attend_back_kernel(
    first, n_after, counts, to_words, to_ents, keys, values, d_context, lse, row_inner, *refs
):
    d_to_words, d_to_ents, d_keys, d_values = refs[n_after:]
    masks = head_masks(counts)
    scale = HEAD ** (-0.5)
    step = pl.program_id(0)
    pair = step + first
    lanes = pl.ds(pl.multiple_of(pair * 128, 128), 128)
    here = pl.ds(pl.multiple_of(step * 128, 128), 128)
    word_query, ent_query = to_words[...], to_ents[...]
    key, value, d_mixed = keys[...], values[...], d_context[:, lanes]
    one, two, three, four = [], [], [], []
    for h in range(2):
        cols = slice(h * HEAD, (h + 1) * HEAD)
        scores = scores_of(masks[h], key, word_query, ent_query)
        probs = jnp.exp(scores - lse[pair, h : h + 1, :])
        d_probs = dot(value * masks[h][0], d_mixed, NT)
        d_scores = (probs * (d_probs - row_inner[pair, h : h + 1, :])).astype(bf16)
        one.append(dot(key[:WORDS, cols], d_scores[:WORDS], TN))
        two.append(dot(key[WORDS:, cols], d_scores[WORDS:], TN))
        three.append(
            jnp.concatenate(
                [
                    dot(d_scores[:WORDS], word_query[:, cols], NN),
                    dot(d_scores[WORDS:], ent_query[:, cols], NN),
                ],
                0,
            )
        )
        four.append(dot(probs.astype(bf16), d_mixed[:, cols], NN))
    d_to_words[:, here] = (jnp.concatenate(one, 0).T * scale).astype(bf16)
    d_to_ents[:, here] = (jnp.concatenate(two, 0).T * scale).astype(bf16)
    d_keys[:, here] = jnp.concatenate(three, 1).astype(bf16)
    d_values[:, here] = jnp.concatenate(four, 1).astype(bf16)


def attend_back(first, counts, to_words, to_ents, keys, values, d_context, lse, row_inner, after=()):
    after = tokens(after)
    pair = pl.BlockSpec((ROWS, 128), lambda i: (0, i + first))
    return pl.pallas_call(
        functools.partial(attend_back_kernel, first, len(after)),
        grid=(HEADS // 4,),
        in_specs=[SMEM] + [pair] * 4 + [VMEM] * 3 + [ANY] * len(after),
        out_specs=[VMEM] * 4,
        out_shape=[(stored if first else kept)((ROWS, D // 2), bf16)] * 4,
        compiler_params=PARAMS,
        cost_estimate=cost(10),
        name="attend_back",
    )(counts, to_words, to_ents, keys, values, d_context, lse, row_inner, *after)


def relative():
    for x in range(2):
        for y in range(2):
            for low in range(2):
                for high in range(2):
                    yield x, y, low, high


def emit(mine, got, outs, half, first, rest, rows, value):
    if not mine:
        outs[0][(half, first) + rest + (rows,)] = value.astype(bf16)
        return
    value = (value + got[(half, first) + rest + (rows,)].astype(f32)).astype(bf16)
    if first:
        outs[half][rest + (rows,)] = value
    else:
        outs[2][(half,) + rest + (rows,)] = value


def grad_call(kernel, name, mine, operands, got, steps, dims, extra, after, specs=(), limit=12):
    after = tokens(after)
    if mine:
        outs = [kept((2,) + dims, bf16)] * 2 + [kept((2, 2) + dims, bf16)]
        operands = list(operands) + [got]
    else:
        outs = [kept((2, 2, 2) + dims, bf16)]
    return pl.pallas_call(
        functools.partial(kernel, mine, len(after), len(outs)),
        grid=(steps,),
        in_specs=list(specs)
        + [VMEM] * (len(operands) - len(specs))
        + [ANY] * len(after),
        out_specs=[VMEM] * len(outs),
        out_shape=outs,
        scratch_shapes=extra,
        compiler_params=pltpu.CompilerParams(vmem_limit_bytes=limit * 2**20),
        cost_estimate=cost(7),
        name=name,
    )(*operands, *after)


def split_refs(mine, n_after, n_outs, refs):
    got, refs = (refs[0], refs[1:]) if mine else (None, refs)
    refs = refs[n_after:]
    return got, refs[:n_outs], refs[n_outs:]


def grad_red_kernel(mine, n_after, n_outs, d_ffn, activated, *refs):
    got, outs, (whole, act, sem) = split_refs(mine, n_after, n_outs, refs)
    wide, narrow = coords()
    for x in range(2):
        n = narrow ^ (x * 2 + (0 if mine else 1))
        pltpu.make_async_copy(activated.at[n], act.at[x], sem.at[x]).start()
    for x in range(2):
        drain(act.at[x], sem.at[x])
        whole[...] = dot(d_ffn[...], act[x], TN)
        for y in range(2):
            for low in range(2):
                for high in range(2):
                    w = wide ^ (high * 4 + low * 2 + y)
                    for half in range(2):
                        rows = pl.ds(pl.multiple_of(w * 96 + half * 48, 16), 48)
                        first, second = (x, y) if half == 0 else (y, x)
                        rest = (second, low, high)
                        emit(mine, got, outs, half, first, rest, slice(0, 48), whole[rows, :])


def grad_red(mine, d_ffn, activated, got=None, after=()):
    scratch = [
        pltpu.VMEM((D, D), f32),
        pltpu.VMEM((2, ROWS, D), bf16),
        pltpu.SemaphoreType.DMA((2,)),
    ]
    operands, specs = (d_ffn, activated), [VMEM, HBM]
    return grad_call(
        grad_red_kernel, "grad_red", mine, operands, got, 1, (2, 2, 48, D), scratch, after, specs, 24
    )


def grad_exp_kernel(
    mine, n_after, n_outs, picks, d_inner, d_out, norms_one, norms_two, *refs
):
    got, outs, (whole, turned, norms, middle, context, sem) = split_refs(
        mine, n_after, n_outs, refs
    )
    wide, narrow = coords()
    step = pl.program_id(0)

    @pl.when(step == 0)
    def _():
        at = 0 if mine else 1
        pltpu.make_async_copy(picks.at[at], middle, sem.at[0]).start()
        pltpu.make_async_copy(picks.at[at + 2], context, sem.at[1]).start()
        drain(middle, sem.at[0])
        drain(context, sem.at[1])
        norms[0:2] = norms_one[...]
        norms[2:4] = norms_two[...]
        turned[...] = dot(d_out[...], context[...], TN)

    z = (wide // 2) ^ step
    whole[...] = dot(middle[...], d_inner[:, pl.ds(pl.multiple_of(z * D, D), D)], TN)
    low, high = step % 2, step // 2
    for y in range(2):
        w = wide ^ (step * 2 + y)
        lanes = pl.ds(pl.multiple_of((w % 2) * 384, 128), 384)
        blocks = packed(turned, w * 96, narrow)
        norm_lanes = pl.ds(pl.multiple_of(jnp.minimum(w, 5) * 128, 128), 128)
        for x in range(2):
            n = narrow ^ (x * 2 + (0 if mine else 1))
            for half in range(2):
                rows = pl.ds(pl.multiple_of((n // 2) * 192 + half * 96, 16), 96)
                first, second = (x, y) if half == 0 else (y, x)
                rest = (second, low, high)
                emit(mine, got, outs, half, first, rest, slice(0, 96), whole[rows, lanes])
            here = lax.broadcasted_iota(jnp.int32, (8, 128), 0) == n
            norm = jnp.sum(jnp.where(here, norms[:, norm_lanes], 0.0), axis=0, keepdims=True)
            norm = jnp.broadcast_to(norm, (16, 128))
            norm = jnp.concatenate([norm] * 3, 1)
            lower = jnp.concatenate([norm, blocks[x][32:]], 0)
            emit(mine, got, outs, 0, x, (y, low, high), slice(96, 128), blocks[x][:32])
            emit(mine, got, outs, 1, y, (x, low, high), slice(96, 128), lower)


def packed(turned, start, narrow):
    upper = pl.ds(pl.multiple_of(start, 16), 48)
    lower = pl.ds(pl.multiple_of(start + 48, 16), 48)
    tail_upper = turned[upper, 256:]
    tail_lower = turned[lower, 256:]
    tails = (
        jnp.concatenate([tail_upper[:, :64], tail_lower[:, :64]], 1),
        jnp.concatenate([tail_upper[:, 64:], tail_lower[:, 64:]], 1),
    )
    x_own = narrow // 2
    out = []
    for x in range(2):
        lanes = pl.ds(pl.multiple_of((x_own ^ x) * 128, 128), 128)
        tail = jnp.where(x_own == x, tails[0], tails[1])
        out.append(jnp.concatenate([turned[upper, lanes], turned[lower, lanes], tail], 1))
    return out


def unpacked(block):
    upper = jnp.concatenate([block[..., :128], block[..., 256:320]], -1)
    lower = jnp.concatenate([block[..., 128:256], block[..., 320:]], -1)
    return jnp.concatenate([upper, lower], -2)


def grad_exp(mine, picks, d_inner, d_out, norms, got=None, after=()):
    operands, specs = (picks, d_inner, d_out) + norms, [HBM]
    scratch = [
        pltpu.VMEM((384, D), f32),
        pltpu.VMEM((D, 384), f32),
        pltpu.VMEM((8, D), f32),
        pltpu.VMEM((ROWS, D // 2), bf16),
        pltpu.VMEM((ROWS, D // 2), bf16),
        pltpu.SemaphoreType.DMA((2,)),
    ]
    return grad_call(
        grad_exp_kernel, "grad_exp", mine, operands, got, 4, (2, 2, 128, 384), scratch, after, specs
    )


def grad_att_kernel(
    part, mine, n_after, n_outs, picked, d_to_words, d_to_ents, d_keys, d_values, *refs
):
    got, outs, (turned,) = split_refs(mine, n_after, n_outs, refs)
    wide, narrow = coords()
    work = (
        (d_keys, slice(0, ROWS), 0, 0),
        (d_to_words, slice(0, WORDS), 0, 1),
        (d_to_words, slice(WORDS, ROWS), 0, 2),
        (d_values, slice(0, ROWS), 1, 0),
        (d_to_ents, slice(0, WORDS), 1, 1),
        (d_to_ents, slice(WORDS, ROWS), 1, 2),
    )
    for ref, rows, half, at in work:
        turned[...] = dot(ref[rows, :], picked[rows, :], TN)
        for y in range(2):
            for low in range(2):
                w = (wide % 4) ^ (low * 2 + y)
                blocks = packed(turned, w * 96, narrow)
                for x in range(2):
                    first, second = (x, y) if half == 0 else (y, x)
                    where = slice(at * 48, at * 48 + 48)
                    emit(mine, got, outs, half, first, (second, low), where, blocks[x])


def grad_att(part, mine, picked, grads, got=None, after=()):
    kernel = functools.partial(grad_att_kernel, part)
    operands = (picked,) + tuple(grads)
    scratch = [pltpu.VMEM((D // 2, 384), f32)]
    return grad_call(
        kernel, "grad_att", mine, operands, got, 1, (2, 144, 384), scratch, after
    )


def grad_hidden_kernel(n_after, kv, q, *refs):
    grads, d_first = refs[:8], refs[8]
    word, ent, joined, first_here, sem = refs[9 + n_after :]
    step = pl.program_id(0)
    upper, lower = slice(0, WORDS), slice(WORDS, ROWS)
    late = pltpu.make_async_copy(d_first, first_here, sem)

    def both(kind):
        joined[:, : D // 2] = grads[kind][...]
        joined[:, D // 2 :] = grads[4 + kind][...]

    @pl.when(step == 0)
    def _():
        late.start()
        both(2)
        word[...] = dot(joined[upper], kv[...], NN)
        ent[...] = dot(joined[lower], kv[...], NN)

    @pl.when(step == 1)
    def _():
        both(3)
        word[...] += dot(joined[upper], kv[...], NN)
        ent[...] += dot(joined[lower], kv[...], NN)

    @pl.when(step == 2)
    def _():
        both(0)
        word[...] += dot(joined[upper], q[...], NN)

    @pl.when(step == 3)
    def _():
        ent[...] += dot(joined[lower], q[...], NN)

    @pl.when(step == 4)
    def _():
        both(1)
        late.wait()
        word[...] += first_here[upper] + dot(joined[upper], q[...], NN)

    @pl.when(step == 5)
    def _():
        ent[...] += first_here[lower] + dot(joined[lower], q[...], NN)


def grad_hidden(d_first, grads, kv, q, after=()):
    after = tokens(after)
    return pl.pallas_call(
        functools.partial(grad_hidden_kernel, len(after)),
        grid=(6,),
        in_specs=[
            pl.BlockSpec((None, D, D), lambda i: (jnp.minimum(i, 1), 0, 0)),
            pl.BlockSpec((None, D, D), lambda i: (jnp.maximum(i - 2, 0), 0, 0)),
        ]
        + [VMEM] * 8
        + [HBM]
        + [ANY] * len(after),
        out_specs=[VMEM] * 2,
        out_shape=[stored((WORDS, D), f32), stored((ENTS, D), f32)],
        scratch_shapes=[
            pltpu.VMEM((ROWS, D), bf16),
            pltpu.VMEM((ROWS, D), f32),
            pltpu.SemaphoreType.DMA,
        ],
        compiler_params=PARAMS,
        cost_estimate=cost(9),
        name="grad_hidden",
    )(kv, q, *grads, d_first, *after)


def flip(axis, bit, value):
    size = lax.axis_size(axis)
    return lax.ppermute(value, axis, [(i, i ^ bit) for i in range(size)])


def over(name, value):
    axis, bit = {
        "core": ("narrow", 1),
        "x": ("narrow", 2),
        "y": ("wide", 1),
        "low": ("wide", 2),
        "high": ("wide", 4),
    }[name]
    return flip(axis, bit, value)


class Links:
    def __init__(self):
        self.past = {}

    def send(self, name, value):
        kind = "z" if name in ("low", "high") else name
        past = self.past.setdefault(kind, [])
        if len(past) > 1:
            value, unused = lax.optimization_barrier((value, past[-2]))
        got = over(name, value)
        past.append(got)
        return got


def later(values, token):
    return lax.optimization_barrier((values, token))[0]


def gather_high(links, first, second):
    both = jnp.concatenate([first, second], 0)
    return both, links.send("high", both)


def gather_low(links, cut, both):
    both = jnp.stack(both, 0)
    got = links.send("low", both)
    left = jnp.stack([both[:, :cut], got[:, :cut]], 0)
    right = jnp.stack([both[:, cut:], got[:, cut:]], 0)
    return left, right


def gather_near(links, left, right, token=None):
    got_left = links.send("x", left)
    got_right = links.send("y", right)
    if token is not None:
        got_left, got_right = later((got_left, got_right), token)
    left = jnp.stack([left, got_left], 0)
    right = jnp.stack([right, got_right], 0)
    return left, right


def gather_far(links, left, right):
    return gather_core(left, right, links.send("y", left), links.send("x", right))


def gather_core(left, right, left_far, right_far):
    left = jnp.stack([left, left_far], 0)
    right = jnp.stack([right, right_far], 0)
    return left, over("core", left), right, over("core", right)


def plus(kept, got):
    return (kept.astype(f32) + got.astype(f32)).astype(bf16)


class Sum:
    def __init__(self, send_left, send_right, keep):
        self.keep = keep
        self.got = over("x", send_left), over("y", send_right)

    def wait(self, token):
        self.got = later(self.got, token) if isinstance(self.got, tuple) else later((self.got,), token)[0]
        return self

    def parts(self):
        left, right = self.got
        keep = self.keep
        return (
            plus(keep[0, 1], left[1]),
            plus(keep[1, 1], right[1]),
            (plus(keep[0, 0], left[0]), plus(keep[1, 0], right[0])),
        )

    def second(self):
        left, right, self.keep = self.parts()
        self.got = over("y", left), over("x", right)

    def near(self):
        left, right = self.got
        return plus(self.keep[0], left), plus(self.keep[1], right)


def flat(blocks, leading):
    return jnp.concatenate([v.reshape(v.shape[:leading] + (-1, 384)) for v in blocks], leading)


def gather_all(value):
    size = lax.axis_size("wide") * lax.axis_size("narrow")
    spread = jnp.broadcast_to(value[None], (size,) + value.shape)
    return lax.all_to_all(spread, ("wide", "narrow"), 0, 0, tiled=False)


def sum_all(value):
    return jnp.sum(gather_all(value), axis=0)


def adapt(weight, grad, first, second, decay):
    first = 0.5 * first + 0.5 * grad
    second = 0.5 * second + 0.5 * grad * grad
    fix_first = 1.0 - 0.5**STEP
    fix_second = 1.0 - 0.5**STEP
    update = first / fix_first / (jnp.sqrt(second / fix_second) + adam_eps) + decay * weight
    return (first, second, update)


def adapt_kernel(own, got, out_rows, weight, moment, square, others, first, second, update, payload):
    lane = lax.broadcasted_iota(jnp.int32, (1, 128), 1)
    row = jnp.where(lane == 7, others[0], jnp.where(lane == 8, others[1], 0.0))
    for k, (half, at) in enumerate(((0, 1), (1, 1), (0, 2), (1, 2), (0, 0), (1, 0), (0, 0))):
        if k < 6:
            rows = pl.ds(half * 144 + at * 48, 48)
            block = own[rows, :].astype(f32) + got[rows, :].astype(f32)
        else:
            block = out_rows[...]
        grad = unpacked(block).T
        new_first = 0.5 * moment[k] + 0.5 * grad
        new_second = 0.5 * square[k] + 0.5 * grad * grad
        fix = 1.0 - 0.5**STEP
        step = new_first / fix / (jnp.sqrt(new_second / fix) + adam_eps) + matrix_decay * weight[k]
        first[k] = new_first
        second[k] = new_second
        update[k] = step
        row = jnp.where(lane == k, jnp.sum(step * step), row)
    payload[...] = jnp.broadcast_to(row[None], payload.shape)


def adapt_attention(devices, own, got, out_rows, weight, moment, square, others):
    dims = weight.shape
    return pl.pallas_call(
        adapt_kernel,
        in_specs=[VMEM] * 6 + [SMEM],
        out_specs=[VMEM] * 4,
        out_shape=[
            stored(dims, f32),
            stored(dims, f32),
            kept(dims, f32),
            shape((devices, 1, 128), f32),
        ],
        compiler_params=PARAMS,
        cost_estimate=cost(3),
        name="adapt_attention",
    )(own, got, out_rows, weight, moment, square, others)


def apply_kernel(rates, att, exp, red, att_update, exp_update, red_update, *new):
    for k in range(7):
        new[0][k] = att[k] - rates[k] * att_update[k]
    new[1][...] = exp[...] - rates[7] * exp_update[...]
    new[2][...] = red[...] - rates[8] * red_update[...]


def apply_updates(rates, weights, updates):
    return pl.pallas_call(
        apply_kernel,
        in_specs=[SMEM] + [VMEM] * 6,
        out_specs=[VMEM] * 3,
        out_shape=[stored(w.shape, f32) for w in weights],
        compiler_params=PARAMS,
        name="apply_updates",
    )(rates, *weights, *updates)


def shards(
    fast,
    word_states,
    entity_states,
    seq_counts,
    attention_weight,
    expand_weight,
    reduce_weight,
    norm_params,
    moment_attention,
    moment_expand,
    moment_reduce,
    moment_norms,
    square_attention,
    square_expand,
    square_reduce,
    square_norms,
    word_cotangent,
    entity_cotangent,
):
    word, ent, counts = word_states[0], entity_states[0], seq_counts[0]
    core = lax.axis_index("narrow") % 2
    high = lax.axis_index("wide") // 4
    if fast:
        keep, send, exp_low, red_low, weight_local = prep(
            attention_weight, expand_weight, reduce_weight.T
        )
        got = over("core", send)
        rows = jnp.where(
            core == 0, jnp.concatenate([keep, got], 2), jnp.concatenate([got, keep], 2)
        )
        links = Links()
        kv = gather_high(links, rows[4], rows[5])
        query = gather_high(
            links,
            jnp.concatenate([rows[0], rows[2]], 0),
            jnp.concatenate([rows[1], rows[3]], 0),
        )
        kv = gather_low(links, 48, kv)
        query = gather_low(links, 96, query)
        kv = gather_near(links, *kv)
        kv_pieces = gather_far(links, *kv)
        query = gather_near(links, *query)
        query_far = links.send("y", query[0]), links.send("x", query[1])
        one = gather_high(
            links,
            jnp.concatenate([exp_low[:96], rows[6, :32]], 0),
            jnp.concatenate([exp_low[96:], rows[6, 32:]], 0),
        )
        one = gather_low(links, 128, one)
        kv_pieces = [v.reshape(v.shape[:4] + (1, 48, 384)) for v in kv_pieces]
    else:
        weight_local = jnp.concatenate(
            [
                jnp.sum(attention_weight * attention_weight, axis=(1, 2)),
                jnp.sum(expand_weight * expand_weight)[None],
                jnp.sum(reduce_weight * reduce_weight)[None],
            ]
        )
        turned = jnp.swapaxes(attention_weight.astype(bf16), 1, 2)
        turned = lax.all_gather(turned, "wide", axis=1, tiled=True)
        turned = lax.all_gather(turned, "narrow", axis=2, tiled=True)
        exp_all = lax.all_gather(expand_weight.astype(bf16), "wide", axis=1, tiled=True)
        exp_all = lax.all_gather(exp_all, "narrow", axis=0, tiled=True)
        red_all = lax.all_gather(reduce_weight.astype(bf16).T, "wide", axis=0, tiled=True)
        red_all = lax.all_gather(red_all, "narrow", axis=1, tiled=True)
        kv_pieces = query_pieces = [turned]
        one_pieces = [turned, exp_all]
        two_pieces = [red_all]
        one = two = (None, None)

    low, keys, values, low_mine, low_other, kv_all = project_kv(fast, word, ent, kv_pieces)
    if fast:
        query_pieces = gather_core(*query, *later(query_far, keys))
        query_pieces = [v.reshape(v.shape[:4] + (2, 48, 384)) for v in query_pieces]
        two = gather_high(links, *later((red_low[:48], red_low[48:]), keys))
        one = gather_near(links, *later(one, keys))
        one_far = links.send("y", one[0]), links.send("x", one[1])
    to_words, to_ents, q_all = project_q(fast, low, query_pieces, after=two)
    if fast:
        two = gather_low(links, 48, two)
    context, exact, lse = attend(counts, to_words, to_ents, keys, values, after=one + two)
    if fast:
        two = gather_near(links, *two, token=context)
        one_pieces = gather_core(*one, *later(one_far, two))
        two_far = links.send("y", two[0]), links.send("x", two[1])
        two_core = over("core", two[0]), over("core", two[1])
    (
        middle,
        middle_low,
        activated,
        slope,
        unit_one,
        picks,
        out_all,
        exp_all,
    ) = feed_in(fast, word, ent, context, norm_params, one_pieces, after=two)
    if fast:
        two_far = later(two_far, activated)
        two_pieces = (two[0], two_core[0], two[1], two_core[1])
        two_pieces += (two_far[0], over("core", two_far[0]), two_far[1], over("core", two_far[1]))
    word_out, ent_out, d_second, d_ffn, grads_two, red_all = feed_out(
        fast, activated, middle, norm_params, word_cotangent[0], entity_cotangent[0], two_pieces
    )
    got = red = exp = att_one = att_two = None
    if fast:
        got = over("core", grad_red(False, d_ffn, activated)[0])
    d_inner, d_first, d_out, d_context, row_inner, grads_one = feed_back(
        d_ffn, red_all, exp_all, slope, norm_params, d_second, unit_one, out_all, exact
    )
    if fast:
        red = Sum(*grad_red(True, d_ffn, activated, got, after=(d_first,)))
    exp_args = (d_inner, d_out)
    norm_args = (grads_one, grads_two)
    att_args = (counts, to_words, to_ents, keys, values, d_context, lse, row_inner)
    if fast:
        sent = grad_exp(False, picks, *exp_args, norm_args, after=(red.keep,))[0]
        got = over("core", sent)
    grads = attend_back(0, *att_args, after=(sent,) if fast else ())
    if fast:
        red.wait(grads[0]).second()
        exp = Sum(
            *grad_exp(True, picks, *exp_args, norm_args, got, after=red.keep)
        )
        sent = grad_att(0, False, low_other, grads, after=(exp.keep,))[0]
        got = over("core", sent)
    more = attend_back(3, *att_args, after=(sent,) if fast else ())
    if fast:
        red_near = red.wait(more[0]).near()
        exp.wait(more[0]).second()
        sent = grad_att(1, False, low_other, more, after=exp.keep + red_near)[0]
        got_two = over("core", sent)
        att_one = Sum(*grad_att(0, True, low_mine, grads, got, after=(sent,)))
        att_two = Sum(*grad_att(1, True, low_mine, more, got_two, after=(att_one.keep,)))
        exp_near = exp.wait(att_two.keep).near()
        near = flat(red_near + exp_near, 2)
        low_got = over("low", near[1])
    word_grad, ent_grad = grad_hidden(
        d_first, grads + more, kv_all, q_all, after=(att_two.keep,) if fast else ()
    )

    if fast:
        att_one.got, att_two.got = later((att_one.got, att_two.got), word_grad)
        one_left, one_right, one_keep = att_one.parts()
        two_left, two_right, two_keep = att_two.parts()
        left_got = over("y", jnp.concatenate([one_left, two_left], 1))
        right_got = over("x", jnp.concatenate([one_right, two_right], 1))
        near = plus(near[0], later(low_got, (two_left, two_right)))
        high_got = over("high", near[1])
        left = plus(jnp.concatenate([one_keep[0], two_keep[0]], 1), left_got)
        right = plus(jnp.concatenate([one_keep[1], two_keep[1]], 1), right_got)
        got = over("low", jnp.concatenate([left[1], right[1]], 0))
        att_low = plus(jnp.concatenate([left[0], right[0]], 0), got).reshape(2, 2, 144, 384)
        att_low = jnp.swapaxes(att_low, 0, 1).reshape(2, 288, 384)
        high_got = later(high_got, att_low)
        near = near[0].astype(f32) + high_got.astype(f32)
        red_sum = near[:192].reshape(2, 48, D)
        exp_sum = near[192:].reshape(2, 128, 384)
        norm_row = jnp.concatenate([exp_sum[1, 96, :128], jnp.pad(weight_local, (0, 119))])
        norm_rows = gather_all(norm_row)
        weight_total = jnp.sum(norm_rows[:, 128:137], axis=0)
        norm_grads = norm_rows[:, :128].reshape(8, 4, 128)[:6]
        norm_grads = jnp.swapaxes(norm_grads, 0, 1).reshape(4, D)
        first, second = att_low[0], att_low[1]
        got = over("high", jnp.where(high == 0, second, first))
        att_own = jnp.where(high == 0, first, second)
        out_rows = jnp.concatenate([exp_sum[0, 96:], exp_sum[1, 112:]], 0)
        exp_grad = jnp.concatenate([exp_sum[0, :96], exp_sum[1, :96]], 0)
        red_grad = jnp.concatenate([red_sum[0], red_sum[1]], 0)
    else:
        d_to_words, d_to_ents, d_keys, d_values = [
            jnp.concatenate([a, b], 1) for a, b in zip(grads, more)
        ]
        norm_grads = sum_all(jnp.concatenate([grads_one, grads_two], 0))
        weight_total = sum_all(weight_local)
        words, ents = low[:WORDS], low[WORDS:]
        turned = jnp.stack(
            [
                dot(d_to_words[:WORDS], words, TN),
                dot(d_to_ents[:WORDS], words, TN),
                dot(d_to_words[WORDS:], ents, TN),
                dot(d_to_ents[WORDS:], ents, TN),
                dot(d_keys, low, TN),
                dot(d_values, low, TN),
                dot(d_out, context, TN),
            ]
        ).astype(bf16)
        turned = lax.psum_scatter(turned, "wide", scatter_dimension=1, tiled=True)
        turned = lax.psum_scatter(turned, "narrow", scatter_dimension=2, tiled=True)
        att_grad = jnp.swapaxes(turned.astype(f32), 1, 2)
        grad = dot(middle_low, d_inner, TN).astype(bf16)
        grad = lax.psum_scatter(grad, "wide", scatter_dimension=1, tiled=True)
        grad = lax.psum_scatter(grad, "narrow", scatter_dimension=0, tiled=True)
        exp_grad = grad.astype(f32)
        activated = jnp.swapaxes(activated, 0, 1).reshape(ROWS, FF)
        grad = dot(d_ffn, activated, TN).astype(bf16)
        grad = lax.psum_scatter(grad, "wide", scatter_dimension=0, tiled=True)
        grad = lax.psum_scatter(grad, "narrow", scatter_dimension=1, tiled=True)
        red_grad = grad.astype(f32)

    exp_first, exp_second, exp_update = adapt(
        expand_weight, exp_grad, moment_expand, square_expand, matrix_decay
    )
    red_first, red_second, red_update = adapt(
        reduce_weight.T, red_grad, moment_reduce.T, square_reduce.T, matrix_decay
    )
    exp_square = jnp.sum(exp_update * exp_update)
    red_square = jnp.sum(red_update * red_update)
    if fast:
        att_first, att_second, att_update, payload = adapt_attention(
            lax.axis_size("wide") * lax.axis_size("narrow"),
            att_own,
            got,
            out_rows,
            attention_weight,
            moment_attention,
            square_attention,
            jnp.stack([exp_square, red_square]),
        )
        totals = lax.all_to_all(payload, ("wide", "narrow"), 0, 0, tiled=False)
        update_total = jnp.sum(totals, axis=(0, 1))[:9]
    else:
        att_first, att_second, att_update = adapt(
            attention_weight, att_grad, moment_attention, square_attention, matrix_decay
        )
        update_total = sum_all(
            jnp.concatenate(
                [
                    jnp.sum(att_update * att_update, axis=(1, 2)),
                    exp_square[None],
                    red_square[None],
                ]
            )
        )
    nrm_first, nrm_second, nrm_update = adapt(
        norm_params, norm_grads, moment_norms, square_norms, 0.0
    )
    weight_norm = jnp.sqrt(
        jnp.concatenate([weight_total, jnp.sum(norm_params * norm_params, axis=1)])
    )
    update_norm = jnp.sqrt(
        jnp.concatenate([update_total, jnp.sum(nrm_update * nrm_update, axis=1)])
    )
    trust = weight_norm / update_norm
    new_attention, new_expand, new_reduce = apply_updates(
        learn_rate * trust[:9],
        (attention_weight, expand_weight, reduce_weight.T),
        (att_update, exp_update, red_update),
    )
    new_reduce = new_reduce.T
    new_norms = norm_params - learn_rate * trust[9:13, None] * nrm_update
    trust_stats = jnp.stack([jnp.log(weight_norm), jnp.log(update_norm), jnp.log(trust)], 1)
    return (
        word_out[None],
        ent_out[None],
        word_grad[None],
        ent_grad[None],
        new_attention,
        new_expand,
        new_reduce,
        new_norms,
        att_first,
        exp_first,
        red_first.T,
        nrm_first,
        att_second,
        exp_second,
        red_second.T,
        nrm_second,
        trust_stats,
    )


def solution(mesh):
    fast = mesh.shape["wide"] == 8 and mesh.shape["narrow"] == 4
    rows = P(("wide", "narrow"), None, None)
    matrix = P("narrow", "wide")
    stack = P(None, "narrow", "wide")
    weights = (stack, matrix, matrix, P())
    return jax.shard_map(
        functools.partial(shards, fast),
        mesh=mesh,
        in_specs=(rows, rows, P(("wide", "narrow"), None)) + weights * 3 + (rows, rows),
        out_specs=(rows,) * 4 + weights * 3 + (P(),),
        check_vma=False,
    )
```

```python
import functools

import jax
import jax.numpy as jnp
from jax import lax
from jax.experimental import pallas as pl
from jax.experimental.pallas import tpu as pltpu
from jax.sharding import PartitionSpec as P

D = 768
FF = 3072
HEADS = 12
HEAD = 64
WORDS = 512
ENTS = 128
ROWS = WORDS + ENTS
STEP = 7

eps_norm = 1e-05
adam_eps = 1e-06
matrix_decay = 0.01
learn_rate = 0.5
masked_score = -1e30

f32 = jnp.float32
bf16 = jnp.bfloat16
NN = (((1,), (0,)), ((), ()))
NT = (((1,), (1,)), ((), ()))
TN = (((0,), (0,)), ((), ()))
VMEM = pl.BlockSpec(memory_space=pltpu.VMEM)
SMEM = pl.BlockSpec(memory_space=pltpu.SMEM)
ANY = pl.BlockSpec(memory_space=pl.ANY)
HBM = pl.BlockSpec(memory_space=pltpu.HBM)
COST_RATE = 4e9
PARAMS = pltpu.CompilerParams(vmem_limit_bytes=12 * 2**20)
WIDE = pltpu.CompilerParams(vmem_limit_bytes=28 * 2**20)


def dot(left, right, dims):
    return lax.dot_general(left, right, dims, preferred_element_type=f32)


def shape(dims, dtype):
    return jax.ShapeDtypeStruct(dims, dtype)


def kept(dims, dtype):
    return pltpu.VMEM(dims, dtype)


def stored(dims, dtype):
    return pltpu.HBM(dims, dtype)


def tokens(values):
    return [v for v in values if v is not None]


def cost(us, rate=COST_RATE):
    return pl.CostEstimate(flops=int(us * rate), bytes_accessed=0, transcendentals=0)


def away_blocks():
    for core in range(2):
        for outer in range(2):
            for lead in range(2):
                for low in range(2):
                    for high in range(2):
                        yield core, outer, lead, low, high


def places(wide, narrow, second, block):
    core, outer, lead, low, high = block
    x_away, y_away = (outer, lead) if second else (lead, outer)
    w = wide ^ (high * 4 + low * 2 + y_away)
    n = narrow ^ (x_away * 2 + core)
    return w, n


def piece_of(bufs, block):
    core, outer, lead, low, high = block
    return bufs[core].at[outer, lead, low, high]


def coords():
    return lax.axis_index("wide"), lax.axis_index("narrow")


def start_attention(bufs, second, target, slots, sem):
    wide, narrow = coords()
    for block in away_blocks():
        w, n = places(wide, narrow, second, block)
        row = pl.multiple_of(w * 96 + (n % 2) * 48, 16)
        lane = pl.multiple_of((n // 2) * 384, 128)
        src = piece_of(bufs, block)
        pltpu.make_async_copy(src, target.at[slots, pl.ds(row, 48), pl.ds(lane, 384)], sem).start()


def drain(ref, sem):
    pltpu.make_async_copy(ref, ref, sem).wait()


def prep_kernel(att, exp, red, keep, send, exp_low, red_low, sums):
    narrow = lax.axis_index("narrow")
    core = narrow % 2
    total = []
    for i in range(7):
        value = att[i]
        total.append(jnp.sum(value * value))
        turned = value.T.astype(bf16)
        halves = turned.reshape(2, 48, 192)

        @pl.when(core == 0)
        def _():
            keep[i] = halves[0]
            send[i] = halves[1]

        @pl.when(core == 1)
        def _():
            keep[i] = halves[1]
            send[i] = halves[0]

    value = exp[...]
    total.append(jnp.sum(value * value))
    exp_low[...] = value.astype(bf16)
    value = red[...]
    total.append(jnp.sum(value * value))
    red_low[...] = value.astype(bf16)
    for i in range(9):
        sums[i] = total[i]


def prep(att, exp, red):
    return pl.pallas_call(
        prep_kernel,
        in_specs=[VMEM] * 3,
        out_specs=[VMEM] * 4 + [SMEM],
        out_shape=[
            shape((7, 48, 192), bf16),
            shape((7, 48, 192), bf16),
            shape((192, 384), bf16),
            shape((96, D), bf16),
            shape((9,), f32),
        ],
        compiler_params=pltpu.CompilerParams(vmem_limit_bytes=60 * 2**20),
        name="prep",
    )(att, exp, red)


def pick_rows(source, mine, other):
    core = lax.axis_index("narrow") % 2
    for c in range(2):

        @pl.when(core == c)
        def _():
            for target, at in ((mine, c * 192), (other, 192 - c * 192)):
                target[:, :192] = source[:, at : at + 192]
                target[:, 192:] = source[:, at + 384 : at + 576]


def pick_tiles(source, mine, other):
    core = lax.axis_index("narrow") % 2
    for c in range(2):

        @pl.when(core == c)
        def _():
            for target, at in ((mine, c * 192), (other, 192 - c * 192)):
                target[:, :128] = source[:, at : at + 128]
                target[:, 128:256] = source[:, at + 384 : at + 512]
                target[:, 256:320] = source[:, at + 128 : at + 192]
                target[:, 320:] = source[:, at + 512 : at + 576]


def project_kv_kernel(fast, n_after, word, ent, *refs):
    if fast:
        first, second, refs = refs[:2], refs[2:4], refs[4:]
    else:
        whole, refs = refs[0], refs[1:]
    low, keys, values, mine, other, saved, target, sem, sem_save = refs[n_after:]
    if fast:
        start_attention(first, False, target, pl.ds(0, 1), sem)
        start_attention(second, True, target, pl.ds(1, 1), sem)
    else:
        pltpu.make_async_copy(whole.at[pl.ds(4, 2)], target, sem).start()
    low[:WORDS] = word[...].astype(bf16)
    low[WORDS:] = ent[...].astype(bf16)
    pick_tiles(low, mine, other)
    drain(target, sem)
    save = pltpu.make_async_copy(target, saved, sem_save)
    save.start()
    keys[...] = dot(low[...], target[0], NT).astype(bf16)
    values[...] = dot(low[...], target[1], NT).astype(bf16)
    save.wait()


def project_kv(fast, word, ent, pieces, after=()):
    after = tokens(after)
    return pl.pallas_call(
        functools.partial(project_kv_kernel, fast, len(after)),
        in_specs=[VMEM, VMEM] + [ANY] * (len(pieces) + len(after)),
        out_specs=[VMEM] * 5 + [HBM],
        out_shape=[kept((ROWS, D), bf16)] * 3
        + [stored((ROWS, D // 2), bf16)] * 2
        + [stored((2, D, D), bf16)],
        scratch_shapes=[
            pltpu.VMEM((2, D, D), bf16),
            pltpu.SemaphoreType.DMA,
            pltpu.SemaphoreType.DMA,
        ],
        compiler_params=PARAMS,
        cost_estimate=cost(6, 4e8),
        name="project_kv",
    )(word, ent, *pieces, *after)


def project_q_kernel(fast, n_after, low, *refs):
    if fast:
        first, second, refs = refs[:2], refs[2:4], refs[4:]
    else:
        whole, refs = refs[0], refs[1:]
    to_words, to_ents, saved, target, sem, sem_save = refs[n_after:]
    if fast:
        start_attention(first, False, target, pl.ds(0, 2), sem)
        start_attention(second, True, target, pl.ds(2, 2), sem)
    else:
        for slot, k in enumerate((0, 2, 1, 3)):
            pltpu.make_async_copy(whole.at[k], target.at[slot], sem).start()
    drain(target, sem)
    save = pltpu.make_async_copy(target, saved, sem_save)
    save.start()
    scale = HEAD ** (-0.5)
    word = low[:WORDS]
    ent = low[WORDS:]
    to_words[:WORDS] = (dot(word, target[0], NT) * scale).astype(bf16)
    to_words[WORDS:] = (dot(ent, target[1], NT) * scale).astype(bf16)
    to_ents[:WORDS] = (dot(word, target[2], NT) * scale).astype(bf16)
    to_ents[WORDS:] = (dot(ent, target[3], NT) * scale).astype(bf16)
    save.wait()


def project_q(fast, low, pieces, after=()):
    after = tokens(after)
    return pl.pallas_call(
        functools.partial(project_q_kernel, fast, len(after)),
        in_specs=[VMEM] + [ANY] * (len(pieces) + len(after)),
        out_specs=[VMEM] * 2 + [HBM],
        out_shape=[kept((ROWS, D), bf16)] * 2 + [stored((4, D, D), bf16)],
        scratch_shapes=[
            pltpu.VMEM((4, D, D), bf16),
            pltpu.SemaphoreType.DMA,
            pltpu.SemaphoreType.DMA,
        ],
        compiler_params=PARAMS,
        cost_estimate=cost(7, 4e8),
        name="project_q",
    )(low, *pieces, *after)


def head_masks(counts):
    lane = lax.broadcasted_iota(jnp.int32, (ROWS, 128), 1)
    row = lax.broadcasted_iota(jnp.int32, (ROWS, 128), 0)
    edge = jnp.where(row < WORDS, counts[0], counts[1] + WORDS)
    bias = jnp.where(row < edge, 0.0, masked_score)
    out = []
    for h in range(2):
        own = jnp.where((lane < HEAD) if h == 0 else (lane >= HEAD), 1.0, 0.0).astype(bf16)
        mark = jnp.where(lane == (HEAD if h == 0 else 0), 1.0, 0.0)
        rest = (1.0 - mark).astype(bf16)
        tag = (bias * mark).astype(bf16)
        out.append((own, mark.astype(bf16), rest, tag))
    return out


def scores_of(masks, keys, to_words, to_ents):
    own, mark, rest, tag = masks
    tagged = keys * own + tag
    upper = dot(tagged[:WORDS], to_words * rest + mark, NT)
    lower = dot(tagged[WORDS:], to_ents * rest + mark, NT)
    return jnp.concatenate([upper, lower], 0)


def attend_kernel(n_after, counts, to_words, to_ents, keys, values, *refs):
    context, exact, lse = refs[n_after:]
    masks = head_masks(counts)
    pair = pl.program_id(0)
    lanes = pl.ds(pl.multiple_of(pair * 128, 128), 128)
    key, value = keys[:, lanes], values[:, lanes]
    outs = []
    for h in range(2):
        scores = scores_of(masks[h], key, to_words[:, lanes], to_ents[:, lanes])
        top = jnp.max(scores, axis=0, keepdims=True)
        expd = jnp.exp(scores - top)
        total = jnp.sum(expd, axis=0, keepdims=True)
        lse[pair, h : h + 1, :] = top + jnp.log(total)
        mixed = dot(value[:, h * HEAD : (h + 1) * HEAD], expd.astype(bf16), TN)
        outs.append(mixed * (1.0 / total))
    joined = jnp.concatenate(outs, 0).T
    exact[...] = joined
    context[:, lanes] = joined.astype(bf16)


def attend(counts, to_words, to_ents, keys, values, after=()):
    after = tokens(after)
    return pl.pallas_call(
        functools.partial(attend_kernel, len(after)),
        grid=(HEADS // 2,),
        in_specs=[SMEM] + [VMEM] * 4 + [ANY] * len(after),
        out_specs=[VMEM, pl.BlockSpec((ROWS, 128), lambda i: (0, i)), VMEM],
        out_shape=[
            kept((ROWS, D), bf16),
            stored((ROWS, D), f32),
            kept((HEADS // 2, 2, ROWS), f32),
        ],
        compiler_params=PARAMS,
        cost_estimate=cost(12, 4e8),
        name="attend",
    )(counts, to_words, to_ents, keys, values, *after)


def normed(value):
    center = value - jnp.mean(value, axis=-1, keepdims=True)
    spread = jnp.mean(center * center, axis=-1, keepdims=True)
    inverse = lax.rsqrt(spread + eps_norm)
    return center * inverse, inverse


def normed_back(unit, inverse, cotangent):
    mean = jnp.mean(cotangent, axis=-1, keepdims=True)
    inner = jnp.mean(cotangent * unit, axis=-1, keepdims=True)
    return inverse * (cotangent - mean - unit * inner)


def column_sum(value):
    return jnp.sum(value, axis=0, keepdims=True)


def feed_in_kernel(fast, n_after, word, ent, context, norms, *refs):
    if fast:
        bufs, refs = (refs[0:2], refs[2:4]), refs[4:]
    else:
        bufs, refs = refs[0:2], refs[2:]
    (
        middle_saved,
        middle_low,
        act_saved,
        slope_saved,
        unit_saved,
        picks_saved,
        out_saved,
        exp_saved,
        middle,
        activated,
        slope,
        unit_here,
        picks,
        out_all,
        exp_all,
        sem_out,
        sem_exp,
        sem_save,
    ) = refs[n_after:]
    step = pl.program_id(0)
    pairs = (
        (unit_here, unit_saved),
        (picks, picks_saved),
        (out_all, out_saved),
        (middle, middle_saved),
    )
    saves = [pltpu.make_async_copy(*pair, sem_save.at[i]) for i, pair in enumerate(pairs)]

    @pl.when(step == 0)
    def _():
        if fast:
            start_feed_in(bufs, out_all, exp_all, sem_out, sem_exp)
        else:
            pltpu.make_async_copy(bufs[0].at[6], out_all, sem_out).start()
            for j in range(4):
                cols = pl.ds(j * D, D)
                pltpu.make_async_copy(bufs[1].at[:, cols], exp_all.at[j], sem_exp.at[j]).start()
        drain(out_all, sem_out)
        saves[2].start()
        hidden = jnp.concatenate([word[...], ent[...]], 0)
        unit, inverse = normed(hidden + dot(context[...], out_all[...], NT))
        value = unit * norms[0:1, :] + norms[1:2, :]
        unit_here[:, :D] = unit
        unit_here[:, D:] = jnp.broadcast_to(inverse, (ROWS, 128))
        saves[0].start()
        middle_low[...] = value.astype(bf16)
        middle[...] = value
        saves[3].start()
        pick_rows(middle_low, picks.at[0], picks.at[1])
        pick_tiles(context, picks.at[2], picks.at[3])
        saves[1].start()

    drain(exp_all.at[step], sem_exp.at[step])
    pltpu.make_async_copy(exp_all.at[step], exp_saved.at[step], sem_save.at[4 + step]).start()
    inner = dot(middle_low[...], exp_all[step], NN)
    share = 0.5 + 0.5 * lax.erf(inner * 0.7071067811865476)
    bell = jnp.exp(-0.5 * inner * inner) * 0.3989422804014327
    slope[step] = (share + inner * bell).astype(bf16)
    activated[step] = (inner * share).astype(bf16)
    pltpu.make_async_copy(slope.at[step], slope_saved.at[step], sem_save.at[8 + step]).start()
    pltpu.make_async_copy(activated.at[step], act_saved.at[step], sem_save.at[12 + step]).start()

    @pl.when(step == 3)
    def _():
        for save in saves:
            save.wait()
        for j in range(4):
            pltpu.make_async_copy(exp_all.at[j], exp_saved.at[j], sem_save.at[4 + j]).wait()
            pltpu.make_async_copy(slope.at[j], slope_saved.at[j], sem_save.at[8 + j]).wait()
            pltpu.make_async_copy(activated.at[j], act_saved.at[j], sem_save.at[12 + j]).wait()


def start_feed_in(bufs, out_all, exp_all, sem_out, sem_exp):
    wide, narrow = coords()
    for half in range(2):
        skip, count = ((0, 32), (32, 16))[half]
        for block in away_blocks():
            w, n = places(wide, narrow, half == 1, block)
            row = pl.multiple_of(w * 96 + (n % 2) * 48 + skip, 16)
            lane = pl.multiple_of((n // 2) * 384, 128)
            src = piece_of(bufs[half], block).at[pl.ds(96, count)]
            dst = out_all.at[pl.ds(row, count), pl.ds(lane, 384)]
            pltpu.make_async_copy(src, dst, sem_out).start()
    for half in range(2):
        for block in away_blocks():
            w, n = places(wide, narrow, half == 1, block)
            src = piece_of(bufs[half], block).at[pl.ds(0, 96)]
            row = pl.multiple_of(n * 192 + half * 96, 16)
            lane = pl.multiple_of((w % 2) * 384, 128)
            dst = exp_all.at[w // 2, pl.ds(row, 96), pl.ds(lane, 384)]
            pltpu.make_async_copy(src, dst, sem_exp.at[w // 2]).start()


def feed_in(fast, word, ent, context, norms, pieces, after=()):
    after = tokens(after)
    return pl.pallas_call(
        functools.partial(feed_in_kernel, fast, len(after)),
        grid=(4,),
        in_specs=[VMEM] * 4 + [ANY] * (len(pieces) + len(after)),
        out_specs=[HBM, VMEM] + [HBM] * 6,
        out_shape=[
            stored((ROWS, D), f32),
            kept((ROWS, D), bf16),
            stored((4, ROWS, D), bf16),
            stored((4, ROWS, D), bf16),
            stored((ROWS, D + 128), f32),
            stored((4, ROWS, D // 2), bf16),
            stored((D, D), bf16),
            stored((4, D, D), bf16),
        ],
        scratch_shapes=[
            pltpu.VMEM((ROWS, D), f32),
            pltpu.VMEM((4, ROWS, D), bf16),
            pltpu.VMEM((4, ROWS, D), bf16),
            pltpu.VMEM((ROWS, D + 128), f32),
            pltpu.VMEM((4, ROWS, D // 2), bf16),
            pltpu.VMEM((D, D), bf16),
            pltpu.VMEM((4, D, D), bf16),
            pltpu.SemaphoreType.DMA,
            pltpu.SemaphoreType.DMA((4,)),
            pltpu.SemaphoreType.DMA((16,)),
        ],
        compiler_params=pltpu.CompilerParams(vmem_limit_bytes=28 * 2**20),
        cost_estimate=cost(0),
        name="feed_in",
    )(word, ent, context, norms, *pieces, *after)


def feed_out_kernel(fast, n_after, norms, activated, middle, word_cot, ent_cot, *refs):
    if fast:
        bufs, refs = (refs[0:2], refs[2:4], refs[4:6], refs[6:8]), refs[8:]
    else:
        bufs, refs = refs[0:1], refs[1:]
    (
        word_out,
        ent_out,
        second_saved,
        d_ffn,
        grads_two,
        red_saved,
        total,
        cot_here,
        middle_here,
        d_second,
        act_here,
        red_all,
        sem_red,
        sem_act,
        sem_save,
        sem_late,
    ) = refs[n_after:]
    step = pl.program_id(0)
    upper, lower = pl.ds(0, WORDS), pl.ds(WORDS, ENTS)
    late = (
        pltpu.make_async_copy(word_cot, cot_here.at[upper], sem_late.at[0]),
        pltpu.make_async_copy(ent_cot, cot_here.at[lower], sem_late.at[1]),
        pltpu.make_async_copy(middle, middle_here, sem_late.at[2]),
    )
    saves = (
        pltpu.make_async_copy(total.at[upper], word_out, sem_save.at[0]),
        pltpu.make_async_copy(total.at[lower], ent_out, sem_save.at[1]),
        pltpu.make_async_copy(d_second, second_saved, sem_save.at[2]),
    )

    @pl.when(step == 0)
    def _():
        if fast:
            start_feed_out(bufs, red_all, sem_red, activated, act_here, sem_act)
        else:
            for j in range(4):
                pltpu.make_async_copy(activated.at[j], act_here.at[j], sem_act.at[j]).start()
                cols = pl.ds(j * D, D)
                pltpu.make_async_copy(bufs[0].at[:, cols], red_all.at[j], sem_red.at[j]).start()
        for copy in late:
            copy.start()

    n = coords()[1] ^ step if fast else step
    drain(act_here.at[n], sem_act.at[n])
    drain(red_all.at[n], sem_red.at[n])
    pltpu.make_async_copy(red_all.at[n], red_saved.at[n], sem_save.at[3 + n]).start()
    part = dot(act_here[n], red_all[n], NT)

    @pl.when(step == 0)
    def _():
        total[...] = part

    @pl.when(step > 0)
    def _():
        total[...] += part

    @pl.when(step == 3)
    def _():
        for copy in late:
            copy.wait()
        unit, inverse = normed(total[...] + middle_here[...])
        total[...] = unit * norms[2:3, :] + norms[3:4, :]
        saves[0].start()
        saves[1].start()
        cot = cot_here[...]
        back = normed_back(unit, inverse, cot * norms[2:3, :])
        d_second[...] = back
        saves[2].start()
        d_ffn[...] = back.astype(bf16)
        grads_two[0:1, :] = column_sum(cot * unit)
        grads_two[1:2, :] = column_sum(cot)
        for save in saves:
            save.wait()
        for j in range(4):
            pltpu.make_async_copy(red_all.at[j], red_saved.at[j], sem_save.at[3 + j]).wait()


def start_feed_out(bufs, red_all, sem_red, activated, act_here, sem_act):
    wide, narrow = coords()
    for away in range(4):
        n = narrow ^ away
        pltpu.make_async_copy(activated.at[n], act_here.at[n], sem_act.at[n]).start()
        for half in range(2):
            for block in away_blocks():
                core, outer, lead, low, high = block
                if (outer if half else lead) * 2 + core != away:
                    continue
                w, n = places(wide, narrow, half == 1, block)
                src = bufs[half + 2 * outer][core].at[lead, low, high]
                row = pl.multiple_of(w * 96 + half * 48, 16)
                pltpu.make_async_copy(src, red_all.at[n, pl.ds(row, 48)], sem_red.at[n]).start()


def feed_out(fast, activated, middle, norms, word_cot, ent_cot, pieces, after=()):
    after = tokens(after)
    return pl.pallas_call(
        functools.partial(feed_out_kernel, fast, len(after)),
        grid=(4,),
        in_specs=[VMEM] + [HBM] * 4 + [ANY] * (len(pieces) + len(after)),
        out_specs=[HBM] * 3 + [VMEM] * 2 + [HBM],
        out_shape=[
            stored((WORDS, D), f32),
            stored((ENTS, D), f32),
            stored((ROWS, D), f32),
            kept((ROWS, D), bf16),
            kept((2, D), f32),
            stored((4, D, D), bf16),
        ],
        scratch_shapes=[
            pltpu.VMEM((ROWS, D), f32),
            pltpu.VMEM((ROWS, D), f32),
            pltpu.VMEM((ROWS, D), f32),
            pltpu.VMEM((ROWS, D), f32),
            pltpu.VMEM((4, ROWS, D), bf16),
            pltpu.VMEM((4, D, D), bf16),
            pltpu.SemaphoreType.DMA((4,)),
            pltpu.SemaphoreType.DMA((4,)),
            pltpu.SemaphoreType.DMA((7,)),
            pltpu.SemaphoreType.DMA((3,)),
        ],
        compiler_params=pltpu.CompilerParams(vmem_limit_bytes=56 * 2**20),
        cost_estimate=cost(12),
        name="feed_out",
    )(norms, activated, middle, word_cot, ent_cot, *pieces, *after)


def feed_back_kernel(
    n_after, d_ffn, norms, red_all, exp_all, slope, d_second, unit_one, out_all, exact, *refs
):
    (
        d_inner,
        d_first,
        d_out,
        d_context,
        row_inner,
        grads_one,
        total,
        red_here,
        exp_here,
        slope_here,
        second_here,
        unit_here,
        out_here,
        exact_here,
        sem_step,
        sem_late,
        sem_save,
    ) = refs[n_after:]
    step = pl.program_id(0)
    pairs = (
        (d_second, second_here),
        (unit_one, unit_here),
        (out_all, out_here),
        (exact, exact_here),
    )
    late = [pltpu.make_async_copy(*pair, sem_late.at[i]) for i, pair in enumerate(pairs)]
    save = pltpu.make_async_copy(total, d_first, sem_save)
    parts = ((red_all, red_here), (slope, slope_here), (exp_all, exp_here))

    @pl.when(step == 0)
    def _():
        for j in range(4):
            for k, (there, here) in enumerate(parts):
                pltpu.make_async_copy(there.at[j], here.at[j], sem_step.at[k, j]).start()
        for copy in late:
            copy.start()

    drain(red_here.at[step], sem_step.at[0, step])
    drain(slope_here.at[step], sem_step.at[1, step])
    drain(exp_here.at[step], sem_step.at[2, step])
    lanes = pl.ds(pl.multiple_of(step * D, D), D)
    back = (dot(d_ffn[...], red_here[step], NN) * slope_here[step].astype(f32)).astype(bf16)
    d_inner[:, lanes] = back
    part = dot(back, exp_here[step], NT)

    @pl.when(step == 0)
    def _():
        total[...] = part

    @pl.when(step > 0)
    def _():
        total[...] += part

    @pl.when(step == 3)
    def _():
        for copy in late:
            copy.wait()
        d_middle = total[...] + second_here[...]
        unit = unit_here[:, :D]
        grads_one[0:1, :] = column_sum(d_middle * unit)
        grads_one[1:2, :] = column_sum(d_middle)
        first = normed_back(unit, unit_here[:, D : D + 1], d_middle * norms[0:1, :])
        total[...] = first
        save.start()
        low_first = first.astype(bf16)
        d_out[...] = low_first
        context = dot(low_first, out_here[...], NN).astype(bf16)
        d_context[...] = context
        product = context.astype(f32) * exact_here[...]
        head = lax.broadcasted_iota(jnp.int32, (16, D), 1) // HEAD
        pick = jnp.where(head == lax.broadcasted_iota(jnp.int32, (16, D), 0), 1.0, 0.0).astype(bf16)
        high = product.astype(bf16)
        low = (product - high.astype(f32)).astype(bf16)
        sums = dot(pick, high, NT) + dot(pick, low, NT)
        for i in range(HEADS // 2):
            row_inner[i] = sums[2 * i : 2 * i + 2]
        save.wait()


def feed_back(d_ffn, red_all, exp_all, slope, norms, d_second, unit_one, out_all, exact, after=()):
    after = tokens(after)
    return pl.pallas_call(
        functools.partial(feed_back_kernel, len(after)),
        grid=(4,),
        in_specs=[VMEM, VMEM] + [HBM] * 7 + [ANY] * len(after),
        out_specs=[VMEM, HBM] + [VMEM] * 4,
        out_shape=[
            kept((ROWS, FF), bf16),
            stored((ROWS, D), f32),
            kept((ROWS, D), bf16),
            kept((ROWS, D), bf16),
            kept((HEADS // 2, 2, ROWS), f32),
            kept((2, D), f32),
        ],
        scratch_shapes=[
            pltpu.VMEM((ROWS, D), f32),
            pltpu.VMEM((4, D, D), bf16),
            pltpu.VMEM((4, D, D), bf16),
            pltpu.VMEM((4, ROWS, D), bf16),
            pltpu.VMEM((ROWS, D), f32),
            pltpu.VMEM((ROWS, D + 128), f32),
            pltpu.VMEM((D, D), bf16),
            pltpu.VMEM((ROWS, D), f32),
            pltpu.SemaphoreType.DMA((3, 4)),
            pltpu.SemaphoreType.DMA((4,)),
            pltpu.SemaphoreType.DMA,
        ],
        compiler_params=pltpu.CompilerParams(vmem_limit_bytes=36 * 2**20),
        cost_estimate=cost(14),
        name="feed_back",
    )(d_ffn, norms, red_all, exp_all, slope, d_second, unit_one, out_all, exact, *after)


def attend_back_kernel(
    first, n_after, counts, to_words, to_ents, keys, values, d_context, lse, row_inner, *refs
):
    d_to_words, d_to_ents, d_keys, d_values = refs[n_after:]
    masks = head_masks(counts)
    scale = HEAD ** (-0.5)
    step = pl.program_id(0)
    pair = step + first
    lanes = pl.ds(pl.multiple_of(pair * 128, 128), 128)
    here = pl.ds(pl.multiple_of(step * 128, 128), 128)
    word_query, ent_query = to_words[...], to_ents[...]
    key, value, d_mixed = keys[...], values[...], d_context[:, lanes]
    one, two, three, four = [], [], [], []
    for h in range(2):
        cols = slice(h * HEAD, (h + 1) * HEAD)
        scores = scores_of(masks[h], key, word_query, ent_query)
        probs = jnp.exp(scores - lse[pair, h : h + 1, :])
        d_probs = dot(value * masks[h][0], d_mixed, NT)
        d_scores = (probs * (d_probs - row_inner[pair, h : h + 1, :])).astype(bf16)
        one.append(dot(key[:WORDS, cols], d_scores[:WORDS], TN))
        two.append(dot(key[WORDS:, cols], d_scores[WORDS:], TN))
        three.append(
            jnp.concatenate(
                [
                    dot(d_scores[:WORDS], word_query[:, cols], NN),
                    dot(d_scores[WORDS:], ent_query[:, cols], NN),
                ],
                0,
            )
        )
        four.append(dot(probs.astype(bf16), d_mixed[:, cols], NN))
    d_to_words[:, here] = (jnp.concatenate(one, 0).T * scale).astype(bf16)
    d_to_ents[:, here] = (jnp.concatenate(two, 0).T * scale).astype(bf16)
    d_keys[:, here] = jnp.concatenate(three, 1).astype(bf16)
    d_values[:, here] = jnp.concatenate(four, 1).astype(bf16)


def attend_back(first, counts, to_words, to_ents, keys, values, d_context, lse, row_inner, after=()):
    after = tokens(after)
    pair = pl.BlockSpec((ROWS, 128), lambda i: (0, i + first))
    return pl.pallas_call(
        functools.partial(attend_back_kernel, first, len(after)),
        grid=(HEADS // 4,),
        in_specs=[SMEM] + [pair] * 4 + [VMEM] * 3 + [ANY] * len(after),
        out_specs=[VMEM] * 4,
        out_shape=[(stored if first else kept)((ROWS, D // 2), bf16)] * 4,
        compiler_params=PARAMS,
        cost_estimate=cost(10),
        name="attend_back",
    )(counts, to_words, to_ents, keys, values, d_context, lse, row_inner, *after)


def relative():
    for x in range(2):
        for y in range(2):
            for low in range(2):
                for high in range(2):
                    yield x, y, low, high


def emit(mine, got, outs, half, first, rest, rows, value):
    if not mine:
        outs[0][(half, first) + rest + (rows,)] = value.astype(bf16)
        return
    value = (value + got[(half, first) + rest + (rows,)].astype(f32)).astype(bf16)
    if first:
        outs[half][rest + (rows,)] = value
    else:
        outs[2][(half,) + rest + (rows,)] = value


def grad_call(kernel, name, mine, operands, got, steps, dims, extra, after, specs=(), limit=12):
    after = tokens(after)
    if mine:
        outs = [kept((2,) + dims, bf16)] * 2 + [kept((2, 2) + dims, bf16)]
        operands = list(operands) + [got]
    else:
        outs = [kept((2, 2, 2) + dims, bf16)]
    return pl.pallas_call(
        functools.partial(kernel, mine, len(after), len(outs)),
        grid=(steps,),
        in_specs=list(specs)
        + [VMEM] * (len(operands) - len(specs))
        + [ANY] * len(after),
        out_specs=[VMEM] * len(outs),
        out_shape=outs,
        scratch_shapes=extra,
        compiler_params=pltpu.CompilerParams(vmem_limit_bytes=limit * 2**20),
        cost_estimate=cost(7),
        name=name,
    )(*operands, *after)


def split_refs(mine, n_after, n_outs, refs):
    got, refs = (refs[0], refs[1:]) if mine else (None, refs)
    refs = refs[n_after:]
    return got, refs[:n_outs], refs[n_outs:]


def grad_red_kernel(mine, n_after, n_outs, d_ffn, activated, *refs):
    got, outs, (whole, act, sem) = split_refs(mine, n_after, n_outs, refs)
    wide, narrow = coords()
    for x in range(2):
        n = narrow ^ (x * 2 + (0 if mine else 1))
        pltpu.make_async_copy(activated.at[n], act.at[x], sem.at[x]).start()
    for x in range(2):
        drain(act.at[x], sem.at[x])
        whole[...] = dot(d_ffn[...], act[x], TN)
        for y in range(2):
            for low in range(2):
                for high in range(2):
                    w = wide ^ (high * 4 + low * 2 + y)
                    for half in range(2):
                        rows = pl.ds(pl.multiple_of(w * 96 + half * 48, 16), 48)
                        first, second = (x, y) if half == 0 else (y, x)
                        rest = (second, low, high)
                        emit(mine, got, outs, half, first, rest, slice(0, 48), whole[rows, :])


def grad_red(mine, d_ffn, activated, got=None, after=()):
    scratch = [
        pltpu.VMEM((D, D), f32),
        pltpu.VMEM((2, ROWS, D), bf16),
        pltpu.SemaphoreType.DMA((2,)),
    ]
    operands, specs = (d_ffn, activated), [VMEM, HBM]
    return grad_call(
        grad_red_kernel, "grad_red", mine, operands, got, 1, (2, 2, 48, D), scratch, after, specs, 24
    )


def grad_exp_kernel(
    mine, n_after, n_outs, picks, d_inner, d_out, norms_one, norms_two, *refs
):
    got, outs, (whole, turned, norms, middle, context, sem) = split_refs(
        mine, n_after, n_outs, refs
    )
    wide, narrow = coords()
    step = pl.program_id(0)

    @pl.when(step == 0)
    def _():
        at = 0 if mine else 1
        pltpu.make_async_copy(picks.at[at], middle, sem.at[0]).start()
        pltpu.make_async_copy(picks.at[at + 2], context, sem.at[1]).start()
        drain(middle, sem.at[0])
        drain(context, sem.at[1])
        norms[0:2] = norms_one[...]
        norms[2:4] = norms_two[...]
        turned[...] = dot(d_out[...], context[...], TN)

    z = (wide // 2) ^ step
    whole[...] = dot(middle[...], d_inner[:, pl.ds(pl.multiple_of(z * D, D), D)], TN)
    low, high = step % 2, step // 2
    for y in range(2):
        w = wide ^ (step * 2 + y)
        lanes = pl.ds(pl.multiple_of((w % 2) * 384, 128), 384)
        blocks = packed(turned, w * 96, narrow)
        norm_lanes = pl.ds(pl.multiple_of(jnp.minimum(w, 5) * 128, 128), 128)
        for x in range(2):
            n = narrow ^ (x * 2 + (0 if mine else 1))
            for half in range(2):
                rows = pl.ds(pl.multiple_of((n // 2) * 192 + half * 96, 16), 96)
                first, second = (x, y) if half == 0 else (y, x)
                rest = (second, low, high)
                emit(mine, got, outs, half, first, rest, slice(0, 96), whole[rows, lanes])
            here = lax.broadcasted_iota(jnp.int32, (8, 128), 0) == n
            norm = jnp.sum(jnp.where(here, norms[:, norm_lanes], 0.0), axis=0, keepdims=True)
            norm = jnp.broadcast_to(norm, (16, 128))
            norm = jnp.concatenate([norm] * 3, 1)
            lower = jnp.concatenate([norm, blocks[x][32:]], 0)
            emit(mine, got, outs, 0, x, (y, low, high), slice(96, 128), blocks[x][:32])
            emit(mine, got, outs, 1, y, (x, low, high), slice(96, 128), lower)


def packed(turned, start, narrow):
    upper = pl.ds(pl.multiple_of(start, 16), 48)
    lower = pl.ds(pl.multiple_of(start + 48, 16), 48)
    tail_upper = turned[upper, 256:]
    tail_lower = turned[lower, 256:]
    tails = (
        jnp.concatenate([tail_upper[:, :64], tail_lower[:, :64]], 1),
        jnp.concatenate([tail_upper[:, 64:], tail_lower[:, 64:]], 1),
    )
    x_own = narrow // 2
    out = []
    for x in range(2):
        lanes = pl.ds(pl.multiple_of((x_own ^ x) * 128, 128), 128)
        tail = jnp.where(x_own == x, tails[0], tails[1])
        out.append(jnp.concatenate([turned[upper, lanes], turned[lower, lanes], tail], 1))
    return out


def unpacked(block):
    upper = jnp.concatenate([block[..., :128], block[..., 256:320]], -1)
    lower = jnp.concatenate([block[..., 128:256], block[..., 320:]], -1)
    return jnp.concatenate([upper, lower], -2)


def grad_exp(mine, picks, d_inner, d_out, norms, got=None, after=()):
    operands, specs = (picks, d_inner, d_out) + norms, [HBM]
    scratch = [
        pltpu.VMEM((384, D), f32),
        pltpu.VMEM((D, 384), f32),
        pltpu.VMEM((8, D), f32),
        pltpu.VMEM((ROWS, D // 2), bf16),
        pltpu.VMEM((ROWS, D // 2), bf16),
        pltpu.SemaphoreType.DMA((2,)),
    ]
    return grad_call(
        grad_exp_kernel, "grad_exp", mine, operands, got, 4, (2, 2, 128, 384), scratch, after, specs
    )


def grad_att_kernel(
    part, mine, n_after, n_outs, picked, d_to_words, d_to_ents, d_keys, d_values, *refs
):
    got, outs, (turned,) = split_refs(mine, n_after, n_outs, refs)
    wide, narrow = coords()
    work = (
        (d_keys, slice(0, ROWS), 0, 0),
        (d_to_words, slice(0, WORDS), 0, 1),
        (d_to_words, slice(WORDS, ROWS), 0, 2),
        (d_values, slice(0, ROWS), 1, 0),
        (d_to_ents, slice(0, WORDS), 1, 1),
        (d_to_ents, slice(WORDS, ROWS), 1, 2),
    )
    for ref, rows, half, at in work:
        turned[...] = dot(ref[rows, :], picked[rows, :], TN)
        for y in range(2):
            for low in range(2):
                w = (wide % 4) ^ (low * 2 + y)
                blocks = packed(turned, w * 96, narrow)
                for x in range(2):
                    first, second = (x, y) if half == 0 else (y, x)
                    where = slice(at * 48, at * 48 + 48)
                    emit(mine, got, outs, half, first, (second, low), where, blocks[x])


def grad_att(part, mine, picked, grads, got=None, after=()):
    kernel = functools.partial(grad_att_kernel, part)
    operands = (picked,) + tuple(grads)
    scratch = [pltpu.VMEM((D // 2, 384), f32)]
    return grad_call(
        kernel, "grad_att", mine, operands, got, 1, (2, 144, 384), scratch, after
    )


def grad_hidden_kernel(n_after, kv, q, *refs):
    grads, d_first = refs[:8], refs[8]
    word, ent, joined, first_here, sem = refs[9 + n_after :]
    step = pl.program_id(0)
    upper, lower = slice(0, WORDS), slice(WORDS, ROWS)
    late = pltpu.make_async_copy(d_first, first_here, sem)

    def both(kind):
        joined[:, : D // 2] = grads[kind][...]
        joined[:, D // 2 :] = grads[4 + kind][...]

    @pl.when(step == 0)
    def _():
        late.start()
        both(2)
        word[...] = dot(joined[upper], kv[...], NN)
        ent[...] = dot(joined[lower], kv[...], NN)

    @pl.when(step == 1)
    def _():
        both(3)
        word[...] += dot(joined[upper], kv[...], NN)
        ent[...] += dot(joined[lower], kv[...], NN)

    @pl.when(step == 2)
    def _():
        both(0)
        word[...] += dot(joined[upper], q[...], NN)

    @pl.when(step == 3)
    def _():
        ent[...] += dot(joined[lower], q[...], NN)

    @pl.when(step == 4)
    def _():
        both(1)
        late.wait()
        word[...] += first_here[upper] + dot(joined[upper], q[...], NN)

    @pl.when(step == 5)
    def _():
        ent[...] += first_here[lower] + dot(joined[lower], q[...], NN)


def grad_hidden(d_first, grads, kv, q, after=()):
    after = tokens(after)
    return pl.pallas_call(
        functools.partial(grad_hidden_kernel, len(after)),
        grid=(6,),
        in_specs=[
            pl.BlockSpec((None, D, D), lambda i: (jnp.minimum(i, 1), 0, 0)),
            pl.BlockSpec((None, D, D), lambda i: (jnp.maximum(i - 2, 0), 0, 0)),
        ]
        + [VMEM] * 8
        + [HBM]
        + [ANY] * len(after),
        out_specs=[VMEM] * 2,
        out_shape=[stored((WORDS, D), f32), stored((ENTS, D), f32)],
        scratch_shapes=[
            pltpu.VMEM((ROWS, D), bf16),
            pltpu.VMEM((ROWS, D), f32),
            pltpu.SemaphoreType.DMA,
        ],
        compiler_params=PARAMS,
        cost_estimate=cost(9),
        name="grad_hidden",
    )(kv, q, *grads, d_first, *after)


def flip(axis, bit, value):
    size = lax.axis_size(axis)
    return lax.ppermute(value, axis, [(i, i ^ bit) for i in range(size)])


def over(name, value):
    axis, bit = {
        "core": ("narrow", 1),
        "x": ("narrow", 2),
        "y": ("wide", 1),
        "low": ("wide", 2),
        "high": ("wide", 4),
    }[name]
    return flip(axis, bit, value)


class Links:
    def __init__(self):
        self.past = {}

    def send(self, name, value):
        kind = "z" if name in ("low", "high") else name
        past = self.past.setdefault(kind, [])
        if len(past) > 1:
            value, unused = lax.optimization_barrier((value, past[-2]))
        got = over(name, value)
        past.append(got)
        return got


def later(values, token):
    return lax.optimization_barrier((values, token))[0]


def gather_high(links, first, second):
    both = jnp.concatenate([first, second], 0)
    return both, links.send("high", both)


def gather_low(links, cut, both):
    both = jnp.stack(both, 0)
    got = links.send("low", both)
    left = jnp.stack([both[:, :cut], got[:, :cut]], 0)
    right = jnp.stack([both[:, cut:], got[:, cut:]], 0)
    return left, right


def gather_near(links, left, right, token=None):
    got_left = links.send("x", left)
    got_right = links.send("y", right)
    if token is not None:
        got_left, got_right = later((got_left, got_right), token)
    left = jnp.stack([left, got_left], 0)
    right = jnp.stack([right, got_right], 0)
    return left, right


def gather_far(links, left, right):
    return gather_core(left, right, links.send("y", left), links.send("x", right))


def gather_core(left, right, left_far, right_far):
    left = jnp.stack([left, left_far], 0)
    right = jnp.stack([right, right_far], 0)
    return left, over("core", left), right, over("core", right)


def plus(kept, got):
    return (kept.astype(f32) + got.astype(f32)).astype(bf16)


class Sum:
    def __init__(self, send_left, send_right, keep):
        self.keep = keep
        self.got = over("x", send_left), over("y", send_right)

    def wait(self, token):
        self.got = later(self.got, token) if isinstance(self.got, tuple) else later((self.got,), token)[0]
        return self

    def parts(self):
        left, right = self.got
        keep = self.keep
        return (
            plus(keep[0, 1], left[1]),
            plus(keep[1, 1], right[1]),
            (plus(keep[0, 0], left[0]), plus(keep[1, 0], right[0])),
        )

    def second(self):
        left, right, self.keep = self.parts()
        self.got = over("y", left), over("x", right)

    def near(self):
        left, right = self.got
        return plus(self.keep[0], left), plus(self.keep[1], right)


def flat(blocks, leading):
    return jnp.concatenate([v.reshape(v.shape[:leading] + (-1, 384)) for v in blocks], leading)


def gather_all(value):
    size = lax.axis_size("wide") * lax.axis_size("narrow")
    spread = jnp.broadcast_to(value[None], (size,) + value.shape)
    return lax.all_to_all(spread, ("wide", "narrow"), 0, 0, tiled=False)


def sum_all(value):
    return jnp.sum(gather_all(value), axis=0)


def adapt(weight, grad, first, second, decay):
    first = 0.5 * first + 0.5 * grad
    second = 0.5 * second + 0.5 * grad * grad
    fix_first = 1.0 - 0.5**STEP
    fix_second = 1.0 - 0.5**STEP
    update = first / fix_first / (jnp.sqrt(second / fix_second) + adam_eps) + decay * weight
    return (first, second, update)


def adapt_kernel(own, got, out_rows, weight, moment, square, others, first, second, update, payload):
    lane = lax.broadcasted_iota(jnp.int32, (1, 128), 1)
    row = jnp.where(lane == 7, others[0], jnp.where(lane == 8, others[1], 0.0))
    for k, (half, at) in enumerate(((0, 1), (1, 1), (0, 2), (1, 2), (0, 0), (1, 0), (0, 0))):
        if k < 6:
            rows = pl.ds(half * 144 + at * 48, 48)
            block = own[rows, :].astype(f32) + got[rows, :].astype(f32)
        else:
            block = out_rows[...]
        grad = unpacked(block).T
        new_first = 0.5 * moment[k] + 0.5 * grad
        new_second = 0.5 * square[k] + 0.5 * grad * grad
        fix = 1.0 - 0.5**STEP
        step = new_first / fix / (jnp.sqrt(new_second / fix) + adam_eps) + matrix_decay * weight[k]
        first[k] = new_first
        second[k] = new_second
        update[k] = step
        row = jnp.where(lane == k, jnp.sum(step * step), row)
    payload[...] = jnp.broadcast_to(row[None], payload.shape)


def adapt_attention(devices, own, got, out_rows, weight, moment, square, others):
    dims = weight.shape
    return pl.pallas_call(
        adapt_kernel,
        in_specs=[VMEM] * 6 + [SMEM],
        out_specs=[VMEM] * 4,
        out_shape=[
            stored(dims, f32),
            stored(dims, f32),
            kept(dims, f32),
            shape((devices, 1, 128), f32),
        ],
        compiler_params=PARAMS,
        cost_estimate=cost(3),
        name="adapt_attention",
    )(own, got, out_rows, weight, moment, square, others)


def apply_kernel(rates, att, exp, red, att_update, exp_update, red_update, *new):
    for k in range(7):
        new[0][k] = att[k] - rates[k] * att_update[k]
    new[1][...] = exp[...] - rates[7] * exp_update[...]
    new[2][...] = red[...] - rates[8] * red_update[...]


def apply_updates(rates, weights, updates):
    return pl.pallas_call(
        apply_kernel,
        in_specs=[SMEM] + [VMEM] * 6,
        out_specs=[VMEM] * 3,
        out_shape=[stored(w.shape, f32) for w in weights],
        compiler_params=PARAMS,
        name="apply_updates",
    )(rates, *weights, *updates)


def shards(
    fast,
    word_states,
    entity_states,
    seq_counts,
    attention_weight,
    expand_weight,
    reduce_weight,
    norm_params,
    moment_attention,
    moment_expand,
    moment_reduce,
    moment_norms,
    square_attention,
    square_expand,
    square_reduce,
    square_norms,
    word_cotangent,
    entity_cotangent,
):
    word, ent, counts = word_states[0], entity_states[0], seq_counts[0]
    core = lax.axis_index("narrow") % 2
    high = lax.axis_index("wide") // 4
    if fast:
        keep, send, exp_low, red_low, weight_local = prep(
            attention_weight, expand_weight, reduce_weight.T
        )
        got = over("core", send)
        def lanes_of_both(k):
            return jnp.where(
                core == 0,
                jnp.concatenate([keep[k], got[k]], -1),
                jnp.concatenate([got[k], keep[k]], -1),
            )

        rows = [lanes_of_both(k) for k in range(7)]
        links = Links()
        kv = gather_high(links, rows[4], rows[5])
        query = gather_high(
            links,
            jnp.concatenate([rows[0], rows[2]], 0),
            jnp.concatenate([rows[1], rows[3]], 0),
        )
        kv = gather_low(links, 48, kv)
        query = gather_low(links, 96, query)
        kv = gather_near(links, *kv)
        kv_pieces = gather_far(links, *kv)
        query = gather_near(links, *query)
        query_far = links.send("y", query[0]), links.send("x", query[1])
        one = gather_high(
            links,
            jnp.concatenate([exp_low[:96], rows[6][:32]], 0),
            jnp.concatenate([exp_low[96:], rows[6][32:]], 0),
        )
        one = gather_low(links, 128, one)
        kv_pieces = [v.reshape(v.shape[:4] + (1, 48, 384)) for v in kv_pieces]
    else:
        weight_local = jnp.concatenate(
            [
                jnp.sum(attention_weight * attention_weight, axis=(1, 2)),
                jnp.sum(expand_weight * expand_weight)[None],
                jnp.sum(reduce_weight * reduce_weight)[None],
            ]
        )
        turned = jnp.swapaxes(attention_weight.astype(bf16), 1, 2)
        turned = lax.all_gather(turned, "wide", axis=1, tiled=True)
        turned = lax.all_gather(turned, "narrow", axis=2, tiled=True)
        exp_all = lax.all_gather(expand_weight.astype(bf16), "wide", axis=1, tiled=True)
        exp_all = lax.all_gather(exp_all, "narrow", axis=0, tiled=True)
        red_all = lax.all_gather(reduce_weight.astype(bf16).T, "wide", axis=0, tiled=True)
        red_all = lax.all_gather(red_all, "narrow", axis=1, tiled=True)
        kv_pieces = query_pieces = [turned]
        one_pieces = [turned, exp_all]
        two_pieces = [red_all]
        one = two = (None, None)

    low, keys, values, low_mine, low_other, kv_all = project_kv(fast, word, ent, kv_pieces)
    if fast:
        query_pieces = gather_core(*query, *later(query_far, keys))
        query_pieces = [v.reshape(v.shape[:4] + (2, 48, 384)) for v in query_pieces]
        two = gather_high(links, *later((red_low[:48], red_low[48:]), keys))
        one = gather_near(links, *later(one, keys))
        one_far = links.send("y", one[0]), links.send("x", one[1])
    to_words, to_ents, q_all = project_q(fast, low, query_pieces, after=two)
    if fast:
        two = gather_low(links, 48, two)
    context, exact, lse = attend(counts, to_words, to_ents, keys, values, after=one + two)
    if fast:
        two = gather_near(links, *two, token=context)
        one_pieces = gather_core(*one, *later(one_far, two))
        two_far = links.send("y", two[0]), links.send("x", two[1])
        two_core = over("core", two[0]), over("core", two[1])
    (
        middle,
        middle_low,
        activated,
        slope,
        unit_one,
        picks,
        out_all,
        exp_all,
    ) = feed_in(fast, word, ent, context, norm_params, one_pieces, after=two)
    if fast:
        two_far = later(two_far, activated)
        two_pieces = (two[0], two_core[0], two[1], two_core[1])
        two_pieces += (two_far[0], over("core", two_far[0]), two_far[1], over("core", two_far[1]))
    word_out, ent_out, d_second, d_ffn, grads_two, red_all = feed_out(
        fast, activated, middle, norm_params, word_cotangent[0], entity_cotangent[0], two_pieces
    )
    got = red = exp = att_one = att_two = None
    if fast:
        got = over("core", grad_red(False, d_ffn, activated)[0])
    d_inner, d_first, d_out, d_context, row_inner, grads_one = feed_back(
        d_ffn, red_all, exp_all, slope, norm_params, d_second, unit_one, out_all, exact
    )
    if fast:
        red = Sum(*grad_red(True, d_ffn, activated, got, after=(d_first,)))
    exp_args = (d_inner, d_out)
    norm_args = (grads_one, grads_two)
    att_args = (counts, to_words, to_ents, keys, values, d_context, lse, row_inner)
    if fast:
        sent = grad_exp(False, picks, *exp_args, norm_args, after=(red.keep,))[0]
        got = over("core", sent)
    grads = attend_back(0, *att_args, after=(sent,) if fast else ())
    if fast:
        red.wait(grads[0]).second()
        exp = Sum(
            *grad_exp(True, picks, *exp_args, norm_args, got, after=red.keep)
        )
        sent = grad_att(0, False, low_other, grads, after=(exp.keep,))[0]
        got = over("core", sent)
    more = attend_back(3, *att_args, after=(sent,) if fast else ())
    if fast:
        red_near = red.wait(more[0]).near()
        exp.wait(more[0]).second()
        sent = grad_att(1, False, low_other, more, after=exp.keep + red_near)[0]
        got_two = over("core", sent)
        att_one = Sum(*grad_att(0, True, low_mine, grads, got, after=(sent,)))
        att_two = Sum(*grad_att(1, True, low_mine, more, got_two, after=(att_one.keep,)))
        exp_near = exp.wait(att_two.keep).near()
        near = flat(red_near + exp_near, 2)
        low_got = over("low", near[1])
    word_grad, ent_grad = grad_hidden(
        d_first, grads + more, kv_all, q_all, after=(att_two.keep,) if fast else ()
    )

    if fast:
        att_one.got, att_two.got = later((att_one.got, att_two.got), word_grad)
        one_left, one_right, one_keep = att_one.parts()
        two_left, two_right, two_keep = att_two.parts()
        left_got = over("y", jnp.concatenate([one_left, two_left], 1))
        right_got = over("x", jnp.concatenate([one_right, two_right], 1))
        near = plus(near[0], later(low_got, (two_left, two_right)))
        high_got = over("high", near[1])
        left = plus(jnp.concatenate([one_keep[0], two_keep[0]], 1), left_got)
        right = plus(jnp.concatenate([one_keep[1], two_keep[1]], 1), right_got)
        got = over("low", jnp.concatenate([left[1], right[1]], 0))
        att_low = plus(jnp.concatenate([left[0], right[0]], 0), got).reshape(2, 2, 144, 384)
        att_low = jnp.swapaxes(att_low, 0, 1).reshape(2, 288, 384)
        high_got = later(high_got, att_low)
        near = near[0].astype(f32) + high_got.astype(f32)
        red_sum = near[:192].reshape(2, 48, D)
        exp_sum = near[192:].reshape(2, 128, 384)
        norm_row = jnp.concatenate([exp_sum[1, 96, :128], jnp.pad(weight_local, (0, 119))])
        norm_rows = gather_all(norm_row)
        weight_total = jnp.sum(norm_rows[:, 128:137], axis=0)
        norm_grads = norm_rows[:, :128].reshape(8, 4, 128)[:6]
        norm_grads = jnp.swapaxes(norm_grads, 0, 1).reshape(4, D)
        first, second = att_low[0], att_low[1]
        got = over("high", jnp.where(high == 0, second, first))
        att_own = jnp.where(high == 0, first, second)
        out_rows = jnp.concatenate([exp_sum[0, 96:], exp_sum[1, 112:]], 0)
        exp_grad = jnp.concatenate([exp_sum[0, :96], exp_sum[1, :96]], 0)
        red_grad = jnp.concatenate([red_sum[0], red_sum[1]], 0)
    else:
        d_to_words, d_to_ents, d_keys, d_values = [
            jnp.concatenate([a, b], 1) for a, b in zip(grads, more)
        ]
        norm_grads = sum_all(jnp.concatenate([grads_one, grads_two], 0))
        weight_total = sum_all(weight_local)
        words, ents = low[:WORDS], low[WORDS:]
        turned = jnp.stack(
            [
                dot(d_to_words[:WORDS], words, TN),
                dot(d_to_ents[:WORDS], words, TN),
                dot(d_to_words[WORDS:], ents, TN),
                dot(d_to_ents[WORDS:], ents, TN),
                dot(d_keys, low, TN),
                dot(d_values, low, TN),
                dot(d_out, context, TN),
            ]
        ).astype(bf16)
        turned = lax.psum_scatter(turned, "wide", scatter_dimension=1, tiled=True)
        turned = lax.psum_scatter(turned, "narrow", scatter_dimension=2, tiled=True)
        att_grad = jnp.swapaxes(turned.astype(f32), 1, 2)
        grad = dot(middle_low, d_inner, TN).astype(bf16)
        grad = lax.psum_scatter(grad, "wide", scatter_dimension=1, tiled=True)
        grad = lax.psum_scatter(grad, "narrow", scatter_dimension=0, tiled=True)
        exp_grad = grad.astype(f32)
        activated = jnp.swapaxes(activated, 0, 1).reshape(ROWS, FF)
        grad = dot(d_ffn, activated, TN).astype(bf16)
        grad = lax.psum_scatter(grad, "wide", scatter_dimension=0, tiled=True)
        grad = lax.psum_scatter(grad, "narrow", scatter_dimension=1, tiled=True)
        red_grad = grad.astype(f32)

    exp_first, exp_second, exp_update = adapt(
        expand_weight, exp_grad, moment_expand, square_expand, matrix_decay
    )
    red_first, red_second, red_update = adapt(
        reduce_weight.T, red_grad, moment_reduce.T, square_reduce.T, matrix_decay
    )
    exp_square = jnp.sum(exp_update * exp_update)
    red_square = jnp.sum(red_update * red_update)
    if fast:
        att_first, att_second, att_update, payload = adapt_attention(
            lax.axis_size("wide") * lax.axis_size("narrow"),
            att_own,
            got,
            out_rows,
            attention_weight,
            moment_attention,
            square_attention,
            jnp.stack([exp_square, red_square]),
        )
        totals = lax.all_to_all(payload, ("wide", "narrow"), 0, 0, tiled=False)
        update_total = jnp.sum(totals, axis=(0, 1))[:9]
    else:
        att_first, att_second, att_update = adapt(
            attention_weight, att_grad, moment_attention, square_attention, matrix_decay
        )
        update_total = sum_all(
            jnp.concatenate(
                [
                    jnp.sum(att_update * att_update, axis=(1, 2)),
                    exp_square[None],
                    red_square[None],
                ]
            )
        )
    nrm_first, nrm_second, nrm_update = adapt(
        norm_params, norm_grads, moment_norms, square_norms, 0.0
    )
    weight_norm = jnp.sqrt(
        jnp.concatenate([weight_total, jnp.sum(norm_params * norm_params, axis=1)])
    )
    update_norm = jnp.sqrt(
        jnp.concatenate([update_total, jnp.sum(nrm_update * nrm_update, axis=1)])
    )
    trust = weight_norm / update_norm
    new_attention, new_expand, new_reduce = apply_updates(
        learn_rate * trust[:9],
        (attention_weight, expand_weight, reduce_weight.T),
        (att_update, exp_update, red_update),
    )
    new_reduce = new_reduce.T
    new_norms = norm_params - learn_rate * trust[9:13, None] * nrm_update
    trust_stats = jnp.stack([jnp.log(weight_norm), jnp.log(update_norm), jnp.log(trust)], 1)
    return (
        word_out[None],
        ent_out[None],
        word_grad[None],
        ent_grad[None],
        new_attention,
        new_expand,
        new_reduce,
        new_norms,
        att_first,
        exp_first,
        red_first.T,
        nrm_first,
        att_second,
        exp_second,
        red_second.T,
        nrm_second,
        trust_stats,
    )


def solution(mesh):
    fast = mesh.shape["wide"] == 8 and mesh.shape["narrow"] == 4
    rows = P(("wide", "narrow"), None, None)
    matrix = P("narrow", "wide")
    stack = P(None, "narrow", "wide")
    weights = (stack, matrix, matrix, P())
    return jax.shard_map(
        functools.partial(shards, fast),
        mesh=mesh,
        in_specs=(rows, rows, P(("wide", "narrow"), None)) + weights * 3 + (rows, rows),
        out_specs=(rows,) * 4 + weights * 3 + (P(),),
        check_vma=False,
    )
```
